32 devices in a mesh: groups: 2 (over y), slab: 4 (over z), chan: 4 (over x, core).
Axes of the slice: x: 2, y: 2, z: 4, core: 2. Of those that a mesh axis runs over, the one named last changes fastest.
Arguments:
- inputs: float32 [256, 128, 20, 128], P(('groups', 'slab'), 'chan'), parts along dimension 0, may hold values from -6 to 6
- cotangent: float32 [256, 128, 20, 128], P(('groups', 'slab'), 'chan'), parts along dimension 0, may hold values from -6 to 6
- spectral: float32 [32, 32, 2, 20, 640], P('slab', 'chan'), may hold values from -2.5 to 2.5
- local_weight: float32 [20, 20], replicated, may hold values from -1.25 to 1.25
- bias_vector: float32 [20], replicated, may hold values from -3 to 3
Outputs:
- output: float32 [256, 128, 20, 128], P(('groups', 'slab'), 'chan'), parts along dimension 0
- grad_inputs: float32 [256, 128, 20, 128], P(('groups', 'slab'), 'chan'), parts along dimension 0
- grad_spectral: float32 [64, 32, 2, 20, 640], P(('groups', 'slab'), 'chan'), parts along dimension 0
The draws below stay inside these ranges and needn't reach their ends.
There are 2 independent parts, one for each index of `groups`. The reference program is written for one: setup_inputs(seed, part) draws one part's arguments, and reference() takes and returns one part's arrays. A program takes and returns all parts, laid end to end along the dimension named above; an argument that names none is the same for every part. Nothing has to cross between parts.
All inputs are finite; a program needn't handle non-finite values.
Results may differ from the reference program's by a relative error of at most 0.0001.
Values sent between devices are 32-bit elements; how exact they have to be, the bound alone decides.
No kernel may reach another device: no remote copies, remote signals or barrier semaphores. Data moves between devices by JAX's collectives and lax.ppermute only.
A program may use at most 320 MiB of HBM per device.

```python
import jax
import jax.numpy as jnp
from jax import lax

NX = 128
NY = 128
NZ = 128
C = 20
MX = 32
MY = 32
MZ = 32


def block_levels(stream_key, shape, pieces, smallest, high):
    level = 1.0
    for dim, blocks in pieces:
        steps = jax.random.uniform(jax.random.fold_in(jax.random.fold_in(stream_key, 6), dim), (blocks,), jnp.float32, smallest / len(pieces), high / len(pieces))
        level = level * jnp.repeat(jnp.exp(steps), shape[dim] // blocks).reshape((-1,) + (1,) * (len(shape) - 1 - dim))
    return level


def noise(key, shape, deviation, reach, split=(), kind=jnp.bfloat16):
    level = block_levels(key, shape, split, -0.22, 0.18) if split else 1.0
    array = jax.random.normal(key, shape, jnp.float32) * deviation * level
    return jnp.minimum(jnp.maximum(array, -reach), reach).astype(kind)


def setup_inputs(seed: int = 0, part: int = 0) -> dict:
    key_of = jax.random.split(jax.random.key(seed), 6)
    part_splits = jax.random.split(jax.random.fold_in(key_of[5], part), 6)
    inputs = noise(part_splits[0], (NX, NY, C, NZ), 1.0, 6.0, ((0, 4), (1, 4)), jnp.float32)
    cotangent = noise(part_splits[1], (NX, NY, C, NZ), 1.0, 6.0, ((0, 4), (1, 4)), jnp.float32)
    spectral = noise(key_of[2], (MY, MZ, 2, C, C * MX), 0.4, 2.5, ((0, 4), (1, 4)), jnp.float32)
    local_weight = noise(key_of[3], (C, C), C ** -0.5, 1.25, (), jnp.float32)
    bias_vector = noise(key_of[4], (C,), 0.5, 3.0, (), jnp.float32)
    return dict(inputs=inputs, cotangent=cotangent, spectral=spectral, local_weight=local_weight, bias_vector=bias_vector)


highest = lax.Precision.HIGHEST
root_half = 0.7071067811865476
inv_root_two_pi = 0.3989422804014327


def retain(values, dimension, kept_count):
    total_count = values.shape[dimension]
    lower_count = kept_count // 2
    return jnp.concatenate([
        lax.slice_in_dim(values, 0, lower_count, axis=dimension),
        lax.slice_in_dim(values, total_count - (kept_count - lower_count), total_count, axis=dimension)], axis=dimension)


def spread(values, dimension, total_count):
    kept_count = values.shape[dimension]
    lower_count = kept_count // 2
    zero_shape = list(values.shape)
    zero_shape[dimension] = total_count - kept_count
    return jnp.concatenate([
        lax.slice_in_dim(values, 0, lower_count, axis=dimension),
        jnp.zeros(zero_shape, values.dtype),
        lax.slice_in_dim(values, lower_count, kept_count, axis=dimension)], axis=dimension)


def analyse(values):
    spectrum = jnp.fft.fftn(values, axes=(0, 1, 3), norm="ortho")
    spectrum = retain(spectrum, 0, MX)
    spectrum = retain(spectrum, 1, MY)
    return retain(spectrum, 3, MZ)


def synthesise(spectrum):
    full_modes = spread(spread(spread(spectrum, 0, NX), 1, NY), 3, NZ)
    return jnp.real(jnp.fft.ifftn(full_modes, axes=(0, 1, 3), norm="ortho"))


def smooth_gate(values):
    return 0.5 * values * (1.0 + jax.scipy.special.erf(values * root_half))


def gate_slope(values):
    return 0.5 * (1.0 + jax.scipy.special.erf(values * root_half)) + values * jnp.exp(-0.5 * values * values) * inv_root_two_pi


def reference(inputs, cotangent, spectral, local_weight, bias_vector):
    weights = spectral.reshape(MY, MZ, 2, C, C, MX)
    complex_weights = weights[:, :, 0] + 1j * weights[:, :, 1]
    in_modes = analyse(inputs)
    out_modes = jnp.einsum('abik,bkioa->abok', in_modes, complex_weights, precision=highest)
    spectral_part = synthesise(out_modes)
    linear_sum = spectral_part + jnp.einsum('xycz,co->xyoz', inputs, local_weight, precision=highest) + bias_vector[:, None]
    output = smooth_gate(linear_sum)
    pre_gradient = cotangent * gate_slope(linear_sum)
    grad_modes = analyse(pre_gradient)
    grad_complex = jnp.einsum('abok,abik->bkioa', grad_modes, jnp.conj(in_modes), precision=highest)
    grad_spectral = jnp.stack([jnp.real(grad_complex), jnp.imag(grad_complex)], axis=2).reshape(MY, MZ, 2, C, C * MX)
    back_modes = jnp.einsum('bkioa,abok->abik', jnp.conj(complex_weights), grad_modes, precision=highest)
    grad_inputs = synthesise(back_modes) + jnp.einsum('xyoz,co->xycz', pre_gradient, local_weight, precision=highest)
    return output, grad_inputs, grad_spectral
```

```python
from functools import partial
import math

import jax
import jax.numpy as jnp
import ml_dtypes
import numpy as np
from jax import lax
from jax.experimental import pallas as pl
from jax.experimental.pallas import tpu as pltpu
from jax.sharding import PartitionSpec as P

f32 = jnp.float32
bf16 = jnp.bfloat16
root_half = 0.7071067811865476
inv_root_two_pi = 0.3989422804014327
VMEM_LIMIT = 60 * 1024 * 1024
NT = (((1,), (1,)), ((), ()))
TN = (((0,), (0,)), ((), ()))


def round_up(value, unit):
    return -(-value // unit) * unit


class Plan:
    def __init__(self, nx, ny, nz, channels, wb, wk, mx, slab_count, chan_count):
        self.nx, self.ny, self.nz, self.c = nx, ny, nz, channels
        self.wb, self.wk, self.mx = wb, wk, mx
        self.s, self.ch = slab_count, chan_count
        self.half = chan_count // 2
        self.na = mx // 2 + 1
        self.span = (wb + 1) * self.na
        self.lw = slab_count * self.span
        self.lp = round_up(self.lw, 128)
        self.ll = round_up(2 * self.span, 128)
        self.mk = self.half * wk
        self.rc = round_up(2 * self.mk + 2 * self.half, 8)
        self.rt = round_up(channels * (wk + 1), 8)
        self.xb = math.gcd(8, nx)
        self.blk = self.xb * ny
        self.rows = channels * wk
        self.full_x, self.full_y = nx * slab_count, ny * chan_count

    def starts(self):
        kept = self.wb * self.s
        return [g * self.wb - (kept if 2 * g >= self.s else 0) for g in range(self.s)]

    def columns(self):
        b = np.concatenate([np.repeat(np.arange(st, st + self.wb + 1), self.na) for st in self.starts()])
        a = np.tile(np.arange(self.na), self.s * (self.wb + 1))
        return a, b

    def plane_table(self):
        a, b = self.columns()
        x = np.repeat(np.arange(self.nx), self.ny)[:, None]
        y = np.tile(np.arange(self.ny), self.nx)[:, None]
        total = self.full_x * self.full_y
        phase = (a * x * self.full_y + b * y * self.full_x) % total * (2.0 * np.pi / total)
        table = np.zeros((self.nx * self.ny, 2 * self.lp))
        scale = 1.0 / math.sqrt(total)
        table[:, : self.lw] = np.cos(phase) * scale
        table[:, self.lp : self.lp + self.lw] = -np.sin(phase) * scale
        return halves(table)

    def turns(self):
        a, b = self.columns()
        x = (np.arange(self.s) * self.nx)[:, None, None]
        y = (np.arange(self.ch) * self.ny)[None, :, None]
        total = self.full_x * self.full_y
        phase = (a * x * self.full_y + b * y * self.full_x) % total * (2.0 * np.pi / total)
        table = np.zeros((self.s, self.ch, 2, self.lp), np.float32)
        table[:, :, 0, : self.lw] = np.cos(phase)
        table[:, :, 1, : self.lw] = np.sin(phase)
        return table

    def depth_rows(self):
        main = np.arange(self.mk)
        edge = (np.arange(self.half) + 1) * self.wk
        z = np.arange(self.nz)
        scale = 1.0 / math.sqrt(self.nz)
        angle = lambda k: (k[:, None] * z) % self.nz * (2.0 * np.pi / self.nz)
        rows = [np.cos(angle(main)), np.sin(angle(main)), np.cos(angle(edge)), np.sin(angle(edge))]
        table = np.zeros((self.rc, self.nz))
        table[: 2 * self.mk + 2 * self.half] = np.concatenate(rows) * scale
        return halves(table)

    def depth_forward(self):
        high, low = self.depth_rows()
        return np.concatenate(
            [np.concatenate([high, high], 1), np.concatenate([low, np.zeros_like(low)], 1)], 0
        )

    def depth_inverse(self):
        high, low = self.depth_rows()
        table = np.zeros((round_up(3 * self.rc, 16), self.nz), ml_dtypes.bfloat16)
        table[: 3 * self.rc] = np.concatenate([high, high, low], 0)
        return table

    def selections(self):
        quarters = 128 // self.mx
        own = np.zeros((self.wb, 2, self.ll, 2, quarters, self.mx), np.float32)
        for b in range(self.wb):
            for r in range(2):
                for a in range(self.mx):
                    if a < self.mx // 2:
                        own[b, 0, r * self.span + b * self.na + a, r, :, a] = 1.0
                    else:
                        spot = r * self.span + (self.wb - b) * self.na + self.mx - a
                        own[b, 1, spot, r, :, a] = 1.0 - 2.0 * r
        own = own.reshape(self.wb, 2 * self.ll, 256)
        back = np.swapaxes(own, 1, 2)
        return own.astype(ml_dtypes.bfloat16), np.ascontiguousarray(back).astype(ml_dtypes.bfloat16)

    def orders(self):
        table = np.zeros((2, self.rows, self.rt), np.float32)
        for c in range(self.c):
            for k in range(self.wk):
                table[0, c * self.wk + k, c * self.wk + k] = 1.0
                mirrored = self.wk - k
                spot = self.rows + c if mirrored == self.wk else c * self.wk + mirrored
                table[1, c * self.wk + k, spot] = 1.0
        return table.astype(ml_dtypes.bfloat16)


def halves(table):
    high = table.astype(np.float32).astype(ml_dtypes.bfloat16)
    low = (table - high.astype(np.float64)).astype(np.float32).astype(ml_dtypes.bfloat16)
    return high, low


def dot(left, right, numbers=(((1,), (0,)), ((), ()))):
    return lax.dot_general(left, right, numbers, preferred_element_type=f32)


def split(value):
    high = value.astype(bf16)
    return high, (value - high.astype(f32)).astype(bf16)


def moved(value, chosen, left=False):
    first = value.astype(bf16)
    rest = value - first.astype(f32)
    second = rest.astype(bf16)
    third = (rest - second.astype(f32)).astype(bf16)
    if left:
        return dot(chosen, first) + dot(chosen, second) + dot(chosen, third)
    return dot(first, chosen) + dot(second, chosen) + dot(third, chosen)


def depth_analysis(plan, table_ref, values):
    high, low = split(values)
    both = dot(table_ref[...], jnp.concatenate([high, low], axis=1), NT)
    return both[: plan.rc] + both[plan.rc :]


def depth_synthesis(plan, table_ref, rows):
    high = rows.astype(bf16).astype(f32)
    parts = [high, rows - high, high]
    extra = table_ref.shape[0] - 3 * plan.rc
    if extra:
        parts.append(jnp.zeros((extra, rows.shape[1]), f32))
    return dot(jnp.concatenate(parts, axis=0).astype(bf16), table_ref[...], TN)


def plane_analysis(plan, step, lines_ref, high_ref, low_ref, total_ref):
    high, low = split(lines_ref[...].reshape(plan.c * plan.rc, plan.blk))
    for start in range(0, 2 * plan.lp, 256):
        size = min(256, 2 * plan.lp - start)
        columns = pl.ds(start, size)
        part = dot(high, high_ref[:, columns]) + dot(low, high_ref[:, columns]) + dot(high, low_ref[:, columns])
        part = part.reshape(plan.c, plan.rc, size)

        @pl.when(step == 0)
        def _():
            total_ref[:, :, columns] = part

        @pl.when(step > 0)
        def _():
            total_ref[:, :, columns] += part


def plane_synthesis(plan, high_rows, low_rows, high_ref, low_ref, lines_ref):
    high_table, low_table = high_ref[...], low_ref[...]
    lines = (
        dot(high_rows[...], high_table, NT)
        + dot(low_rows[...], high_table, NT)
        + dot(high_rows[...], low_table, NT)
    )
    lines_ref[...] = lines.reshape(plan.c, plan.rc, plan.blk)


def emit_modes(plan, flag_ref, turn_ref, total_ref, keep_ref, send_ref):
    lp, wk, mk, half = plan.lp, plan.wk, plan.mk, plan.half
    odd = flag_ref[0] == 1
    cosine, sine = turn_ref[0:1, :], turn_ref[1:2, :]
    for c in range(plan.c):
        real, imag = total_ref[c, :, :lp], total_ref[c, :, lp:]
        real, imag = real * cosine + imag * sine, imag * cosine - real * sine
        for first, size, base, shift in ((0, wk, c * wk, mk), (2 * mk, 1, plan.rows + c, half)):
            made = []
            for g in range(plan.ch):
                h = g if g < half else plan.ch - 1 - g
                even_rows = slice(first + h * size, first + (h + 1) * size)
                odd_rows = slice(first + shift + h * size, first + shift + (h + 1) * size)
                if g < half:
                    made.append((real[even_rows] + imag[odd_rows], imag[even_rows] - real[odd_rows]))
                else:
                    made.append((real[even_rows] - imag[odd_rows], imag[even_rows] + real[odd_rows]))
            for pair in range(half):
                for r in range(2):
                    low, high = made[2 * pair][r], made[2 * pair + 1][r]
                    keep_ref[pair, r, base : base + size, :] = jnp.where(odd, high, low)
                    send_ref[pair, r, base : base + size, :] = jnp.where(odd, low, high)
    used = plan.c * (wk + 1)
    if used < plan.rt:
        blank = jnp.zeros((plan.half, 2, plan.rt - used, lp), f32)
        keep_ref[:, :, used:, :] = blank
        send_ref[:, :, used:, :] = blank


def take_modes(plan, flag_ref, turn_ref, own_ref, other_ref, total_ref, high_rows, low_rows):
    lp, wk, mk, half = plan.lp, plan.wk, plan.mk, plan.half
    odd = flag_ref[0] == 1
    cosine, sine = turn_ref[0:1, :], turn_ref[1:2, :]

    def group(g, r, rows):
        own, other = own_ref[g // 2, r, rows, :], other_ref[g // 2, r, rows, :]
        return jnp.where(odd, own, other) if g % 2 else jnp.where(odd, other, own)

    for c in range(plan.c):
        for first, size, base, shift in ((0, wk, c * wk, mk), (2 * mk, 1, plan.rows + c, half)):
            rows = slice(base, base + size)
            for h in range(half):
                plus = [group(h, r, rows) for r in range(2)]
                minus = [group(plan.ch - 1 - h, r, rows) for r in range(2)]
                real, imag = plus[0] + minus[0], plus[1] + minus[1]
                here = slice(first + h * size, first + (h + 1) * size)
                total_ref[c, here, :lp] = real * cosine - imag * sine
                total_ref[c, here, lp:] = imag * cosine + real * sine
                real, imag = plus[0] - minus[0], plus[1] - minus[1]
                here = slice(first + shift + h * size, first + shift + (h + 1) * size)
                total_ref[c, here, :lp] = -(imag * cosine + real * sine)
                total_ref[c, here, lp:] = real * cosine - imag * sine
        used = 2 * mk + 2 * half
        if used < plan.rc:
            total_ref[c, used:, :] = jnp.zeros((plan.rc - used, 2 * lp), f32)
    high, low = split(total_ref[...].reshape(plan.c * plan.rc, 2 * lp))
    high_rows[...] = high
    low_rows[...] = low


def analyse_kernel(plan, flag_ref, values_ref, high_ref, low_ref, depth_ref, turn_ref, keep_ref, send_ref, lines_ref, total_ref):
    step = pl.program_id(0)

    @pl.loop(0, plan.c)
    def _(c):
        lines_ref[c] = depth_analysis(plan, depth_ref, values_ref[:, c].reshape(plan.blk, plan.nz))

    plane_analysis(plan, step, lines_ref, high_ref, low_ref, total_ref)

    @pl.when(step == pl.num_programs(0) - 1)
    def _():
        emit_modes(plan, flag_ref, turn_ref, total_ref, keep_ref, send_ref)


def middle_kernel(
    plan, flag_ref, own_ref, other_ref, linear_ref, cotangent_ref, high_ref, low_ref, depth_ref, inverse_ref, turn_ref,
    output_ref, gradient_ref, keep_ref, send_ref, lines_ref, back_ref, total_ref, high_rows, low_rows,
):
    step = pl.program_id(0)

    @pl.when(step == 0)
    def _():
        take_modes(plan, flag_ref, turn_ref, own_ref, other_ref, total_ref, high_rows, low_rows)

    plane_synthesis(plan, high_rows, low_rows, high_ref, low_ref, lines_ref)
    shape = (plan.xb, plan.ny, plan.nz)

    @pl.loop(0, plan.c)
    def _(o):
        field = depth_synthesis(plan, inverse_ref, lines_ref[o])
        value = field + linear_ref[:, o].reshape(plan.blk, plan.nz)
        gate = 0.5 * (1.0 + lax.erf(value * root_half))
        slope = gate + value * jnp.exp(-0.5 * value * value) * inv_root_two_pi
        output_ref[:, o] = (value * gate).reshape(shape)
        gradient = cotangent_ref[:, o].reshape(plan.blk, plan.nz) * slope
        gradient_ref[:, o] = gradient.reshape(shape)
        back_ref[o] = depth_analysis(plan, depth_ref, gradient)

    plane_analysis(plan, step, back_ref, high_ref, low_ref, total_ref)

    @pl.when(step == pl.num_programs(0) - 1)
    def _():
        emit_modes(plan, flag_ref, turn_ref, total_ref, keep_ref, send_ref)


def synthesise_kernel(
    plan, flag_ref, own_ref, other_ref, linear_ref, high_ref, low_ref, inverse_ref, turn_ref,
    output_ref, lines_ref, total_ref, high_rows, low_rows,
):
    @pl.when(pl.program_id(0) == 0)
    def _():
        take_modes(plan, flag_ref, turn_ref, own_ref, other_ref, total_ref, high_rows, low_rows)

    plane_synthesis(plan, high_rows, low_rows, high_ref, low_ref, lines_ref)

    @pl.loop(0, plan.c)
    def _(o):
        value = depth_synthesis(plan, inverse_ref, lines_ref[o]) + linear_ref[:, o].reshape(plan.blk, plan.nz)
        output_ref[:, o] = value.reshape(plan.xb, plan.ny, plan.nz)


def linear_kernel(plan, values_ref, matrix_ref, bias_ref, output_ref):
    tiles = plan.ny // 8
    values = [values_ref[0, :, t * 8 : (t + 1) * 8, :].reshape(plan.c * 8, plan.nz) for t in range(tiles)]
    high, low = split(jnp.concatenate(values, axis=1))
    high_matrix, low_matrix = split(matrix_ref[...])
    mixed = dot(high_matrix, high) + dot(high_matrix, low) + dot(low_matrix, high) + bias_ref[...]
    for t in range(tiles):
        output_ref[0, :, t * 8 : (t + 1) * 8, :] = mixed[:, t * plan.nz : (t + 1) * plan.nz].reshape(plan.c, 8, plan.nz)


def pick(plan, own_ref, mirror_ref, order_ref, chosen_ref, ordered_ref):
    @pl.when(pl.program_id(0) == 0)
    def _():
        ordered_ref[:, : plan.ll] = moved(own_ref[...], order_ref[...], left=True)
        ordered_ref[:, plan.ll :] = moved(mirror_ref[...], order_ref[...], left=True)

    return moved(ordered_ref[...], chosen_ref[0])


def give(plan, made_ref, order_ref, back_ref, own_ref, mirror_ref, sums_ref):
    part = moved(made_ref[...], back_ref[0])
    step = pl.program_id(0)

    @pl.when(step == 0)
    def _():
        sums_ref[...] = part

    @pl.when(step > 0)
    def _():
        sums_ref[...] += part

    @pl.when(step == pl.num_programs(0) - 1)
    def _():
        own_ref[...] = moved(sums_ref[:, : plan.ll], order_ref[...], left=True)
        mirror_ref[...] = moved(sums_ref[:, plan.ll :], order_ref[...], left=True)


def mix_kernel(
    plan, own_ref, mirror_ref, order_ref, disorder_ref, chosen_ref, back_ref, weight_ref,
    modes_ref, own_out, mirror_out, ordered_ref, made_ref, sums_ref,
):
    wk, quarters = plan.wk, 128 // plan.mx
    modes = pick(plan, own_ref, mirror_ref, order_ref, chosen_ref, ordered_ref)
    modes_ref[0] = modes
    place = lax.broadcasted_iota(jnp.int32, (wk, 128), 1) // plan.mx
    for t in range(plan.c // quarters):
        columns = slice(t * 128, (t + 1) * 128)
        real = imag = 0.0
        for i in range(plan.c):
            x_real, x_imag = modes[i * wk : (i + 1) * wk, :128], modes[i * wk : (i + 1) * wk, 128:]
            w_real, w_imag = weight_ref[0, 0, i, :, columns], weight_ref[0, 1, i, :, columns]
            real = real + (w_real * x_real - w_imag * x_imag)
            imag = imag + (w_real * x_imag + w_imag * x_real)
        for q in range(quarters):
            o = t * quarters + q
            made_ref[o * wk : (o + 1) * wk, :128] = jnp.where(place == q, real, 0.0)
            made_ref[o * wk : (o + 1) * wk, 128:] = jnp.where(place == q, imag, 0.0)
    give(plan, made_ref, disorder_ref, back_ref, own_out, mirror_out, sums_ref)


def mix_back_kernel(
    plan, own_ref, mirror_ref, order_ref, disorder_ref, chosen_ref, back_ref, weight_ref, modes_ref,
    gradient_ref, own_out, mirror_out, ordered_ref, made_ref, sums_ref,
):
    wk, quarters = plan.wk, 128 // plan.mx
    grads = pick(plan, own_ref, mirror_ref, order_ref, chosen_ref, ordered_ref)
    place = lax.broadcasted_iota(jnp.int32, (wk, 128), 1) // plan.mx
    lined = []
    for t in range(plan.c // quarters):
        real = imag = 0.0
        for q in range(quarters):
            o = t * quarters + q
            real = jnp.where(place == q, grads[o * wk : (o + 1) * wk, :128], real)
            imag = jnp.where(place == q, grads[o * wk : (o + 1) * wk, 128:], imag)
        lined.append((real, imag))
    for i in range(plan.c):
        rows = slice(i * wk, (i + 1) * wk)
        x_real, x_imag = modes_ref[0, rows, :128], modes_ref[0, rows, 128:]
        back_real = back_imag = 0.0
        for t, (real, imag) in enumerate(lined):
            columns = slice(t * 128, (t + 1) * 128)
            gradient_ref[0, 0, i, :, columns] = real * x_real + imag * x_imag
            gradient_ref[0, 1, i, :, columns] = imag * x_real - real * x_imag
            w_real, w_imag = weight_ref[0, 0, i, :, columns], weight_ref[0, 1, i, :, columns]
            back_real = back_real + (w_real * real + w_imag * imag)
            back_imag = back_imag + (w_real * imag - w_imag * real)
        made_ref[rows, :128] = back_real
        made_ref[rows, 128:] = back_imag
    give(plan, made_ref, disorder_ref, back_ref, own_out, mirror_out, sums_ref)


def whole(array):
    zeros = (0,) * array.ndim
    return pl.BlockSpec(array.shape, lambda i: zeros, pipeline_mode=pl.Buffered(1))


def whole_shape(shape):
    zeros = (0,) * len(shape)
    return pl.BlockSpec(shape, lambda i: zeros, pipeline_mode=pl.Buffered(1))


def leading(shape):
    rest = (0,) * (len(shape) - 1)
    return pl.BlockSpec(shape, lambda i: (i,) + rest)


def shaped(*shape):
    return jax.ShapeDtypeStruct(shape, f32)


def scalar():
    return pl.BlockSpec(memory_space=pltpu.SMEM)


def call(kernel, name, grid, in_specs, out_specs, out_shape, scratch, flops, size):
    return pl.pallas_call(
        kernel,
        grid=(grid,),
        in_specs=in_specs,
        out_specs=out_specs,
        out_shape=out_shape,
        scratch_shapes=scratch,
        name=name,
        compiler_params=pltpu.CompilerParams(vmem_limit_bytes=VMEM_LIMIT, dimension_semantics=("arbitrary",)),
        cost_estimate=pl.CostEstimate(flops=flops, bytes_accessed=size, transcendentals=0),
    )


class Program:
    def __init__(self, plan):
        self.plan = plan
        self.plane = [jnp.asarray(t) for t in plan.plane_table()]
        self.depth = jnp.asarray(plan.depth_forward())
        self.inverse = jnp.asarray(plan.depth_inverse())
        slab, chan = lax.axis_index("slab"), lax.axis_index("chan")
        self.slab, self.chan = slab, chan
        turns = jnp.asarray(plan.turns())
        self.turn = lax.dynamic_index_in_dim(
            lax.dynamic_index_in_dim(turns, slab, 0, False), chan, 0, False
        )
        self.flag = (chan % 2).astype(jnp.int32).reshape(1)
        orders = jnp.asarray(plan.orders())
        upper = (chan >= plan.half).astype(jnp.int32)
        self.order = lax.dynamic_index_in_dim(orders, upper, 0, False)
        self.disorder = self.order.T
        chosen, back = plan.selections()
        self.chosen, self.back = jnp.asarray(chosen), jnp.asarray(back)
        self.matmul = 6 * plan.c * plan.rc * 2 * plan.lp * plan.nx * plan.ny
        self.field = plan.nx * plan.ny * plan.nz * plan.c * 4

    def half_shape(self):
        plan = self.plan
        return (plan.half, 2, plan.rt, plan.lp)

    def field_spec(self):
        plan = self.plan
        return leading((plan.xb, plan.c, plan.ny, plan.nz))

    def tables(self):
        plan = self.plan
        return [leading((plan.blk, 2 * plan.lp))] * 2

    def lines(self):
        plan = self.plan
        return pltpu.VMEM((plan.c, plan.rc, plan.blk), f32)

    def spectra(self):
        plan = self.plan
        rows = pltpu.VMEM((plan.c * plan.rc, 2 * plan.lp), bf16)
        return [pltpu.VMEM((plan.c, plan.rc, 2 * plan.lp), f32), rows, rows]

    def analyse(self, values):
        plan = self.plan
        half = self.half_shape()
        return call(
            partial(analyse_kernel, plan), "analyse", plan.nx // plan.xb,
            [scalar(), self.field_spec(), *self.tables(), whole(self.depth), whole(self.turn)],
            [whole_shape(half)] * 2, [shaped(*half)] * 2,
            [self.lines(), self.spectra()[0]], self.matmul, self.field,
        )(self.flag, values, *self.plane, self.depth, self.turn)

    def middle(self, own, other, linear, cotangent):
        plan = self.plan
        half = self.half_shape()
        field = shaped(plan.nx, plan.c, plan.ny, plan.nz)
        return call(
            partial(middle_kernel, plan), "middle", plan.nx // plan.xb,
            [scalar(), whole_shape(half), whole_shape(half), self.field_spec(), self.field_spec(), *self.tables(),
             whole(self.depth), whole(self.inverse), whole(self.turn)],
            [self.field_spec(), self.field_spec(), whole_shape(half), whole_shape(half)],
            [field, field, shaped(*half), shaped(*half)],
            [self.lines(), self.lines(), *self.spectra()], 2 * self.matmul, 4 * self.field,
        )(self.flag, own, other, linear, cotangent, *self.plane, self.depth, self.inverse, self.turn)

    def synthesise(self, own, other, linear):
        plan = self.plan
        half = self.half_shape()
        return call(
            partial(synthesise_kernel, plan), "synthesise", plan.nx // plan.xb,
            [scalar(), whole_shape(half), whole_shape(half), self.field_spec(), *self.tables(),
             whole(self.inverse), whole(self.turn)],
            self.field_spec(), shaped(plan.nx, plan.c, plan.ny, plan.nz),
            [self.lines(), *self.spectra()], self.matmul, 2 * self.field,
        )(self.flag, own, other, linear, *self.plane, self.inverse, self.turn)

    def linear(self, values, matrix, bias):
        plan = self.plan
        wide = jnp.kron(matrix, jnp.eye(8, dtype=f32))
        column = jnp.repeat(bias, 8)[:, None]
        spec = leading((1, plan.c, plan.ny, plan.nz))
        return call(
            partial(linear_kernel, plan), "linear", plan.nx,
            [spec, whole(wide), whole(column)],
            spec, shaped(plan.nx, plan.c, plan.ny, plan.nz), [],
            6 * (8 * plan.c) ** 2 * plan.nx * plan.ny // 8 * plan.nz, 2 * self.field,
        )(values, wide, column)

    def mix_specs(self):
        plan = self.plan
        modes = (plan.rt, plan.ll)
        ins = [
            whole_shape(modes), whole_shape(modes), whole(self.order), whole(self.disorder),
            leading((1,) + self.chosen.shape[1:]), leading((1,) + self.back.shape[1:]),
            leading((1, 2, plan.c, plan.wk, plan.c * plan.mx)),
        ]
        scratch = [
            pltpu.VMEM((plan.rows, 2 * plan.ll), f32),
            pltpu.VMEM((plan.rows, 256), f32),
            pltpu.VMEM((plan.rows, 2 * plan.ll), f32),
        ]
        return ins, [whole_shape(modes)] * 2, [shaped(*modes)] * 2, scratch

    def mix(self, own, mirror, weights):
        plan = self.plan
        ins, outs, shapes, scratch = self.mix_specs()
        kept = leading((1, plan.rows, 256))
        return call(
            partial(mix_kernel, plan), "mix", plan.wb, ins, [kept, *outs],
            [shaped(plan.wb, plan.rows, 256), *shapes], scratch, 10**9, 4 * weights.size,
        )(own, mirror, self.order, self.disorder, self.chosen, self.back, weights)

    def mix_back(self, own, mirror, weights, modes):
        plan = self.plan
        ins, outs, shapes, scratch = self.mix_specs()
        kept = leading((1, plan.rows, 256))
        return call(
            partial(mix_back_kernel, plan), "mix_back", plan.wb, ins + [kept], [ins[-1], *outs],
            [shaped(*weights.shape), *shapes], scratch, 10**9, 8 * weights.size,
        )(own, mirror, self.order, self.disorder, self.chosen, self.back, weights, modes)

    def across(self, value, axis, bit):
        size = lax.axis_size(axis)
        return lax.ppermute(value, axis, [(i, i ^ bit) for i in range(size)])

    def mirrored(self, value):
        total = self.plan.s * self.plan.ch
        return lax.ppermute(value, ("slab", "chan"), [(i, total - 1 - i) for i in range(total)])

    def gather_sums(self, keep, send):
        plan = self.plan
        total = keep + self.across(send, "chan", 1)
        bit = 2
        while bit < plan.ch:
            mine = (self.chan // bit) % 2
            pairs = total.reshape((total.shape[0] // 2, 2) + total.shape[1:])
            send = lax.dynamic_index_in_dim(pairs, 1 - mine, 1, False)
            total = lax.dynamic_index_in_dim(pairs, mine, 1, False) + self.across(send, "chan", bit)
            bit *= 2
        total = total[0]
        blank = jnp.zeros((plan.rt, plan.ll - 2 * plan.span), f32)
        pieces = []
        for g in range(plan.s):
            window = slice(g * plan.span, (g + 1) * plan.span)
            pieces.append(jnp.concatenate([total[0, :, window], total[1, :, window], blank], axis=1))
        pieces = jnp.stack(pieces)
        mine = lax.dynamic_index_in_dim(pieces, self.slab, 0, False)
        arrived = [
            self.across(lax.dynamic_index_in_dim(pieces, self.slab ^ j, 0, False), "slab", j)
            for j in range(1, plan.s)
        ]
        for piece in arrived:
            mine = mine + piece
        return mine, self.mirrored(mine)

    def spread_modes(self, own, mirror):
        plan = self.plan
        mine = own + self.mirrored(mirror)
        held = jnp.stack([mine] + [self.across(mine, "slab", j) for j in range(1, plan.s)])
        pieces = [lax.dynamic_index_in_dim(held, self.slab ^ g, 0, False) for g in range(plan.s)]
        blank = jnp.zeros((plan.rt, plan.lp - plan.lw), f32)
        total = jnp.stack([
            jnp.concatenate([p[:, r * plan.span : (r + 1) * plan.span] for p in pieces] + [blank], axis=1)
            for r in range(2)
        ])[None]
        bit = plan.ch // 2
        while bit > 1:
            other = self.across(total, "chan", bit)
            upper = (self.chan // bit) % 2 == 1
            total = jnp.stack([jnp.where(upper, other, total), jnp.where(upper, total, other)], axis=1)
            total = total.reshape((-1,) + total.shape[2:])
            bit //= 2
        return total, self.across(total, "chan", 1)


def local(inputs, cotangent, spectral, local_weight, bias_vector):
    nx, ny, channels, nz = inputs.shape
    wb, wk = spectral.shape[0], spectral.shape[1]
    plan = Plan(nx, ny, nz, channels, wb, wk, spectral.shape[4] // channels, lax.axis_size("slab"), lax.axis_size("chan"))
    program = Program(plan)
    values = jnp.transpose(inputs, (0, 2, 1, 3))
    weights = jnp.transpose(spectral, (0, 2, 3, 1, 4))
    own, mirror = program.gather_sums(*program.analyse(values))
    linear = program.linear(values, local_weight.T, bias_vector)
    modes, own, mirror = program.mix(own, mirror, weights)
    own, other = program.spread_modes(own, mirror)
    output, gradient, keep, send = program.middle(own, other, linear, jnp.transpose(cotangent, (0, 2, 1, 3)))
    own, mirror = program.gather_sums(keep, send)
    linear = program.linear(gradient, local_weight, jnp.zeros_like(bias_vector))
    grad_spectral, own, mirror = program.mix_back(own, mirror, weights, modes)
    own, other = program.spread_modes(own, mirror)
    grad_inputs = program.synthesise(own, other, linear)
    return (
        jnp.transpose(output, (0, 2, 1, 3)),
        jnp.transpose(grad_inputs, (0, 2, 1, 3)),
        jnp.transpose(grad_spectral, (0, 3, 1, 2, 4)),
    )


def solution(mesh):
    in_specs = (
        P(("groups", "slab"), "chan", None, None),
        P(("groups", "slab"), "chan", None, None),
        P("slab", "chan", None, None, None),
        P(),
        P(),
    )
    out_specs = (
        P(("groups", "slab"), "chan", None, None),
        P(("groups", "slab"), "chan", None, None),
        P(("groups", "slab"), "chan", None, None, None),
    )
    return jax.shard_map(local, mesh=mesh, in_specs=in_specs, out_specs=out_specs, check_vma=False)
```

```python
from functools import partial
import math

import jax
import jax.numpy as jnp
import ml_dtypes
import numpy as np
from jax import lax
from jax.experimental import pallas as pl
from jax.experimental.pallas import tpu as pltpu
from jax.sharding import PartitionSpec as P

f32 = jnp.float32
bf16 = jnp.bfloat16
root_half = 0.7071067811865476
inv_root_two_pi = 0.3989422804014327
VMEM_LIMIT = 60 * 1024 * 1024
NT = (((1,), (1,)), ((), ()))
TN = (((0,), (0,)), ((), ()))


def round_up(value, unit):
    return -(-value // unit) * unit


class Plan:
    def __init__(self, nx, ny, nz, channels, wb, wk, mx, slab_count, chan_count):
        self.nx, self.ny, self.nz, self.c = nx, ny, nz, channels
        self.wb, self.wk, self.mx = wb, wk, mx
        self.s, self.ch = slab_count, chan_count
        self.half = chan_count // 2
        self.na = mx // 2 + 1
        self.span = (wb + 1) * self.na
        self.lw = slab_count * self.span
        self.lp = round_up(self.lw, 128)
        self.ll = round_up(2 * self.span, 128)
        self.mk = self.half * wk
        self.rc = round_up(2 * self.mk + 2 * self.half, 8)
        self.rt = round_up(channels * (wk + 1), 8)
        self.xb = math.gcd(8, nx)
        self.blk = self.xb * ny
        self.rows = channels * wk
        self.lb = math.gcd(4, nx)
        self.batch = max(d for d in range(1, 5) if channels % d == 0)
        self.full_x, self.full_y = nx * slab_count, ny * chan_count

    def starts(self):
        kept = self.wb * self.s
        return [g * self.wb - (kept if 2 * g >= self.s else 0) for g in range(self.s)]

    def columns(self):
        b = np.concatenate([np.repeat(np.arange(st, st + self.wb + 1), self.na) for st in self.starts()])
        a = np.tile(np.arange(self.na), self.s * (self.wb + 1))
        return a, b

    def plane_table(self):
        a, b = self.columns()
        x = np.repeat(np.arange(self.nx), self.ny)[:, None]
        y = np.tile(np.arange(self.ny), self.nx)[:, None]
        total = self.full_x * self.full_y
        phase = (a * x * self.full_y + b * y * self.full_x) % total * (2.0 * np.pi / total)
        table = np.zeros((self.nx * self.ny, 2 * self.lp))
        scale = 1.0 / math.sqrt(total)
        table[:, : self.lw] = np.cos(phase) * scale
        table[:, self.lp : self.lp + self.lw] = -np.sin(phase) * scale
        high, low = (t.reshape(self.nx // self.xb, 1, self.blk, 2 * self.lp) for t in halves(table))
        return np.concatenate([high, high, low], 1).reshape(-1, 3 * self.blk, 2 * self.lp)

    def turns(self):
        a, b = self.columns()
        x = (np.arange(self.s) * self.nx)[:, None, None]
        y = (np.arange(self.ch) * self.ny)[None, :, None]
        total = self.full_x * self.full_y
        phase = (a * x * self.full_y + b * y * self.full_x) % total * (2.0 * np.pi / total)
        table = np.zeros((self.s, self.ch, 2, self.lp), np.float32)
        table[:, :, 0, : self.lw] = np.cos(phase)
        table[:, :, 1, : self.lw] = np.sin(phase)
        return table

    def depth_rows(self):
        main = np.arange(self.mk)
        edge = (np.arange(self.half) + 1) * self.wk
        z = np.arange(self.nz)
        scale = 1.0 / math.sqrt(self.nz)
        angle = lambda k: (k[:, None] * z) % self.nz * (2.0 * np.pi / self.nz)
        rows = [np.cos(angle(main)), np.sin(angle(main)), np.cos(angle(edge)), np.sin(angle(edge))]
        table = np.zeros((self.rc, self.nz))
        table[: 2 * self.mk + 2 * self.half] = np.concatenate(rows) * scale
        return halves(table)

    def depth_forward(self):
        high, low = self.depth_rows()
        return np.concatenate(
            [np.concatenate([high, high], 1), np.concatenate([low, np.zeros_like(low)], 1)], 0
        )

    def depth_inverse(self):
        high, low = self.depth_rows()
        table = np.zeros((round_up(3 * self.rc, 16), self.nz), ml_dtypes.bfloat16)
        table[: 3 * self.rc] = np.concatenate([high, high, low], 0)
        return table

    def selections(self):
        quarters = 128 // self.mx
        own = np.zeros((self.wb, 2, self.ll, 2, quarters, self.mx), np.float32)
        for b in range(self.wb):
            for r in range(2):
                for a in range(self.mx):
                    if a < self.mx // 2:
                        own[b, 0, r * self.span + b * self.na + a, r, :, a] = 1.0
                    else:
                        spot = r * self.span + (self.wb - b) * self.na + self.mx - a
                        own[b, 1, spot, r, :, a] = 1.0 - 2.0 * r
        own = own.reshape(self.wb, 2 * self.ll, 256)
        back = np.swapaxes(own, 1, 2)
        return own.astype(ml_dtypes.bfloat16), np.ascontiguousarray(back).astype(ml_dtypes.bfloat16)

    def orders(self):
        table = np.zeros((2, self.rows, self.rt), np.float32)
        for c in range(self.c):
            for k in range(self.wk):
                table[0, c * self.wk + k, c * self.wk + k] = 1.0
                mirrored = self.wk - k
                spot = self.rows + c if mirrored == self.wk else c * self.wk + mirrored
                table[1, c * self.wk + k, spot] = 1.0
        return table.astype(ml_dtypes.bfloat16)


def halves(table):
    high = table.astype(np.float32).astype(ml_dtypes.bfloat16)
    low = (table - high.astype(np.float64)).astype(np.float32).astype(ml_dtypes.bfloat16)
    return high, low


def dot(left, right, numbers=(((1,), (0,)), ((), ()))):
    return lax.dot_general(left, right, numbers, preferred_element_type=f32)


def split(value):
    high = value.astype(bf16)
    return high, (value - high.astype(f32)).astype(bf16)


def moved(value, chosen, left=False):
    first, second = split(value)
    if left:
        return dot(chosen, first) + dot(chosen, second)
    rows = value.shape[0]
    if rows % 16:
        return dot(first, chosen) + dot(second, chosen)
    both = dot(jnp.concatenate([first, second], axis=0), chosen)
    return both[:rows] + both[rows:]


def depth_analysis(plan, table_ref, values):
    rows = []
    for value in values:
        high, low = split(value)
        rows.append(jnp.concatenate([high, low], axis=1))
    both = dot(table_ref[...], jnp.concatenate(rows, axis=0), NT)
    lines = both[: plan.rc] + both[plan.rc :]
    return [lines[:, j * plan.blk : (j + 1) * plan.blk] for j in range(len(values))]


def depth_synthesis(plan, table_ref, rows):
    high = rows.astype(bf16).astype(f32)
    parts = [high, rows - high, high]
    extra = table_ref.shape[0] - 3 * plan.rc
    if extra:
        parts.append(jnp.zeros((extra, rows.shape[1]), f32))
    return dot(jnp.concatenate(parts, axis=0).astype(bf16), table_ref[...], TN)


def plane_analysis(plan, step, lines_ref, plane_ref, total_ref):
    high, low = split(lines_ref[...].reshape(plan.c * plan.rc, plan.blk))
    rows = jnp.concatenate([high, low, high], axis=1)
    for start in range(0, 2 * plan.lp, 256):
        size = min(256, 2 * plan.lp - start)
        columns = pl.ds(start, size)
        part = dot(rows, plane_ref[0, :, columns]).reshape(plan.c, plan.rc, size)

        @pl.when(step == 0)
        def _():
            total_ref[:, :, columns] = part

        @pl.when(step > 0)
        def _():
            total_ref[:, :, columns] += part


def plane_synthesis(plan, high_rows, low_rows, plane_ref, lines_ref):
    high_table, low_table = plane_ref[0, : plan.blk], plane_ref[0, 2 * plan.blk :]
    lines = (
        dot(high_rows[...], high_table, NT)
        + dot(low_rows[...], high_table, NT)
        + dot(high_rows[...], low_table, NT)
    )
    lines_ref[...] = lines.reshape(plan.c, plan.rc, plan.blk)


def emit_modes(plan, flag_ref, turn_ref, total_ref, keep_ref, send_ref):
    lp, wk, mk, half = plan.lp, plan.wk, plan.mk, plan.half
    odd = flag_ref[0] == 1
    cosine, sine = turn_ref[0:1, :], turn_ref[1:2, :]
    for c in range(plan.c):
        real, imag = total_ref[c, :, :lp], total_ref[c, :, lp:]
        real, imag = real * cosine + imag * sine, imag * cosine - real * sine
        for first, size, base, shift in ((0, wk, c * wk, mk), (2 * mk, 1, plan.rows + c, half)):
            made = []
            for g in range(plan.ch):
                h = g if g < half else plan.ch - 1 - g
                even_rows = slice(first + h * size, first + (h + 1) * size)
                odd_rows = slice(first + shift + h * size, first + shift + (h + 1) * size)
                if g < half:
                    made.append((real[even_rows] + imag[odd_rows], imag[even_rows] - real[odd_rows]))
                else:
                    made.append((real[even_rows] - imag[odd_rows], imag[even_rows] + real[odd_rows]))
            for pair in range(half):
                for r in range(2):
                    low, high = made[2 * pair][r], made[2 * pair + 1][r]
                    keep_ref[pair, r, base : base + size, :] = jnp.where(odd, high, low)
                    send_ref[pair, r, base : base + size, :] = jnp.where(odd, low, high)
    used = plan.c * (wk + 1)
    if used < plan.rt:
        blank = jnp.zeros((plan.half, 2, plan.rt - used, lp), f32)
        keep_ref[:, :, used:, :] = blank
        send_ref[:, :, used:, :] = blank


def take_modes(plan, flag_ref, turn_ref, own_ref, other_ref, total_ref, high_rows, low_rows):
    lp, wk, mk, half = plan.lp, plan.wk, plan.mk, plan.half
    odd = flag_ref[0] == 1
    cosine, sine = turn_ref[0:1, :], turn_ref[1:2, :]

    def group(g, r, rows):
        own, other = own_ref[g // 2, r, rows, :], other_ref[g // 2, r, rows, :]
        return jnp.where(odd, own, other) if g % 2 else jnp.where(odd, other, own)

    for c in range(plan.c):
        for first, size, base, shift in ((0, wk, c * wk, mk), (2 * mk, 1, plan.rows + c, half)):
            rows = slice(base, base + size)
            for h in range(half):
                plus = [group(h, r, rows) for r in range(2)]
                minus = [group(plan.ch - 1 - h, r, rows) for r in range(2)]
                real, imag = plus[0] + minus[0], plus[1] + minus[1]
                here = slice(first + h * size, first + (h + 1) * size)
                total_ref[c, here, :lp] = real * cosine - imag * sine
                total_ref[c, here, lp:] = imag * cosine + real * sine
                real, imag = plus[0] - minus[0], plus[1] - minus[1]
                here = slice(first + shift + h * size, first + shift + (h + 1) * size)
                total_ref[c, here, :lp] = -(imag * cosine + real * sine)
                total_ref[c, here, lp:] = real * cosine - imag * sine
        used = 2 * mk + 2 * half
        if used < plan.rc:
            total_ref[c, used:, :] = jnp.zeros((plan.rc - used, 2 * lp), f32)
    high, low = split(total_ref[...].reshape(plan.c * plan.rc, 2 * lp))
    high_rows[...] = high
    low_rows[...] = low


def analyse_kernel(plan, flag_ref, values_ref, plane_ref, depth_ref, turn_ref, keep_ref, send_ref, lines_ref, total_ref):
    step = pl.program_id(0)

    @pl.loop(0, plan.c, step=plan.batch)
    def _(c):
        values = [values_ref[:, c + j].reshape(plan.blk, plan.nz) for j in range(plan.batch)]
        for j, lines in enumerate(depth_analysis(plan, depth_ref, values)):
            lines_ref[c + j] = lines

    plane_analysis(plan, step, lines_ref, plane_ref, total_ref)

    @pl.when(step == pl.num_programs(0) - 1)
    def _():
        emit_modes(plan, flag_ref, turn_ref, total_ref, keep_ref, send_ref)


def fields(plan, inverse_ref, lines_ref, first):
    lines = jnp.concatenate([lines_ref[first + j] for j in range(plan.batch)], axis=1)
    values = depth_synthesis(plan, inverse_ref, lines)
    return [values[j * plan.blk : (j + 1) * plan.blk] for j in range(plan.batch)]


def middle_kernel(
    plan, flag_ref, own_ref, other_ref, linear_ref, cotangent_ref, plane_ref, depth_ref, inverse_ref, turn_ref,
    output_ref, gradient_ref, keep_ref, send_ref, lines_ref, back_ref, total_ref, high_rows, low_rows,
):
    step = pl.program_id(0)

    @pl.when(step == 0)
    def _():
        take_modes(plan, flag_ref, turn_ref, own_ref, other_ref, total_ref, high_rows, low_rows)

    plane_synthesis(plan, high_rows, low_rows, plane_ref, lines_ref)
    shape = (plan.xb, plan.ny, plan.nz)

    @pl.loop(0, plan.c, step=plan.batch)
    def _(first):
        gradients = []
        for j, field in enumerate(fields(plan, inverse_ref, lines_ref, first)):
            value = field + linear_ref[:, first + j].reshape(plan.blk, plan.nz)
            gate = 0.5 * (1.0 + lax.erf(value * root_half))
            slope = gate + value * jnp.exp(-0.5 * value * value) * inv_root_two_pi
            output_ref[:, first + j] = (value * gate).reshape(shape)
            gradients.append(cotangent_ref[:, first + j].reshape(plan.blk, plan.nz) * slope)
            gradient_ref[:, first + j] = gradients[-1].reshape(shape)
        for j, lines in enumerate(depth_analysis(plan, depth_ref, gradients)):
            back_ref[first + j] = lines

    plane_analysis(plan, step, back_ref, plane_ref, total_ref)

    @pl.when(step == pl.num_programs(0) - 1)
    def _():
        emit_modes(plan, flag_ref, turn_ref, total_ref, keep_ref, send_ref)


def synthesise_kernel(
    plan, flag_ref, own_ref, other_ref, linear_ref, plane_ref, inverse_ref, turn_ref,
    output_ref, lines_ref, total_ref, high_rows, low_rows,
):
    @pl.when(pl.program_id(0) == 0)
    def _():
        take_modes(plan, flag_ref, turn_ref, own_ref, other_ref, total_ref, high_rows, low_rows)

    plane_synthesis(plan, high_rows, low_rows, plane_ref, lines_ref)

    @pl.loop(0, plan.c, step=plan.batch)
    def _(first):
        for j, field in enumerate(fields(plan, inverse_ref, lines_ref, first)):
            value = field + linear_ref[:, first + j].reshape(plan.blk, plan.nz)
            output_ref[:, first + j] = value.reshape(plan.xb, plan.ny, plan.nz)


def linear_kernel(plan, after_ref, values_ref, matrix_ref, bias_ref, output_ref):
    tiles = [(x, slice(t * 8, (t + 1) * 8)) for x in range(plan.lb) for t in range(plan.ny // 8)]
    values = [values_ref[x, :, t, :].reshape(plan.c * 8, plan.nz) for x, t in tiles]
    high, low = split(jnp.concatenate(values, axis=1))
    high_matrix, low_matrix = split(matrix_ref[...])
    matrix = jnp.concatenate([high_matrix, high_matrix, low_matrix], axis=1)
    mixed = dot(matrix, jnp.concatenate([high, low, high], axis=0)) + bias_ref[...]
    for n, (x, t) in enumerate(tiles):
        output_ref[x, :, t, :] = mixed[:, n * plan.nz : (n + 1) * plan.nz].reshape(plan.c, 8, plan.nz)


def pick(plan, own_ref, mirror_ref, order_ref, chosen_ref, ordered_ref):
    @pl.when(pl.program_id(0) == 0)
    def _():
        ordered_ref[:, : plan.ll] = moved(own_ref[...], order_ref[...], left=True)
        ordered_ref[:, plan.ll :] = moved(mirror_ref[...], order_ref[...], left=True)

    return moved(ordered_ref[...], chosen_ref[0])


def give(plan, made_ref, order_ref, back_ref, own_ref, mirror_ref, sums_ref):
    part = moved(made_ref[...], back_ref[0])
    step = pl.program_id(0)

    @pl.when(step == 0)
    def _():
        sums_ref[...] = part

    @pl.when(step > 0)
    def _():
        sums_ref[...] += part

    @pl.when(step == pl.num_programs(0) - 1)
    def _():
        own_ref[...] = moved(sums_ref[:, : plan.ll], order_ref[...], left=True)
        mirror_ref[...] = moved(sums_ref[:, plan.ll :], order_ref[...], left=True)


def mix_kernel(
    plan, after_ref, own_ref, mirror_ref, order_ref, disorder_ref, chosen_ref, back_ref, weight_ref,
    modes_ref, own_out, mirror_out, ordered_ref, made_ref, sums_ref,
):
    wk, quarters = plan.wk, 128 // plan.mx
    modes = pick(plan, own_ref, mirror_ref, order_ref, chosen_ref, ordered_ref)
    modes_ref[0] = modes
    place = lax.broadcasted_iota(jnp.int32, (wk, 128), 1) // plan.mx
    for t in range(plan.c // quarters):
        columns = slice(t * 128, (t + 1) * 128)
        real = imag = 0.0
        for i in range(plan.c):
            x_real, x_imag = modes[i * wk : (i + 1) * wk, :128], modes[i * wk : (i + 1) * wk, 128:]
            w_real, w_imag = weight_ref[0, 0, i, :, columns], weight_ref[0, 1, i, :, columns]
            real = real + (w_real * x_real - w_imag * x_imag)
            imag = imag + (w_real * x_imag + w_imag * x_real)
        for q in range(quarters):
            o = t * quarters + q
            made_ref[o * wk : (o + 1) * wk, :128] = jnp.where(place == q, real, 0.0)
            made_ref[o * wk : (o + 1) * wk, 128:] = jnp.where(place == q, imag, 0.0)
    give(plan, made_ref, disorder_ref, back_ref, own_out, mirror_out, sums_ref)


def mix_back_kernel(
    plan, after_ref, own_ref, mirror_ref, order_ref, disorder_ref, chosen_ref, back_ref, weight_ref, modes_ref,
    gradient_ref, own_out, mirror_out, ordered_ref, made_ref, sums_ref,
):
    wk, quarters = plan.wk, 128 // plan.mx
    grads = pick(plan, own_ref, mirror_ref, order_ref, chosen_ref, ordered_ref)
    place = lax.broadcasted_iota(jnp.int32, (wk, 128), 1) // plan.mx
    lined = []
    for t in range(plan.c // quarters):
        real = imag = 0.0
        for q in range(quarters):
            o = t * quarters + q
            real = jnp.where(place == q, grads[o * wk : (o + 1) * wk, :128], real)
            imag = jnp.where(place == q, grads[o * wk : (o + 1) * wk, 128:], imag)
        lined.append((real, imag))
    for i in range(plan.c):
        rows = slice(i * wk, (i + 1) * wk)
        x_real, x_imag = modes_ref[0, rows, :128], modes_ref[0, rows, 128:]
        back_real = back_imag = 0.0
        for t, (real, imag) in enumerate(lined):
            columns = slice(t * 128, (t + 1) * 128)
            gradient_ref[0, 0, i, :, columns] = real * x_real + imag * x_imag
            gradient_ref[0, 1, i, :, columns] = imag * x_real - real * x_imag
            w_real, w_imag = weight_ref[0, 0, i, :, columns], weight_ref[0, 1, i, :, columns]
            back_real = back_real + (w_real * real + w_imag * imag)
            back_imag = back_imag + (w_real * imag - w_imag * real)
        made_ref[rows, :128] = back_real
        made_ref[rows, 128:] = back_imag
    give(plan, made_ref, disorder_ref, back_ref, own_out, mirror_out, sums_ref)


def whole(array):
    zeros = (0,) * array.ndim
    return pl.BlockSpec(array.shape, lambda i: zeros, pipeline_mode=pl.Buffered(1))


def whole_shape(shape):
    zeros = (0,) * len(shape)
    return pl.BlockSpec(shape, lambda i: zeros, pipeline_mode=pl.Buffered(1))


def leading(shape):
    rest = (0,) * (len(shape) - 1)
    return pl.BlockSpec(shape, lambda i: (i,) + rest)


def shaped(*shape):
    return jax.ShapeDtypeStruct(shape, f32)


def anywhere():
    return pl.BlockSpec(memory_space=pl.ANY)


def scalar():
    return pl.BlockSpec(memory_space=pltpu.SMEM)


def call(kernel, name, grid, in_specs, out_specs, out_shape, scratch, flops, size):
    return pl.pallas_call(
        kernel,
        grid=(grid,),
        in_specs=in_specs,
        out_specs=out_specs,
        out_shape=out_shape,
        scratch_shapes=scratch,
        name=name,
        compiler_params=pltpu.CompilerParams(vmem_limit_bytes=VMEM_LIMIT, dimension_semantics=("arbitrary",)),
        cost_estimate=pl.CostEstimate(flops=flops, bytes_accessed=size, transcendentals=0),
    )


class Program:
    def __init__(self, plan):
        self.plan = plan
        self.plane = jnp.asarray(plan.plane_table())
        self.depth = jnp.asarray(plan.depth_forward())
        self.inverse = jnp.asarray(plan.depth_inverse())
        slab, chan = lax.axis_index("slab"), lax.axis_index("chan")
        self.slab, self.chan = slab, chan
        turns = jnp.asarray(plan.turns())
        self.turn = lax.dynamic_index_in_dim(
            lax.dynamic_index_in_dim(turns, slab, 0, False), chan, 0, False
        )
        self.flag = (chan % 2).astype(jnp.int32).reshape(1)
        orders = jnp.asarray(plan.orders())
        upper = (chan >= plan.half).astype(jnp.int32)
        self.order = lax.dynamic_index_in_dim(orders, upper, 0, False)
        self.disorder = self.order.T
        chosen, back = plan.selections()
        self.chosen, self.back = jnp.asarray(chosen), jnp.asarray(back)
        self.matmul = 6 * plan.c * plan.rc * 2 * plan.lp * plan.nx * plan.ny
        self.field = plan.nx * plan.ny * plan.nz * plan.c * 4

    def half_shape(self):
        plan = self.plan
        return (plan.half, 2, plan.rt, plan.lp)

    def field_spec(self):
        plan = self.plan
        return leading((plan.xb, plan.c, plan.ny, plan.nz))

    def table(self):
        plan = self.plan
        return leading((1, 3 * plan.blk, 2 * plan.lp))

    def lines(self):
        plan = self.plan
        return pltpu.VMEM((plan.c, plan.rc, plan.blk), f32)

    def spectra(self):
        plan = self.plan
        rows = pltpu.VMEM((plan.c * plan.rc, 2 * plan.lp), bf16)
        return [pltpu.VMEM((plan.c, plan.rc, 2 * plan.lp), f32), rows, rows]

    def analyse(self, values):
        plan = self.plan
        half = self.half_shape()
        return call(
            partial(analyse_kernel, plan), "analyse", plan.nx // plan.xb,
            [scalar(), self.field_spec(), self.table(), whole(self.depth), whole(self.turn)],
            [whole_shape(half)] * 2, [shaped(*half)] * 2,
            [self.lines(), self.spectra()[0]], self.matmul, self.field,
        )(self.flag, values, self.plane, self.depth, self.turn)

    def middle(self, own, other, linear, cotangent):
        plan = self.plan
        half = self.half_shape()
        field = shaped(plan.nx, plan.c, plan.ny, plan.nz)
        return call(
            partial(middle_kernel, plan), "middle", plan.nx // plan.xb,
            [scalar(), whole_shape(half), whole_shape(half), self.field_spec(), self.field_spec(), self.table(),
             whole(self.depth), whole(self.inverse), whole(self.turn)],
            [self.field_spec(), self.field_spec(), whole_shape(half), whole_shape(half)],
            [field, field, shaped(*half), shaped(*half)],
            [self.lines(), self.lines(), *self.spectra()], 2 * self.matmul, 4 * self.field,
        )(self.flag, own, other, linear, cotangent, self.plane, self.depth, self.inverse, self.turn)

    def synthesise(self, own, other, linear):
        plan = self.plan
        half = self.half_shape()
        return call(
            partial(synthesise_kernel, plan), "synthesise", plan.nx // plan.xb,
            [scalar(), whole_shape(half), whole_shape(half), self.field_spec(), self.table(),
             whole(self.inverse), whole(self.turn)],
            self.field_spec(), shaped(plan.nx, plan.c, plan.ny, plan.nz),
            [self.lines(), *self.spectra()], self.matmul, 2 * self.field,
        )(self.flag, own, other, linear, self.plane, self.inverse, self.turn)

    def linear(self, after, values, matrix, bias):
        plan = self.plan
        wide = jnp.kron(matrix, jnp.eye(8, dtype=f32))
        column = jnp.repeat(bias, 8)[:, None]
        spec = leading((plan.lb, plan.c, plan.ny, plan.nz))
        return call(
            partial(linear_kernel, plan), "linear", plan.nx // plan.lb,
            [anywhere(), spec, whole(wide), whole(column)],
            spec, shaped(plan.nx, plan.c, plan.ny, plan.nz), [],
            6 * (8 * plan.c) ** 2 * plan.nx * plan.ny // 8 * plan.nz, 2 * self.field,
        )(after, values, wide, column)

    def mix_specs(self):
        plan = self.plan
        modes = (plan.rt, plan.ll)
        ins = [
            anywhere(), whole_shape(modes), whole_shape(modes), whole(self.order), whole(self.disorder),
            leading((1,) + self.chosen.shape[1:]), leading((1,) + self.back.shape[1:]),
            leading((1, 2, plan.c, plan.wk, plan.c * plan.mx)),
        ]
        scratch = [
            pltpu.VMEM((plan.rows, 2 * plan.ll), f32),
            pltpu.VMEM((plan.rows, 256), f32),
            pltpu.VMEM((plan.rows, 2 * plan.ll), f32),
        ]
        return ins, [whole_shape(modes)] * 2, [shaped(*modes)] * 2, scratch

    def mix(self, after, own, mirror, weights):
        plan = self.plan
        ins, outs, shapes, scratch = self.mix_specs()
        kept = leading((1, plan.rows, 256))
        return call(
            partial(mix_kernel, plan), "mix", plan.wb, ins, [kept, *outs],
            [shaped(plan.wb, plan.rows, 256), *shapes], scratch, 10**9, 4 * weights.size,
        )(after, own, mirror, self.order, self.disorder, self.chosen, self.back, weights)

    def mix_back(self, after, own, mirror, weights, modes):
        plan = self.plan
        ins, outs, shapes, scratch = self.mix_specs()
        kept = leading((1, plan.rows, 256))
        return call(
            partial(mix_back_kernel, plan), "mix_back", plan.wb, ins + [kept], [ins[-1], *outs],
            [shaped(*weights.shape), *shapes], scratch, 10**9, 8 * weights.size,
        )(after, own, mirror, self.order, self.disorder, self.chosen, self.back, weights, modes)

    def across(self, value, axis, bit):
        size = lax.axis_size(axis)
        return lax.ppermute(value, axis, [(i, i ^ bit) for i in range(size)])

    def mirrored(self, value):
        total = self.plan.s * self.plan.ch
        return lax.ppermute(value, ("slab", "chan"), [(i, total - 1 - i) for i in range(total)])

    def gather_sums(self, keep, send):
        plan = self.plan
        total = keep + self.across(send, "chan", 1)
        bit = 2
        while bit < plan.ch:
            mine = (self.chan // bit) % 2
            pairs = total.reshape((total.shape[0] // 2, 2) + total.shape[1:])
            send = lax.dynamic_index_in_dim(pairs, 1 - mine, 1, False)
            total = lax.dynamic_index_in_dim(pairs, mine, 1, False) + self.across(send, "chan", bit)
            bit *= 2
        total = total[0]
        blank = jnp.zeros((plan.rt, plan.ll - 2 * plan.span), f32)
        pieces = []
        for g in range(plan.s):
            window = slice(g * plan.span, (g + 1) * plan.span)
            pieces.append(jnp.concatenate([total[0, :, window], total[1, :, window], blank], axis=1))
        pieces = jnp.stack(pieces)
        mine = lax.dynamic_index_in_dim(pieces, self.slab, 0, False)
        arrived = [
            self.across(lax.dynamic_index_in_dim(pieces, self.slab ^ j, 0, False), "slab", j)
            for j in range(1, plan.s)
        ]
        for piece in arrived:
            mine = mine + piece
        return mine, self.mirrored(mine)

    def spread_modes(self, own, mirror):
        plan = self.plan
        mine = own + self.mirrored(mirror)
        held = jnp.stack([mine] + [self.across(mine, "slab", j) for j in range(1, plan.s)])
        pieces = [lax.dynamic_index_in_dim(held, self.slab ^ g, 0, False) for g in range(plan.s)]
        blank = jnp.zeros((plan.rt, plan.lp - plan.lw), f32)
        total = jnp.stack([
            jnp.concatenate([p[:, r * plan.span : (r + 1) * plan.span] for p in pieces] + [blank], axis=1)
            for r in range(2)
        ])[None]
        bit = plan.ch // 2
        while bit > 1:
            other = self.across(total, "chan", bit)
            upper = (self.chan // bit) % 2 == 1
            total = jnp.stack([jnp.where(upper, other, total), jnp.where(upper, total, other)], axis=1)
            total = total.reshape((-1,) + total.shape[2:])
            bit //= 2
        return total, self.across(total, "chan", 1)


def local(inputs, cotangent, spectral, local_weight, bias_vector):
    nx, ny, channels, nz = inputs.shape
    wb, wk = spectral.shape[0], spectral.shape[1]
    plan = Plan(nx, ny, nz, channels, wb, wk, spectral.shape[4] // channels, lax.axis_size("slab"), lax.axis_size("chan"))
    program = Program(plan)
    values = jnp.transpose(inputs, (0, 2, 1, 3))
    weights = jnp.transpose(spectral, (0, 2, 3, 1, 4))
    keep, send = program.analyse(values)
    linear = program.linear(send, values, local_weight.T, bias_vector)
    own, mirror = program.gather_sums(keep, send)
    modes, own, mirror = program.mix(linear, own, mirror, weights)
    own, other = program.spread_modes(own, mirror)
    output, gradient, keep, send = program.middle(own, other, linear, jnp.transpose(cotangent, (0, 2, 1, 3)))
    linear = program.linear(send, gradient, local_weight, jnp.zeros_like(bias_vector))
    own, mirror = program.gather_sums(keep, send)
    grad_spectral, own, mirror = program.mix_back(linear, own, mirror, weights, modes)
    own, other = program.spread_modes(own, mirror)
    grad_inputs = program.synthesise(own, other, linear)
    return (
        jnp.transpose(output, (0, 2, 1, 3)),
        jnp.transpose(grad_inputs, (0, 2, 1, 3)),
        jnp.transpose(grad_spectral, (0, 3, 1, 2, 4)),
    )


def solution(mesh):
    in_specs = (
        P(("groups", "slab"), "chan", None, None),
        P(("groups", "slab"), "chan", None, None),
        P("slab", "chan", None, None, None),
        P(),
        P(),
    )
    out_specs = (
        P(("groups", "slab"), "chan", None, None),
        P(("groups", "slab"), "chan", None, None),
        P(("groups", "slab"), "chan", None, None, None),
    )
    return jax.shard_map(local, mesh=mesh, in_specs=in_specs, out_specs=out_specs, check_vma=False)
```

```python
from functools import partial
import math

import jax
import jax.numpy as jnp
import ml_dtypes
import numpy as np
from jax import lax
from jax.experimental import pallas as pl
from jax.experimental.pallas import tpu as pltpu
from jax.sharding import PartitionSpec as P

f32 = jnp.float32
bf16 = jnp.bfloat16
root_half = 0.7071067811865476
inv_root_two_pi = 0.3989422804014327
VMEM_LIMIT = 60 * 1024 * 1024
NT = (((1,), (1,)), ((), ()))
TN = (((0,), (0,)), ((), ()))


def round_up(value, unit):
    return -(-value // unit) * unit


class Plan:
    def __init__(self, nx, ny, nz, channels, wb, wk, mx, slab_count, chan_count):
        self.nx, self.ny, self.nz, self.c = nx, ny, nz, channels
        self.wb, self.wk, self.mx = wb, wk, mx
        self.s, self.ch = slab_count, chan_count
        self.half = chan_count // 2
        self.na = mx // 2 + 1
        self.span = (wb + 1) * self.na
        self.lw = slab_count * self.span
        self.lp = round_up(self.lw, 128)
        self.ll = round_up(2 * self.span, 128)
        self.mk = self.half * wk
        self.rc = round_up(2 * self.mk + 2 * self.half, 8)
        self.chunks = math.gcd(2, channels)
        self.cc = channels // self.chunks
        self.rt = round_up(self.cc * (wk + 1), 8)
        self.xb = math.gcd(8, nx)
        self.blk = self.xb * ny
        self.rows = self.cc * wk
        self.lb = math.gcd(4, nx)
        self.batch = max(d for d in range(1, 6) if self.cc % d == 0)
        self.full_x, self.full_y = nx * slab_count, ny * chan_count

    def starts(self):
        kept = self.wb * self.s
        return [g * self.wb - (kept if 2 * g >= self.s else 0) for g in range(self.s)]

    def columns(self):
        b = np.concatenate([np.repeat(np.arange(st, st + self.wb + 1), self.na) for st in self.starts()])
        a = np.tile(np.arange(self.na), self.s * (self.wb + 1))
        return a, b

    def plane_table(self):
        a, b = self.columns()
        x = np.repeat(np.arange(self.nx), self.ny)[:, None]
        y = np.tile(np.arange(self.ny), self.nx)[:, None]
        total = self.full_x * self.full_y
        phase = (a * x * self.full_y + b * y * self.full_x) % total * (2.0 * np.pi / total)
        table = np.zeros((self.nx * self.ny, 2 * self.lp))
        scale = 1.0 / math.sqrt(total)
        table[:, : self.lw] = np.cos(phase) * scale
        table[:, self.lp : self.lp + self.lw] = -np.sin(phase) * scale
        high, low = (t.reshape(self.nx // self.xb, 1, self.blk, 2 * self.lp) for t in halves(table))
        return np.concatenate([high, high, low], 1).reshape(-1, 3 * self.blk, 2 * self.lp)

    def turns(self):
        a, b = self.columns()
        x = (np.arange(self.s) * self.nx)[:, None, None]
        y = (np.arange(self.ch) * self.ny)[None, :, None]
        total = self.full_x * self.full_y
        phase = (a * x * self.full_y + b * y * self.full_x) % total * (2.0 * np.pi / total)
        table = np.zeros((self.s, self.ch, 2, self.lp), np.float32)
        table[:, :, 0, : self.lw] = np.cos(phase)
        table[:, :, 1, : self.lw] = np.sin(phase)
        return table

    def depth_rows(self):
        main = np.arange(self.mk)
        edge = (np.arange(self.half) + 1) * self.wk
        z = np.arange(self.nz)
        scale = 1.0 / math.sqrt(self.nz)
        angle = lambda k: (k[:, None] * z) % self.nz * (2.0 * np.pi / self.nz)
        rows = [np.cos(angle(main)), np.sin(angle(main)), np.cos(angle(edge)), np.sin(angle(edge))]
        table = np.zeros((self.rc, self.nz))
        table[: 2 * self.mk + 2 * self.half] = np.concatenate(rows) * scale
        return halves(table)

    def depth_forward(self):
        high, low = self.depth_rows()
        return np.concatenate(
            [np.concatenate([high, high], 1), np.concatenate([low, np.zeros_like(low)], 1)], 0
        )

    def depth_inverse(self):
        high, low = self.depth_rows()
        table = np.zeros((round_up(3 * self.rc, 16), self.nz), ml_dtypes.bfloat16)
        table[: 3 * self.rc] = np.concatenate([high, high, low], 0)
        return table

    def selections(self):
        quarters = 128 // self.mx
        own = np.zeros((self.wb, 2, self.ll, 2, quarters, self.mx), np.float32)
        for b in range(self.wb):
            for r in range(2):
                for a in range(self.mx):
                    if a < self.mx // 2:
                        own[b, 0, r * self.span + b * self.na + a, r, :, a] = 1.0
                    else:
                        spot = r * self.span + (self.wb - b) * self.na + self.mx - a
                        own[b, 1, spot, r, :, a] = 1.0 - 2.0 * r
        own = own.reshape(self.wb, 2 * self.ll, 256)
        back = np.swapaxes(own, 1, 2)
        return own.astype(ml_dtypes.bfloat16), np.ascontiguousarray(back).astype(ml_dtypes.bfloat16)

    def orders(self):
        table = np.zeros((2, self.rows, self.rt), np.float32)
        for c in range(self.cc):
            for k in range(self.wk):
                table[0, c * self.wk + k, c * self.wk + k] = 1.0
                mirrored = self.wk - k
                spot = self.rows + c if mirrored == self.wk else c * self.wk + mirrored
                table[1, c * self.wk + k, spot] = 1.0
        return table.astype(ml_dtypes.bfloat16)


def halves(table):
    high = table.astype(np.float32).astype(ml_dtypes.bfloat16)
    low = (table - high.astype(np.float64)).astype(np.float32).astype(ml_dtypes.bfloat16)
    return high, low


def dot(left, right, numbers=(((1,), (0,)), ((), ()))):
    return lax.dot_general(left, right, numbers, preferred_element_type=f32)


def split(value):
    high = value.astype(bf16)
    return high, (value - high.astype(f32)).astype(bf16)


def moved(value, chosen, left=False):
    first, second = split(value)
    if left:
        return dot(chosen, first) + dot(chosen, second)
    rows = value.shape[0]
    if rows % 16:
        return dot(first, chosen) + dot(second, chosen)
    both = dot(jnp.concatenate([first, second], axis=0), chosen)
    return both[:rows] + both[rows:]


def depth_analysis(plan, table_ref, values):
    rows = []
    for value in values:
        high, low = split(value)
        rows.append(jnp.concatenate([high, low], axis=1))
    both = dot(table_ref[...], jnp.concatenate(rows, axis=0), NT)
    lines = both[: plan.rc] + both[plan.rc :]
    return [lines[:, j * plan.blk : (j + 1) * plan.blk] for j in range(len(values))]


def depth_synthesis(plan, table_ref, rows):
    high = rows.astype(bf16).astype(f32)
    parts = [high, rows - high, high]
    extra = table_ref.shape[0] - 3 * plan.rc
    if extra:
        parts.append(jnp.zeros((extra, rows.shape[1]), f32))
    return dot(jnp.concatenate(parts, axis=0).astype(bf16), table_ref[...], TN)


def plane_analysis(plan, step, lines_ref, plane_ref, total_ref):
    high, low = split(lines_ref[...].reshape(plan.cc * plan.rc, plan.blk))
    rows = jnp.concatenate([high, low, high], axis=1)
    for start in range(0, 2 * plan.lp, 256):
        size = min(256, 2 * plan.lp - start)
        columns = pl.ds(start, size)
        part = dot(rows, plane_ref[0, :, columns]).reshape(plan.cc, plan.rc, size)

        @pl.when(step == 0)
        def _():
            total_ref[:, :, columns] = part

        @pl.when(step > 0)
        def _():
            total_ref[:, :, columns] += part


def plane_synthesis(plan, high_rows, low_rows, plane_ref, lines_ref):
    high_table, low_table = plane_ref[0, : plan.blk], plane_ref[0, 2 * plan.blk :]
    lines = (
        dot(high_rows[...], high_table, NT)
        + dot(low_rows[...], high_table, NT)
        + dot(high_rows[...], low_table, NT)
    )
    lines_ref[...] = lines.reshape(plan.cc, plan.rc, plan.blk)


def emit_modes(plan, flag_ref, turn_ref, total_ref, keep_ref, send_ref):
    lp, wk, mk, half = plan.lp, plan.wk, plan.mk, plan.half
    odd = flag_ref[0] == 1
    cosine, sine = turn_ref[0:1, :], turn_ref[1:2, :]
    for c in range(plan.cc):
        real, imag = total_ref[c, :, :lp], total_ref[c, :, lp:]
        real, imag = real * cosine + imag * sine, imag * cosine - real * sine
        for first, size, base, shift in ((0, wk, c * wk, mk), (2 * mk, 1, plan.rows + c, half)):
            made = []
            for g in range(plan.ch):
                h = g if g < half else plan.ch - 1 - g
                even_rows = slice(first + h * size, first + (h + 1) * size)
                odd_rows = slice(first + shift + h * size, first + shift + (h + 1) * size)
                if g < half:
                    made.append((real[even_rows] + imag[odd_rows], imag[even_rows] - real[odd_rows]))
                else:
                    made.append((real[even_rows] - imag[odd_rows], imag[even_rows] + real[odd_rows]))
            for pair in range(half):
                for r in range(2):
                    low, high = made[2 * pair][r], made[2 * pair + 1][r]
                    keep_ref[pair, r, base : base + size, :] = jnp.where(odd, high, low)
                    send_ref[pair, r, base : base + size, :] = jnp.where(odd, low, high)
    used = plan.cc * (wk + 1)
    if used < plan.rt:
        blank = jnp.zeros((plan.half, 2, plan.rt - used, lp), f32)
        keep_ref[:, :, used:, :] = blank
        send_ref[:, :, used:, :] = blank


def take_modes(plan, flag_ref, turn_ref, own_ref, other_ref, total_ref, high_rows, low_rows):
    lp, wk, mk, half = plan.lp, plan.wk, plan.mk, plan.half
    odd = flag_ref[0] == 1
    cosine, sine = turn_ref[0:1, :], turn_ref[1:2, :]

    def group(g, r, rows):
        own, other = own_ref[g // 2, r, rows, :], other_ref[g // 2, r, rows, :]
        return jnp.where(odd, own, other) if g % 2 else jnp.where(odd, other, own)

    for c in range(plan.cc):
        for first, size, base, shift in ((0, wk, c * wk, mk), (2 * mk, 1, plan.rows + c, half)):
            rows = slice(base, base + size)
            for h in range(half):
                plus = [group(h, r, rows) for r in range(2)]
                minus = [group(plan.ch - 1 - h, r, rows) for r in range(2)]
                real, imag = plus[0] + minus[0], plus[1] + minus[1]
                here = slice(first + h * size, first + (h + 1) * size)
                total_ref[c, here, :lp] = real * cosine - imag * sine
                total_ref[c, here, lp:] = imag * cosine + real * sine
                real, imag = plus[0] - minus[0], plus[1] - minus[1]
                here = slice(first + shift + h * size, first + shift + (h + 1) * size)
                total_ref[c, here, :lp] = -(imag * cosine + real * sine)
                total_ref[c, here, lp:] = real * cosine - imag * sine
        used = 2 * mk + 2 * half
        if used < plan.rc:
            total_ref[c, used:, :] = jnp.zeros((plan.rc - used, 2 * lp), f32)
    high, low = split(total_ref[...].reshape(plan.cc * plan.rc, 2 * lp))
    high_rows[...] = high
    low_rows[...] = low


def analyse_kernel(plan, flag_ref, values_ref, plane_ref, depth_ref, turn_ref, keep_ref, send_ref, lines_ref, total_ref):
    step = pl.program_id(0)

    @pl.loop(0, plan.cc, step=plan.batch)
    def _(c):
        values = [values_ref[:, c + j].reshape(plan.blk, plan.nz) for j in range(plan.batch)]
        for j, lines in enumerate(depth_analysis(plan, depth_ref, values)):
            lines_ref[c + j] = lines

    plane_analysis(plan, step, lines_ref, plane_ref, total_ref)

    @pl.when(step == pl.num_programs(0) - 1)
    def _():
        emit_modes(plan, flag_ref, turn_ref, total_ref, keep_ref, send_ref)


def fields(plan, inverse_ref, lines_ref, first):
    lines = jnp.concatenate([lines_ref[first + j] for j in range(plan.batch)], axis=1)
    values = depth_synthesis(plan, inverse_ref, lines)
    return [values[j * plan.blk : (j + 1) * plan.blk] for j in range(plan.batch)]


def middle_kernel(
    plan, flag_ref, own_ref, other_ref, linear_ref, cotangent_ref, plane_ref, depth_ref, inverse_ref, turn_ref,
    output_ref, gradient_ref, keep_ref, send_ref, lines_ref, back_ref, total_ref, high_rows, low_rows,
):
    step = pl.program_id(0)

    @pl.when(step == 0)
    def _():
        take_modes(plan, flag_ref, turn_ref, own_ref, other_ref, total_ref, high_rows, low_rows)

    plane_synthesis(plan, high_rows, low_rows, plane_ref, lines_ref)
    shape = (plan.xb, plan.ny, plan.nz)

    @pl.loop(0, plan.cc, step=plan.batch)
    def _(first):
        gradients = []
        for j, field in enumerate(fields(plan, inverse_ref, lines_ref, first)):
            value = field + linear_ref[:, first + j].reshape(plan.blk, plan.nz)
            gate = 0.5 * (1.0 + lax.erf(value * root_half))
            slope = gate + value * jnp.exp(-0.5 * value * value) * inv_root_two_pi
            output_ref[:, first + j] = (value * gate).reshape(shape)
            gradients.append(cotangent_ref[:, first + j].reshape(plan.blk, plan.nz) * slope)
            gradient_ref[:, first + j] = gradients[-1].reshape(shape)
        for j, lines in enumerate(depth_analysis(plan, depth_ref, gradients)):
            back_ref[first + j] = lines

    plane_analysis(plan, step, back_ref, plane_ref, total_ref)

    @pl.when(step == pl.num_programs(0) - 1)
    def _():
        emit_modes(plan, flag_ref, turn_ref, total_ref, keep_ref, send_ref)


def synthesise_kernel(
    plan, flag_ref, own_ref, other_ref, linear_ref, plane_ref, inverse_ref, turn_ref,
    output_ref, lines_ref, total_ref, high_rows, low_rows,
):
    @pl.when(pl.program_id(0) == 0)
    def _():
        take_modes(plan, flag_ref, turn_ref, own_ref, other_ref, total_ref, high_rows, low_rows)

    plane_synthesis(plan, high_rows, low_rows, plane_ref, lines_ref)

    @pl.loop(0, plan.cc, step=plan.batch)
    def _(first):
        for j, field in enumerate(fields(plan, inverse_ref, lines_ref, first)):
            value = field + linear_ref[:, first + j].reshape(plan.blk, plan.nz)
            output_ref[:, first + j] = value.reshape(plan.xb, plan.ny, plan.nz)


def linear_kernel(plan, values_ref, matrix_ref, bias_ref, output_ref):
    tiles = [(x, slice(t * 8, (t + 1) * 8)) for x in range(plan.lb) for t in range(plan.ny // 8)]
    values = [values_ref[x, :, t, :].reshape(plan.c * 8, plan.nz) for x, t in tiles]
    high, low = split(jnp.concatenate(values, axis=1))
    high_matrix, low_matrix = split(matrix_ref[...])
    matrix = jnp.concatenate([high_matrix, high_matrix, low_matrix], axis=1)
    mixed = dot(matrix, jnp.concatenate([high, low, high], axis=0)) + bias_ref[...]
    for n, (x, t) in enumerate(tiles):
        output_ref[x, :, t, :] = mixed[:, n * plan.nz : (n + 1) * plan.nz].reshape(plan.c, 8, plan.nz)


def pick(plan, own_refs, mirror_refs, order_ref, chosen_ref, ordered_ref):
    @pl.when(pl.program_id(0) == 0)
    def _():
        for n in range(plan.chunks):
            rows = slice(n * plan.rows, (n + 1) * plan.rows)
            ordered_ref[rows, : plan.ll] = moved(own_refs[n][...], order_ref[...], left=True)
            ordered_ref[rows, plan.ll :] = moved(mirror_refs[n][...], order_ref[...], left=True)

    return moved(ordered_ref[...], chosen_ref[0])


def give(plan, made_ref, order_ref, back_ref, own_refs, mirror_refs, sums_ref):
    part = moved(made_ref[...], back_ref[0])
    step = pl.program_id(0)

    @pl.when(step == 0)
    def _():
        sums_ref[...] = part

    @pl.when(step > 0)
    def _():
        sums_ref[...] += part

    @pl.when(step == pl.num_programs(0) - 1)
    def _():
        for n in range(plan.chunks):
            rows = slice(n * plan.rows, (n + 1) * plan.rows)
            own_refs[n][...] = moved(sums_ref[rows, : plan.ll], order_ref[...], left=True)
            mirror_refs[n][...] = moved(sums_ref[rows, plan.ll :], order_ref[...], left=True)


def mix_kernel(plan, *refs):
    n = plan.chunks
    owns, mirrors, refs = refs[:n], refs[n : 2 * n], refs[2 * n :]
    order_ref, disorder_ref, chosen_ref, back_ref, weight_ref, modes_ref = refs[:6]
    own_outs, mirror_outs, (ordered_ref, made_ref, sums_ref) = refs[6 : 6 + n], refs[6 + n : 6 + 2 * n], refs[6 + 2 * n :]
    wk, quarters = plan.wk, 128 // plan.mx
    modes = pick(plan, owns, mirrors, order_ref, chosen_ref, ordered_ref)
    modes_ref[0] = modes
    place = lax.broadcasted_iota(jnp.int32, (wk, 128), 1) // plan.mx
    for t in range(plan.c // quarters):
        columns = slice(t * 128, (t + 1) * 128)
        real = imag = 0.0
        for i in range(plan.c):
            x_real, x_imag = modes[i * wk : (i + 1) * wk, :128], modes[i * wk : (i + 1) * wk, 128:]
            w_real, w_imag = weight_ref[0, 0, i, :, columns], weight_ref[0, 1, i, :, columns]
            real = real + (w_real * x_real - w_imag * x_imag)
            imag = imag + (w_real * x_imag + w_imag * x_real)
        for q in range(quarters):
            o = t * quarters + q
            made_ref[o * wk : (o + 1) * wk, :128] = jnp.where(place == q, real, 0.0)
            made_ref[o * wk : (o + 1) * wk, 128:] = jnp.where(place == q, imag, 0.0)
    give(plan, made_ref, disorder_ref, back_ref, own_outs, mirror_outs, sums_ref)


def mix_back_kernel(plan, *refs):
    n = plan.chunks
    owns, mirrors, refs = refs[:n], refs[n : 2 * n], refs[2 * n :]
    order_ref, disorder_ref, chosen_ref, back_ref, weight_ref, modes_ref, gradient_ref = refs[:7]
    own_outs, mirror_outs, (ordered_ref, made_ref, sums_ref) = refs[7 : 7 + n], refs[7 + n : 7 + 2 * n], refs[7 + 2 * n :]
    wk, quarters = plan.wk, 128 // plan.mx
    grads = pick(plan, owns, mirrors, order_ref, chosen_ref, ordered_ref)
    place = lax.broadcasted_iota(jnp.int32, (wk, 128), 1) // plan.mx
    lined = []
    for t in range(plan.c // quarters):
        real = imag = 0.0
        for q in range(quarters):
            o = t * quarters + q
            real = jnp.where(place == q, grads[o * wk : (o + 1) * wk, :128], real)
            imag = jnp.where(place == q, grads[o * wk : (o + 1) * wk, 128:], imag)
        lined.append((real, imag))
    for i in range(plan.c):
        rows = slice(i * wk, (i + 1) * wk)
        x_real, x_imag = modes_ref[0, rows, :128], modes_ref[0, rows, 128:]
        back_real = back_imag = 0.0
        for t, (real, imag) in enumerate(lined):
            columns = slice(t * 128, (t + 1) * 128)
            gradient_ref[0, 0, i, :, columns] = real * x_real + imag * x_imag
            gradient_ref[0, 1, i, :, columns] = imag * x_real - real * x_imag
            w_real, w_imag = weight_ref[0, 0, i, :, columns], weight_ref[0, 1, i, :, columns]
            back_real = back_real + (w_real * real + w_imag * imag)
            back_imag = back_imag + (w_real * imag - w_imag * real)
        made_ref[rows, :128] = back_real
        made_ref[rows, 128:] = back_imag
    give(plan, made_ref, disorder_ref, back_ref, own_outs, mirror_outs, sums_ref)


def whole(array):
    zeros = (0,) * array.ndim
    return pl.BlockSpec(array.shape, lambda i: zeros, pipeline_mode=pl.Buffered(1))


def whole_shape(shape):
    zeros = (0,) * len(shape)
    return pl.BlockSpec(shape, lambda i: zeros, pipeline_mode=pl.Buffered(1))


def leading(shape):
    rest = (0,) * (len(shape) - 1)
    return pl.BlockSpec(shape, lambda i: (i,) + rest)


def shaped(*shape):
    return jax.ShapeDtypeStruct(shape, f32)


def anywhere():
    return pl.BlockSpec(memory_space=pl.ANY)


def scalar():
    return pl.BlockSpec(memory_space=pltpu.SMEM)


def call(kernel, name, grid, in_specs, out_specs, out_shape, scratch, cost, before=(), aliases=None):
    skipped = len(before)
    run = pl.pallas_call(
        lambda *refs: kernel(*refs[skipped:]),
        grid=(grid,),
        in_specs=[anywhere()] * skipped + list(in_specs),
        out_specs=out_specs,
        out_shape=out_shape,
        scratch_shapes=scratch,
        name=name,
        input_output_aliases=aliases or {},
        compiler_params=pltpu.CompilerParams(vmem_limit_bytes=VMEM_LIMIT, dimension_semantics=("arbitrary",)),
        cost_estimate=pl.CostEstimate(flops=int(cost * 1.15e9), bytes_accessed=int(cost * 3.6e6), transcendentals=0),
    )
    return partial(run, *before)


def tie(value, *before):
    if not before:
        return value
    return pl.pallas_call(
        lambda *refs: None,
        in_specs=[anywhere()] * (1 + len(before)),
        out_specs=anywhere(),
        out_shape=jax.ShapeDtypeStruct(value.shape, value.dtype),
        input_output_aliases={0: 0},
        name="tie",
    )(value, *before)


class Program:
    def __init__(self, plan):
        self.plan = plan
        self.plane = jnp.asarray(plan.plane_table())
        self.depth = jnp.asarray(plan.depth_forward())
        self.inverse = jnp.asarray(plan.depth_inverse())
        slab, chan = lax.axis_index("slab"), lax.axis_index("chan")
        self.slab, self.chan = slab, chan
        turns = jnp.asarray(plan.turns())
        self.turn = lax.dynamic_index_in_dim(
            lax.dynamic_index_in_dim(turns, slab, 0, False), chan, 0, False
        )
        self.flag = (chan % 2).astype(jnp.int32).reshape(1)
        orders = jnp.asarray(plan.orders())
        upper = (chan >= plan.half).astype(jnp.int32)
        self.order = lax.dynamic_index_in_dim(orders, upper, 0, False)
        self.disorder = self.order.T
        chosen, back = plan.selections()
        self.chosen, self.back = jnp.asarray(chosen), jnp.asarray(back)

    def half_shape(self):
        plan = self.plan
        return (plan.half, 2, plan.rt, plan.lp)

    def field_spec(self, chunk):
        plan = self.plan
        return pl.BlockSpec((plan.xb, plan.cc, plan.ny, plan.nz), lambda i: (i, chunk, 0, 0))

    def table(self):
        plan = self.plan
        return leading((1, 3 * plan.blk, 2 * plan.lp))

    def lines(self):
        plan = self.plan
        return pltpu.VMEM((plan.cc, plan.rc, plan.blk), f32)

    def spectra(self):
        plan = self.plan
        rows = pltpu.VMEM((plan.cc * plan.rc, 2 * plan.lp), bf16)
        return [pltpu.VMEM((plan.cc, plan.rc, 2 * plan.lp), f32), rows, rows]

    def analyse(self, chunk, before, values):
        plan = self.plan
        half = self.half_shape()
        return call(
            partial(analyse_kernel, plan), "analyse", plan.nx // plan.xb,
            [scalar(), self.field_spec(chunk), self.table(), whole(self.depth), whole(self.turn)],
            [whole_shape(half)] * 2, [shaped(*half)] * 2,
            [self.lines(), self.spectra()[0]], 14, before,
        )(self.flag, values, self.plane, self.depth, self.turn)

    def middle(self, chunk, before, filled, own, other, linear, cotangent):
        plan = self.plan
        half = self.half_shape()
        field, spec = shaped(plan.nx, plan.c, plan.ny, plan.nz), self.field_spec(chunk)
        return call(
            partial(middle_kernel, plan), "middle", plan.nx // plan.xb,
            [scalar(), whole_shape(half), whole_shape(half), spec, spec, self.table(),
             whole(self.depth), whole(self.inverse), whole(self.turn)],
            [spec, spec, whole_shape(half), whole_shape(half)],
            [field, field, shaped(*half), shaped(*half)],
            [self.lines(), self.lines(), *self.spectra()], 24,
            (*filled, *before), {n: n for n in range(len(filled))},
        )(self.flag, own, other, linear, cotangent, self.plane, self.depth, self.inverse, self.turn)

    def synthesise(self, chunk, before, filled, own, other, linear):
        plan = self.plan
        half = self.half_shape()
        spec = self.field_spec(chunk)
        return call(
            partial(synthesise_kernel, plan), "synthesise", plan.nx // plan.xb,
            [scalar(), whole_shape(half), whole_shape(half), spec, self.table(),
             whole(self.inverse), whole(self.turn)],
            [spec], [shaped(plan.nx, plan.c, plan.ny, plan.nz)],
            [self.lines(), *self.spectra()], 10,
            (*filled, *before), {n: n for n in range(len(filled))},
        )(self.flag, own, other, linear, self.plane, self.inverse, self.turn)

    def linear(self, before, values, matrix, bias):
        plan = self.plan
        wide = jnp.kron(matrix, jnp.eye(8, dtype=f32))
        column = jnp.repeat(bias, 8)[:, None]
        spec = leading((plan.lb, plan.c, plan.ny, plan.nz))
        return call(
            partial(linear_kernel, plan), "linear", plan.nx // plan.lb,
            [spec, whole(wide), whole(column)],
            spec, shaped(plan.nx, plan.c, plan.ny, plan.nz), [],
            12, before,
        )(values, wide, column)

    def mix_specs(self):
        plan = self.plan
        modes = (plan.rt, plan.ll)
        ins = [
            *[whole_shape(modes)] * (2 * plan.chunks), whole(self.order), whole(self.disorder),
            leading((1,) + self.chosen.shape[1:]), leading((1,) + self.back.shape[1:]),
            leading((1, 2, plan.c, plan.wk, plan.c * plan.mx)),
        ]
        scratch = [
            pltpu.VMEM((plan.c * plan.wk, 2 * plan.ll), f32),
            pltpu.VMEM((plan.c * plan.wk, 256), f32),
            pltpu.VMEM((plan.c * plan.wk, 2 * plan.ll), f32),
        ]
        count = 2 * plan.chunks
        return ins, [whole_shape(modes)] * count, [shaped(*modes)] * count, scratch

    def mix(self, before, owns, mirrors, weights):
        plan = self.plan
        ins, outs, shapes, scratch = self.mix_specs()
        rows = plan.c * plan.wk
        modes, *made = call(
            partial(mix_kernel, plan), "mix", plan.wb, ins, [leading((1, rows, 256)), *outs],
            [shaped(plan.wb, rows, 256), *shapes], scratch, 13, before,
        )(*owns, *mirrors, self.order, self.disorder, self.chosen, self.back, weights)
        return modes, made[: plan.chunks], made[plan.chunks :]

    def mix_back(self, before, owns, mirrors, weights, modes):
        plan = self.plan
        ins, outs, shapes, scratch = self.mix_specs()
        kept = leading((1, plan.c * plan.wk, 256))
        gradient, *made = call(
            partial(mix_back_kernel, plan), "mix_back", plan.wb, ins + [kept], [ins[-1], *outs],
            [shaped(*weights.shape), *shapes], scratch, 14, before,
        )(*owns, *mirrors, self.order, self.disorder, self.chosen, self.back, weights, modes)
        return gradient, made[: plan.chunks], made[plan.chunks :]

    def across(self, value, axis, bit):
        size = lax.axis_size(axis)
        return lax.ppermute(value, axis, [(i, i ^ bit) for i in range(size)])

    def mirrored(self, value):
        total = self.plan.s * self.plan.ch
        return lax.ppermute(value, ("slab", "chan"), [(i, total - 1 - i) for i in range(total)])

    def sums_over_chan(self, keep, send):
        plan = self.plan
        arrived = self.across(send, "chan", 1)
        bit = 2
        while bit < plan.ch:
            mine = (self.chan // bit) % 2
            total = keep + arrived
            pairs = total.reshape((total.shape[0] // 2, 2) + total.shape[1:])
            send = lax.dynamic_index_in_dim(pairs, 1 - mine, 1, False)
            keep = lax.dynamic_index_in_dim(pairs, mine, 1, False)
            arrived = self.across(send, "chan", bit)
            bit *= 2
        return keep, send, arrived

    def sums_over_slab(self, total):
        plan = self.plan
        blank = jnp.zeros((plan.rt, plan.ll - 2 * plan.span), f32)
        pieces = []
        for g in range(plan.s):
            window = slice(g * plan.span, (g + 1) * plan.span)
            pieces.append(jnp.concatenate([total[0, :, window], total[1, :, window], blank], axis=1))
        pieces = jnp.stack(pieces)
        mine = lax.dynamic_index_in_dim(pieces, self.slab, 0, False)
        arrived = [
            self.across(lax.dynamic_index_in_dim(pieces, self.slab ^ j, 0, False), "slab", j)
            for j in range(1, plan.s)
        ]
        for piece in arrived:
            mine = mine + piece
        return mine

    def gather_chunks(self, run, linear):
        arrived, before, owns, mirrors, mixed = [], [], [], [], None
        sums = []
        for n in range(self.plan.chunks):
            keep, send = run(n, before)
            sums.append(self.sums_over_chan(keep, tie(send, *arrived)))
            arrived, before = [sums[-1][2]], [sums[-1][1]]
        for n, (keep, _, arrived) in enumerate(sums):
            if n == self.plan.chunks - 1:
                mixed = linear(before)
                arrived = tie(arrived, mixed, *owns)
            else:
                arrived = tie(arrived, sums[n + 1][1])
            owns.append(self.sums_over_slab((keep + arrived)[0]))
            mirrors.append(self.mirrored(owns[-1]))
        return owns, mirrors, mixed

    def spread_over_slab(self, owns, mirrors):
        plan = self.plan
        blank = jnp.zeros((plan.rt, plan.lp - plan.lw), f32)
        totals = []
        sums = [own + self.mirrored(mirror) for own, mirror in zip(owns, mirrors)]
        for mine in sums:
            mine = tie(mine, *totals[-1:])
            arrived = [self.across(mine, "slab", j) for j in range(1, plan.s)]
            held = jnp.stack([mine] + arrived)
            pieces = [lax.dynamic_index_in_dim(held, self.slab ^ g, 0, False) for g in range(plan.s)]
            totals.append(jnp.stack([
                jnp.concatenate([p[:, r * plan.span : (r + 1) * plan.span] for p in pieces] + [blank], axis=1)
                for r in range(2)
            ])[None])
        return totals

    def spread_chunks(self, owns, mirrors):
        plan = self.plan
        totals = self.spread_over_slab(owns, mirrors)
        sent, arrived = [], []
        for total in totals:
            sent.append(tie(total, *arrived[-1:]))
            arrived.append(self.across(sent[-1], "chan", plan.ch // 2) if plan.ch > 2 else sent[-1])

        def take(n, before):
            total, other = sent[n], tie(arrived[n], *before)
            bit = plan.ch // 2
            while bit > 1:
                upper = (self.chan // bit) % 2 == 1
                total = jnp.stack([jnp.where(upper, other, total), jnp.where(upper, total, other)], axis=1)
                total = total.reshape((-1,) + total.shape[2:])
                bit //= 2
                other = self.across(total, "chan", bit)
            return total, other

        return take


def local(inputs, cotangent, spectral, local_weight, bias_vector):
    nx, ny, channels, nz = inputs.shape
    wb, wk = spectral.shape[0], spectral.shape[1]
    plan = Plan(nx, ny, nz, channels, wb, wk, spectral.shape[4] // channels, lax.axis_size("slab"), lax.axis_size("chan"))
    program = Program(plan)
    values = jnp.transpose(inputs, (0, 2, 1, 3))
    slopes = jnp.transpose(cotangent, (0, 2, 1, 3))
    weights = jnp.transpose(spectral, (0, 2, 3, 1, 4))

    owns, mirrors, linear = program.gather_chunks(
        lambda n, before: program.analyse(n, before, values),
        lambda before: program.linear(before, values, local_weight.T, bias_vector),
    )
    modes, owns, mirrors = program.mix([linear], owns, mirrors, weights)

    take = program.spread_chunks(owns, mirrors)
    filled = []

    def middle(n, before):
        own, other = take(n, filled[2:])
        output, gradient, keep, send = program.middle(n, before, filled[:2], own, other, linear, slopes)
        filled[:] = [output, gradient, keep]
        return keep, send

    owns, mirrors, mixed = program.gather_chunks(
        middle, lambda before: program.linear(before, filled[1], local_weight, jnp.zeros_like(bias_vector))
    )
    output = filled[0]
    grad_spectral, owns, mirrors = program.mix_back([mixed], owns, mirrors, weights, modes)

    take = program.spread_chunks(owns, mirrors)
    made = []
    for n in range(plan.chunks):
        own, other = take(n, made)
        made = program.synthesise(n, [], made, own, other, mixed)
    (grad_inputs,) = made
    return (
        jnp.transpose(output, (0, 2, 1, 3)),
        jnp.transpose(grad_inputs, (0, 2, 1, 3)),
        jnp.transpose(grad_spectral, (0, 3, 1, 2, 4)),
    )


def solution(mesh):
    in_specs = (
        P(("groups", "slab"), "chan", None, None),
        P(("groups", "slab"), "chan", None, None),
        P("slab", "chan", None, None, None),
        P(),
        P(),
    )
    out_specs = (
        P(("groups", "slab"), "chan", None, None),
        P(("groups", "slab"), "chan", None, None),
        P(("groups", "slab"), "chan", None, None, None),
    )
    return jax.shard_map(local, mesh=mesh, in_specs=in_specs, out_specs=out_specs, check_vma=False)
```

```python
from functools import partial
import math

import jax
import jax.numpy as jnp
import ml_dtypes
import numpy as np
from jax import lax
from jax.experimental import pallas as pl
from jax.experimental.pallas import tpu as pltpu
from jax.sharding import PartitionSpec as P

f32 = jnp.float32
bf16 = jnp.bfloat16
root_half = 0.7071067811865476
inv_root_two_pi = 0.3989422804014327
VMEM_LIMIT = 60 * 1024 * 1024
NT = (((1,), (1,)), ((), ()))
TN = (((0,), (0,)), ((), ()))


def round_up(value, unit):
    return -(-value // unit) * unit


class Plan:
    def __init__(self, nx, ny, nz, channels, wb, wk, mx, slab_count, chan_count):
        self.nx, self.ny, self.nz, self.c = nx, ny, nz, channels
        self.wb, self.wk, self.mx = wb, wk, mx
        self.s, self.ch = slab_count, chan_count
        self.half = chan_count // 2
        self.na = mx // 2 + 1
        self.span = (wb + 1) * self.na
        self.lw = slab_count * self.span
        self.lp = round_up(self.lw, 128)
        self.ll = round_up(2 * self.span, 128)
        self.mk = self.half * wk
        self.rc = round_up(2 * self.mk + 2 * self.half, 8)
        self.chunks = math.gcd(2, channels)
        self.cc = channels // self.chunks
        self.rt = round_up(self.cc * (wk + 1), 8)
        self.xb = math.gcd(8, nx)
        self.blk = self.xb * ny
        self.rows = self.cc * wk
        self.bb = math.gcd(2, wb)
        self.lb = math.gcd(4, nx)
        self.batch = max(d for d in range(1, 6) if self.cc % d == 0)
        self.full_x, self.full_y = nx * slab_count, ny * chan_count

    def starts(self):
        kept = self.wb * self.s
        return [g * self.wb - (kept if 2 * g >= self.s else 0) for g in range(self.s)]

    def columns(self):
        b = np.concatenate([np.repeat(np.arange(st, st + self.wb + 1), self.na) for st in self.starts()])
        a = np.tile(np.arange(self.na), self.s * (self.wb + 1))
        return a, b

    def plane_table(self):
        a, b = self.columns()
        x = np.repeat(np.arange(self.nx), self.ny)[:, None]
        y = np.tile(np.arange(self.ny), self.nx)[:, None]
        total = self.full_x * self.full_y
        phase = (a * x * self.full_y + b * y * self.full_x) % total * (2.0 * np.pi / total)
        table = np.zeros((self.nx * self.ny, 2 * self.lp))
        scale = 1.0 / math.sqrt(total)
        table[:, : self.lw] = np.cos(phase) * scale
        table[:, self.lp : self.lp + self.lw] = -np.sin(phase) * scale
        high, low = (t.reshape(self.nx // self.xb, 1, self.blk, 2 * self.lp) for t in halves(table))
        return np.concatenate([high, high, low], 1).reshape(-1, 3 * self.blk, 2 * self.lp)

    def turns(self):
        a, b = self.columns()
        x = (np.arange(self.s) * self.nx)[:, None, None]
        y = (np.arange(self.ch) * self.ny)[None, :, None]
        total = self.full_x * self.full_y
        phase = (a * x * self.full_y + b * y * self.full_x) % total * (2.0 * np.pi / total)
        table = np.zeros((self.s, self.ch, 2, self.lp), np.float32)
        table[:, :, 0, : self.lw] = np.cos(phase)
        table[:, :, 1, : self.lw] = np.sin(phase)
        return table

    def depth_rows(self):
        main = np.arange(self.mk)
        edge = (np.arange(self.half) + 1) * self.wk
        z = np.arange(self.nz)
        scale = 1.0 / math.sqrt(self.nz)
        angle = lambda k: (k[:, None] * z) % self.nz * (2.0 * np.pi / self.nz)
        rows = [np.cos(angle(main)), np.sin(angle(main)), np.cos(angle(edge)), np.sin(angle(edge))]
        table = np.zeros((self.rc, self.nz))
        table[: 2 * self.mk + 2 * self.half] = np.concatenate(rows) * scale
        return halves(table)

    def depth_forward(self):
        high, low = self.depth_rows()
        return np.concatenate(
            [np.concatenate([high, high], 1), np.concatenate([low, np.zeros_like(low)], 1)], 0
        )

    def depth_inverse(self):
        high, low = self.depth_rows()
        table = np.zeros((round_up(3 * self.rc, 16), self.nz), ml_dtypes.bfloat16)
        table[: 3 * self.rc] = np.concatenate([high, high, low], 0)
        return table

    def selections(self):
        quarters = 128 // self.mx
        own = np.zeros((self.wb, 2, self.ll, 2, quarters, self.mx), np.float32)
        for b in range(self.wb):
            for r in range(2):
                for a in range(self.mx):
                    if a < self.mx // 2:
                        own[b, 0, r * self.span + b * self.na + a, r, :, a] = 1.0
                    else:
                        spot = r * self.span + (self.wb - b) * self.na + self.mx - a
                        own[b, 1, spot, r, :, a] = 1.0 - 2.0 * r
        own = own.reshape(self.wb, 2 * self.ll, 256)
        back = np.swapaxes(own, 1, 2)
        return own.astype(ml_dtypes.bfloat16), np.ascontiguousarray(back).astype(ml_dtypes.bfloat16)

    def orders(self):
        table = np.zeros((2, self.rows, self.rt), np.float32)
        for c in range(self.cc):
            for k in range(self.wk):
                table[0, c * self.wk + k, c * self.wk + k] = 1.0
                mirrored = self.wk - k
                spot = self.rows + c if mirrored == self.wk else c * self.wk + mirrored
                table[1, c * self.wk + k, spot] = 1.0
        return table.astype(ml_dtypes.bfloat16)


def halves(table):
    high = table.astype(np.float32).astype(ml_dtypes.bfloat16)
    low = (table - high.astype(np.float64)).astype(np.float32).astype(ml_dtypes.bfloat16)
    return high, low


def dot(left, right, numbers=(((1,), (0,)), ((), ()))):
    return lax.dot_general(left, right, numbers, preferred_element_type=f32)


def split(value):
    high = value.astype(bf16)
    return high, (value - high.astype(f32)).astype(bf16)


def moved(value, chosen, left=False):
    first, second = split(value)
    if left:
        return dot(chosen, first) + dot(chosen, second)
    rows = value.shape[0]
    if rows % 16:
        return dot(first, chosen) + dot(second, chosen)
    both = dot(jnp.concatenate([first, second], axis=0), chosen)
    return both[:rows] + both[rows:]


def depth_analysis(plan, table_ref, values):
    rows = []
    for value in values:
        high, low = split(value)
        rows.append(jnp.concatenate([high, low], axis=1))
    both = dot(table_ref[...], jnp.concatenate(rows, axis=0), NT)
    lines = both[: plan.rc] + both[plan.rc :]
    return [lines[:, j * plan.blk : (j + 1) * plan.blk] for j in range(len(values))]


def depth_synthesis(plan, table_ref, rows):
    high = rows.astype(bf16).astype(f32)
    parts = [high, rows - high, high]
    extra = table_ref.shape[0] - 3 * plan.rc
    if extra:
        parts.append(jnp.zeros((extra, rows.shape[1]), f32))
    return dot(jnp.concatenate(parts, axis=0).astype(bf16), table_ref[...], TN)


def plane_analysis(plan, step, lines_ref, plane_ref, total_ref):
    high, low = split(lines_ref[...].reshape(plan.cc * plan.rc, plan.blk))
    rows = jnp.concatenate([high, low, high], axis=1)
    for start in range(0, 2 * plan.lp, 256):
        size = min(256, 2 * plan.lp - start)
        columns = pl.ds(start, size)
        part = dot(rows, plane_ref[0, :, columns]).reshape(plan.cc, plan.rc, size)

        @pl.when(step == 0)
        def _():
            total_ref[:, :, columns] = part

        @pl.when(step > 0)
        def _():
            total_ref[:, :, columns] += part


def plane_synthesis(plan, high_rows, low_rows, plane_ref, lines_ref):
    high_table, low_table = plane_ref[0, : plan.blk], plane_ref[0, 2 * plan.blk :]
    lines = (
        dot(high_rows[...], high_table, NT)
        + dot(low_rows[...], high_table, NT)
        + dot(high_rows[...], low_table, NT)
    )
    lines_ref[...] = lines.reshape(plan.cc, plan.rc, plan.blk)


def emit_modes(plan, flag_ref, turn_ref, total_ref, keep_ref, send_ref):
    lp, wk, mk, half = plan.lp, plan.wk, plan.mk, plan.half
    odd = flag_ref[0] == 1
    cosine, sine = turn_ref[0:1, :], turn_ref[1:2, :]
    for c in range(plan.cc):
        real, imag = total_ref[c, :, :lp], total_ref[c, :, lp:]
        real, imag = real * cosine + imag * sine, imag * cosine - real * sine
        for first, size, base, shift in ((0, wk, c * wk, mk), (2 * mk, 1, plan.rows + c, half)):
            made = []
            for g in range(plan.ch):
                h = g if g < half else plan.ch - 1 - g
                even_rows = slice(first + h * size, first + (h + 1) * size)
                odd_rows = slice(first + shift + h * size, first + shift + (h + 1) * size)
                if g < half:
                    made.append((real[even_rows] + imag[odd_rows], imag[even_rows] - real[odd_rows]))
                else:
                    made.append((real[even_rows] - imag[odd_rows], imag[even_rows] + real[odd_rows]))
            for pair in range(half):
                for r in range(2):
                    low, high = made[2 * pair][r], made[2 * pair + 1][r]
                    keep_ref[pair, r, base : base + size, :] = jnp.where(odd, high, low)
                    send_ref[pair, r, base : base + size, :] = jnp.where(odd, low, high)
    used = plan.cc * (wk + 1)
    if used < plan.rt:
        blank = jnp.zeros((plan.half, 2, plan.rt - used, lp), f32)
        keep_ref[:, :, used:, :] = blank
        send_ref[:, :, used:, :] = blank


def take_modes(plan, flag_ref, turn_ref, own_ref, other_ref, total_ref, high_rows, low_rows):
    lp, wk, mk, half = plan.lp, plan.wk, plan.mk, plan.half
    odd = flag_ref[0] == 1
    cosine, sine = turn_ref[0:1, :], turn_ref[1:2, :]

    def group(g, r, rows):
        own, other = own_ref[g // 2, r, rows, :], other_ref[g // 2, r, rows, :]
        return jnp.where(odd, own, other) if g % 2 else jnp.where(odd, other, own)

    for c in range(plan.cc):
        for first, size, base, shift in ((0, wk, c * wk, mk), (2 * mk, 1, plan.rows + c, half)):
            rows = slice(base, base + size)
            for h in range(half):
                plus = [group(h, r, rows) for r in range(2)]
                minus = [group(plan.ch - 1 - h, r, rows) for r in range(2)]
                real, imag = plus[0] + minus[0], plus[1] + minus[1]
                here = slice(first + h * size, first + (h + 1) * size)
                total_ref[c, here, :lp] = real * cosine - imag * sine
                total_ref[c, here, lp:] = imag * cosine + real * sine
                real, imag = plus[0] - minus[0], plus[1] - minus[1]
                here = slice(first + shift + h * size, first + shift + (h + 1) * size)
                total_ref[c, here, :lp] = -(imag * cosine + real * sine)
                total_ref[c, here, lp:] = real * cosine - imag * sine
        used = 2 * mk + 2 * half
        if used < plan.rc:
            total_ref[c, used:, :] = jnp.zeros((plan.rc - used, 2 * lp), f32)
    high, low = split(total_ref[...].reshape(plan.cc * plan.rc, 2 * lp))
    high_rows[...] = high
    low_rows[...] = low


def analyse_kernel(plan, flag_ref, values_ref, plane_ref, depth_ref, turn_ref, keep_ref, send_ref, lines_ref, total_ref):
    step = pl.program_id(0)

    @pl.loop(0, plan.cc, step=plan.batch)
    def _(c):
        values = [values_ref[:, c + j].reshape(plan.blk, plan.nz) for j in range(plan.batch)]
        for j, lines in enumerate(depth_analysis(plan, depth_ref, values)):
            lines_ref[c + j] = lines

    plane_analysis(plan, step, lines_ref, plane_ref, total_ref)

    @pl.when(step == pl.num_programs(0) - 1)
    def _():
        emit_modes(plan, flag_ref, turn_ref, total_ref, keep_ref, send_ref)


def fields(plan, inverse_ref, lines_ref, first):
    lines = jnp.concatenate([lines_ref[first + j] for j in range(plan.batch)], axis=1)
    values = depth_synthesis(plan, inverse_ref, lines)
    return [values[j * plan.blk : (j + 1) * plan.blk] for j in range(plan.batch)]


def middle_kernel(
    plan, flag_ref, own_ref, other_ref, linear_ref, cotangent_ref, plane_ref, depth_ref, inverse_ref, turn_ref,
    output_ref, gradient_ref, keep_ref, send_ref, lines_ref, back_ref, total_ref, high_rows, low_rows,
):
    step = pl.program_id(0)

    @pl.when(step == 0)
    def _():
        take_modes(plan, flag_ref, turn_ref, own_ref, other_ref, total_ref, high_rows, low_rows)

    plane_synthesis(plan, high_rows, low_rows, plane_ref, lines_ref)
    shape = (plan.xb, plan.ny, plan.nz)

    @pl.loop(0, plan.cc, step=plan.batch)
    def _(first):
        gradients = []
        for j, field in enumerate(fields(plan, inverse_ref, lines_ref, first)):
            value = field + linear_ref[:, first + j].reshape(plan.blk, plan.nz)
            gate = 0.5 * (1.0 + lax.erf(value * root_half))
            slope = gate + value * jnp.exp(-0.5 * value * value) * inv_root_two_pi
            output_ref[:, first + j] = (value * gate).reshape(shape)
            gradients.append(cotangent_ref[:, first + j].reshape(plan.blk, plan.nz) * slope)
            gradient_ref[:, first + j] = gradients[-1].reshape(shape)
        for j, lines in enumerate(depth_analysis(plan, depth_ref, gradients)):
            back_ref[first + j] = lines

    plane_analysis(plan, step, back_ref, plane_ref, total_ref)

    @pl.when(step == pl.num_programs(0) - 1)
    def _():
        emit_modes(plan, flag_ref, turn_ref, total_ref, keep_ref, send_ref)


def synthesise_kernel(
    plan, flag_ref, own_ref, other_ref, linear_ref, plane_ref, inverse_ref, turn_ref,
    output_ref, lines_ref, total_ref, high_rows, low_rows,
):
    @pl.when(pl.program_id(0) == 0)
    def _():
        take_modes(plan, flag_ref, turn_ref, own_ref, other_ref, total_ref, high_rows, low_rows)

    plane_synthesis(plan, high_rows, low_rows, plane_ref, lines_ref)

    @pl.loop(0, plan.cc, step=plan.batch)
    def _(first):
        for j, field in enumerate(fields(plan, inverse_ref, lines_ref, first)):
            value = field + linear_ref[:, first + j].reshape(plan.blk, plan.nz)
            output_ref[:, first + j] = value.reshape(plan.xb, plan.ny, plan.nz)


def linear_kernel(plan, values_ref, weight_ref, bias_ref, output_ref):
    tiles = [(x, slice(t * 8, (t + 1) * 8)) for x in range(plan.lb) for t in range(plan.ny // 8)]
    values = [values_ref[x, :, t, :].reshape(plan.c * 8, plan.nz) for x, t in tiles]
    high, low = split(jnp.concatenate(values, axis=1))
    size = 8 * plan.c
    row, column = (lax.broadcasted_iota(jnp.int32, (size, plan.c), n) for n in (0, 1))
    repeat = (row // 8 == column).astype(f32)
    exact = partial(lax.dot_general, precision=lax.Precision.HIGHEST, preferred_element_type=f32)
    spread = exact(exact(repeat, weight_ref[...], (((1,), (0,)), ((), ()))), repeat, NT)
    row, column = (lax.broadcasted_iota(jnp.int32, (size, size), n) for n in (0, 1))
    high_matrix, low_matrix = split(jnp.where(row % 8 == column % 8, spread, 0.0))
    bias = exact(repeat, bias_ref[...], (((1,), (1,)), ((), ())))
    matrix = jnp.concatenate([high_matrix, high_matrix, low_matrix], axis=1)
    mixed = dot(matrix, jnp.concatenate([high, low, high], axis=0)) + bias
    for n, (x, t) in enumerate(tiles):
        output_ref[x, :, t, :] = mixed[:, n * plan.nz : (n + 1) * plan.nz].reshape(plan.c, 8, plan.nz)


def pick(plan, own_refs, mirror_refs, order_ref, chosen_ref, ordered_ref):
    @pl.when(pl.program_id(0) == 0)
    def _():
        for n in range(plan.chunks):
            rows = slice(n * plan.rows, (n + 1) * plan.rows)
            ordered_ref[rows, : plan.ll] = moved(own_refs[n][...], order_ref[...], left=True)
            ordered_ref[rows, plan.ll :] = moved(mirror_refs[n][...], order_ref[...], left=True)

    return [moved(ordered_ref[...], chosen_ref[n]) for n in range(plan.bb)]


def give(plan, made_ref, order_ref, back_ref, own_refs, mirror_refs, sums_ref):
    part = moved(made_ref[0], back_ref[0])
    for n in range(1, plan.bb):
        part = part + moved(made_ref[n], back_ref[n])
    step = pl.program_id(0)

    @pl.when(step == 0)
    def _():
        sums_ref[...] = part

    @pl.when(step > 0)
    def _():
        sums_ref[...] += part

    @pl.when(step == pl.num_programs(0) - 1)
    def _():
        for n in range(plan.chunks):
            rows = slice(n * plan.rows, (n + 1) * plan.rows)
            own_refs[n][...] = moved(sums_ref[rows, : plan.ll], order_ref[...], left=True)
            mirror_refs[n][...] = moved(sums_ref[rows, plan.ll :], order_ref[...], left=True)


def mix_kernel(plan, *refs):
    n = plan.chunks
    owns, mirrors, refs = refs[:n], refs[n : 2 * n], refs[2 * n :]
    order_ref, disorder_ref, chosen_ref, back_ref, weight_ref, modes_ref = refs[:6]
    own_outs, mirror_outs, (ordered_ref, made_ref, sums_ref) = refs[6 : 6 + n], refs[6 + n : 6 + 2 * n], refs[6 + 2 * n :]
    wk, quarters = plan.wk, 128 // plan.mx
    picked = pick(plan, owns, mirrors, order_ref, chosen_ref, ordered_ref)
    place = lax.broadcasted_iota(jnp.int32, (wk, 128), 1) // plan.mx
    for n, modes in enumerate(picked):
        modes_ref[n] = modes
        for t in range(plan.c // quarters):
            columns = slice(t * 128, (t + 1) * 128)
            real = imag = 0.0
            for i in range(plan.c):
                x_real, x_imag = modes[i * wk : (i + 1) * wk, :128], modes[i * wk : (i + 1) * wk, 128:]
                w_real, w_imag = weight_ref[n, 0, i, :, columns], weight_ref[n, 1, i, :, columns]
                real = real + (w_real * x_real - w_imag * x_imag)
                imag = imag + (w_real * x_imag + w_imag * x_real)
            for q in range(quarters):
                o = t * quarters + q
                made_ref[n, o * wk : (o + 1) * wk, :128] = jnp.where(place == q, real, 0.0)
                made_ref[n, o * wk : (o + 1) * wk, 128:] = jnp.where(place == q, imag, 0.0)
    give(plan, made_ref, disorder_ref, back_ref, own_outs, mirror_outs, sums_ref)


def mix_back_kernel(plan, *refs):
    n = plan.chunks
    owns, mirrors, refs = refs[:n], refs[n : 2 * n], refs[2 * n :]
    order_ref, disorder_ref, chosen_ref, back_ref, weight_ref, modes_ref, gradient_ref = refs[:7]
    own_outs, mirror_outs, (ordered_ref, made_ref, sums_ref) = refs[7 : 7 + n], refs[7 + n : 7 + 2 * n], refs[7 + 2 * n :]
    wk, quarters = plan.wk, 128 // plan.mx
    picked = pick(plan, owns, mirrors, order_ref, chosen_ref, ordered_ref)
    place = lax.broadcasted_iota(jnp.int32, (wk, 128), 1) // plan.mx
    for n, grads in enumerate(picked):
        lined = []
        for t in range(plan.c // quarters):
            real = imag = 0.0
            for q in range(quarters):
                o = t * quarters + q
                real = jnp.where(place == q, grads[o * wk : (o + 1) * wk, :128], real)
                imag = jnp.where(place == q, grads[o * wk : (o + 1) * wk, 128:], imag)
            lined.append((real, imag))
        for i in range(plan.c):
            rows = slice(i * wk, (i + 1) * wk)
            x_real, x_imag = modes_ref[n, rows, :128], modes_ref[n, rows, 128:]
            back_real = back_imag = 0.0
            for t, (real, imag) in enumerate(lined):
                columns = slice(t * 128, (t + 1) * 128)
                gradient_ref[n, 0, i, :, columns] = real * x_real + imag * x_imag
                gradient_ref[n, 1, i, :, columns] = imag * x_real - real * x_imag
                w_real, w_imag = weight_ref[n, 0, i, :, columns], weight_ref[n, 1, i, :, columns]
                back_real = back_real + (w_real * real + w_imag * imag)
                back_imag = back_imag + (w_real * imag - w_imag * real)
            made_ref[n, rows, :128] = back_real
            made_ref[n, rows, 128:] = back_imag
    give(plan, made_ref, disorder_ref, back_ref, own_outs, mirror_outs, sums_ref)


def halve_kernel(flag_ref, keep_ref, arrived_ref, kept_ref, send_ref):
    odd = flag_ref[0] == 1
    for pair in range(kept_ref.shape[0]):
        low = keep_ref[2 * pair] + arrived_ref[2 * pair]
        high = keep_ref[2 * pair + 1] + arrived_ref[2 * pair + 1]
        kept_ref[pair] = jnp.where(odd, high, low)
        send_ref[pair] = jnp.where(odd, low, high)


def cut_kernel(plan, slab_ref, keep_ref, arrived_ref, *refs):
    out_refs, held_ref = refs[:-1], refs[-1]
    lane = lax.broadcasted_iota(jnp.int32, (plan.rt, plan.ll), 1)
    real = keep_ref[0, 0] + arrived_ref[0, 0]
    imag = keep_ref[0, 1] + arrived_ref[0, 1]
    for g in range(plan.s):
        first = pltpu.roll(real, (plan.lp - g * plan.span) % plan.lp, 1)[:, : plan.ll]
        second = pltpu.roll(imag, (plan.lp - g * plan.span + plan.span) % plan.lp, 1)[:, : plan.ll]
        held_ref[g] = jnp.where(lane < plan.span, first, jnp.where(lane < 2 * plan.span, second, 0.0))
    for j, out_ref in enumerate(out_refs):
        out_ref[...] = held_ref[slab_ref[0] ^ j]


def join_kernel(plan, slab_ref, *refs):
    piece_refs, total_ref, held_ref = refs[:-2], refs[-2], refs[-1]
    for j, piece_ref in enumerate(piece_refs):
        held_ref[j] = piece_ref[...]
    lane = lax.broadcasted_iota(jnp.int32, (plan.rt, plan.lp), 1)
    real = imag = jnp.zeros((plan.rt, plan.lp), f32)
    blank = jnp.zeros((plan.rt, plan.lp - plan.ll), f32)
    for g in range(plan.s):
        piece = jnp.concatenate([held_ref[slab_ref[0] ^ g], blank], axis=1)
        here = (lane >= g * plan.span) & (lane < (g + 1) * plan.span)
        real = jnp.where(here, pltpu.roll(piece, g * plan.span, 1), real)
        imag = jnp.where(here, pltpu.roll(piece, (g * plan.span - plan.span) % plan.lp, 1), imag)
    total_ref[0, 0] = real
    total_ref[0, 1] = imag


def whole(array):
    zeros = (0,) * array.ndim
    return pl.BlockSpec(array.shape, lambda i: zeros, pipeline_mode=pl.Buffered(1))


def whole_shape(shape):
    zeros = (0,) * len(shape)
    return pl.BlockSpec(shape, lambda i: zeros, pipeline_mode=pl.Buffered(1))


def leading(shape):
    rest = (0,) * (len(shape) - 1)
    return pl.BlockSpec(shape, lambda i: (i,) + rest)


def shaped(*shape):
    return jax.ShapeDtypeStruct(shape, f32)


def anywhere():
    return pl.BlockSpec(memory_space=pl.ANY)


def scalar():
    return pl.BlockSpec(memory_space=pltpu.SMEM)


def call(kernel, name, grid, in_specs, out_specs, out_shape, scratch, cost, before=(), aliases=None):
    skipped = len(before)
    run = pl.pallas_call(
        lambda *refs: kernel(*refs[skipped:]),
        grid=(grid,),
        in_specs=[anywhere()] * skipped + list(in_specs),
        out_specs=out_specs,
        out_shape=out_shape,
        scratch_shapes=scratch,
        name=name,
        input_output_aliases=aliases or {},
        compiler_params=pltpu.CompilerParams(vmem_limit_bytes=VMEM_LIMIT, dimension_semantics=("arbitrary",)),
        cost_estimate=pl.CostEstimate(flops=int(cost * 1.15e9), bytes_accessed=int(cost * 3.6e6), transcendentals=0),
    )
    return partial(run, *before)


def tie(value, *before):
    if not before:
        return value
    return pl.pallas_call(
        lambda *refs: None,
        in_specs=[anywhere()] * (1 + len(before)),
        out_specs=anywhere(),
        out_shape=jax.ShapeDtypeStruct(value.shape, value.dtype),
        input_output_aliases={0: 0},
        name="tie",
    )(value, *before)


class Program:
    def __init__(self, plan):
        self.plan = plan
        self.plane = jnp.asarray(plan.plane_table())
        self.depth = jnp.asarray(plan.depth_forward())
        self.inverse = jnp.asarray(plan.depth_inverse())
        slab, chan = lax.axis_index("slab"), lax.axis_index("chan")
        self.slab, self.chan = slab, chan
        turns = jnp.asarray(plan.turns())
        self.turn = lax.dynamic_index_in_dim(
            lax.dynamic_index_in_dim(turns, slab, 0, False), chan, 0, False
        )
        self.slab_index = slab.astype(jnp.int32).reshape(1)
        self.flag = (chan % 2).astype(jnp.int32).reshape(1)
        orders = jnp.asarray(plan.orders())
        upper = (chan >= plan.half).astype(jnp.int32)
        self.order = lax.dynamic_index_in_dim(orders, upper, 0, False)
        self.disorder = self.order.T
        chosen, back = plan.selections()
        self.chosen, self.back = jnp.asarray(chosen), jnp.asarray(back)

    def half_shape(self):
        plan = self.plan
        return (plan.half, 2, plan.rt, plan.lp)

    def field_spec(self, chunk):
        plan = self.plan
        return pl.BlockSpec((plan.xb, plan.cc, plan.ny, plan.nz), lambda i: (i, chunk, 0, 0))

    def table(self):
        plan = self.plan
        return leading((1, 3 * plan.blk, 2 * plan.lp))

    def lines(self):
        plan = self.plan
        return pltpu.VMEM((plan.cc, plan.rc, plan.blk), f32)

    def spectra(self):
        plan = self.plan
        rows = pltpu.VMEM((plan.cc * plan.rc, 2 * plan.lp), bf16)
        return [pltpu.VMEM((plan.cc, plan.rc, 2 * plan.lp), f32), rows, rows]

    def analyse(self, chunk, before, values):
        plan = self.plan
        half = self.half_shape()
        return call(
            partial(analyse_kernel, plan), "analyse", plan.nx // plan.xb,
            [scalar(), self.field_spec(chunk), self.table(), whole(self.depth), whole(self.turn)],
            [whole_shape(half)] * 2, [shaped(*half)] * 2,
            [self.lines(), self.spectra()[0]], 14, before,
        )(self.flag, values, self.plane, self.depth, self.turn)

    def middle(self, chunk, before, filled, own, other, linear, cotangent):
        plan = self.plan
        half = self.half_shape()
        field, spec = shaped(plan.nx, plan.c, plan.ny, plan.nz), self.field_spec(chunk)
        return call(
            partial(middle_kernel, plan), "middle", plan.nx // plan.xb,
            [scalar(), whole_shape(half), whole_shape(half), spec, spec, self.table(),
             whole(self.depth), whole(self.inverse), whole(self.turn)],
            [spec, spec, whole_shape(half), whole_shape(half)],
            [field, field, shaped(*half), shaped(*half)],
            [self.lines(), self.lines(), *self.spectra()], 24,
            (*filled, *before), {n: n for n in range(len(filled))},
        )(self.flag, own, other, linear, cotangent, self.plane, self.depth, self.inverse, self.turn)

    def synthesise(self, chunk, before, filled, own, other, linear):
        plan = self.plan
        half = self.half_shape()
        spec = self.field_spec(chunk)
        return call(
            partial(synthesise_kernel, plan), "synthesise", plan.nx // plan.xb,
            [scalar(), whole_shape(half), whole_shape(half), spec, self.table(),
             whole(self.inverse), whole(self.turn)],
            [spec], [shaped(plan.nx, plan.c, plan.ny, plan.nz)],
            [self.lines(), *self.spectra()], 10,
            (*filled, *before), {n: n for n in range(len(filled))},
        )(self.flag, own, other, linear, self.plane, self.inverse, self.turn)

    def linear(self, before, values, matrix, bias):
        plan = self.plan
        bias = bias[None]
        spec = leading((plan.lb, plan.c, plan.ny, plan.nz))
        return call(
            partial(linear_kernel, plan), "linear", plan.nx // plan.lb,
            [spec, whole(matrix), whole(bias)],
            spec, shaped(plan.nx, plan.c, plan.ny, plan.nz), [],
            12, before,
        )(values, matrix, bias)

    def mix_specs(self):
        plan = self.plan
        modes = (plan.rt, plan.ll)
        ins = [
            *[whole_shape(modes)] * (2 * plan.chunks), whole(self.order), whole(self.disorder),
            leading((plan.bb,) + self.chosen.shape[1:]), leading((plan.bb,) + self.back.shape[1:]),
            leading((plan.bb, 2, plan.c, plan.wk, plan.c * plan.mx)),
        ]
        scratch = [
            pltpu.VMEM((plan.c * plan.wk, 2 * plan.ll), f32),
            pltpu.VMEM((plan.bb, plan.c * plan.wk, 256), f32),
            pltpu.VMEM((plan.c * plan.wk, 2 * plan.ll), f32),
        ]
        count = 2 * plan.chunks
        return ins, [whole_shape(modes)] * count, [shaped(*modes)] * count, scratch

    def mix(self, before, owns, mirrors, weights):
        plan = self.plan
        ins, outs, shapes, scratch = self.mix_specs()
        rows = plan.c * plan.wk
        modes, *made = call(
            partial(mix_kernel, plan), "mix", plan.wb // plan.bb, ins, [leading((plan.bb, rows, 256)), *outs],
            [shaped(plan.wb, rows, 256), *shapes], scratch, 13, before,
        )(*owns, *mirrors, self.order, self.disorder, self.chosen, self.back, weights)
        return modes, made[: plan.chunks], made[plan.chunks :]

    def mix_back(self, before, owns, mirrors, weights, modes):
        plan = self.plan
        ins, outs, shapes, scratch = self.mix_specs()
        kept = leading((plan.bb, plan.c * plan.wk, 256))
        gradient, *made = call(
            partial(mix_back_kernel, plan), "mix_back", plan.wb // plan.bb, ins + [kept], [ins[-1], *outs],
            [shaped(*weights.shape), *shapes], scratch, 14, before,
        )(*owns, *mirrors, self.order, self.disorder, self.chosen, self.back, weights, modes)
        return gradient, made[: plan.chunks], made[plan.chunks :]

    def across(self, value, axis, bit):
        size = lax.axis_size(axis)
        return lax.ppermute(value, axis, [(i, i ^ bit) for i in range(size)])

    def mirrored(self, value):
        total = self.plan.s * self.plan.ch
        return lax.ppermute(value, ("slab", "chan"), [(i, total - 1 - i) for i in range(total)])

    def sums_over_chan(self, keep, send):
        plan = self.plan
        arrived = self.across(send, "chan", 1)
        bit = 2
        while bit < plan.ch:
            mine = ((self.chan // bit) % 2).astype(jnp.int32).reshape(1)
            half = (keep.shape[0] // 2,) + keep.shape[1:]
            keep, send = call(
                halve_kernel, "halve", 1, [scalar(), whole(keep), whole(keep)], [whole_shape(half)] * 2,
                [shaped(*half)] * 2, [], 2,
            )(mine, keep, arrived)
            arrived = self.across(send, "chan", bit)
            bit *= 2
        return keep, send, arrived

    def sums_over_slab(self, keep, arrived):
        plan = self.plan
        size = (plan.rt, plan.ll)
        mine, *pieces = call(
            partial(cut_kernel, plan), "cut", 1, [scalar(), whole(keep), whole(keep)],
            [whole_shape(size)] * plan.s, [shaped(*size)] * plan.s, [pltpu.VMEM((plan.s, *size), f32)], 2,
        )(self.slab_index, keep, arrived)
        for j, piece in enumerate(pieces):
            mine = mine + self.across(piece, "slab", j + 1)
        return mine

    def gather_chunks(self, run, linear):
        arrived, before, owns, mirrors, mixed = [], [], [], [], None
        sums = []
        for n in range(self.plan.chunks):
            keep, send = run(n, before)
            sums.append(self.sums_over_chan(keep, tie(send, *arrived)))
            arrived, before = [sums[-1][2]], [sums[-1][1]]
        for n, (keep, _, arrived) in enumerate(sums):
            if n == self.plan.chunks - 1:
                mixed = linear(before)
                arrived = tie(arrived, mixed, *owns)
            else:
                arrived = tie(arrived, sums[n + 1][1])
            owns.append(self.sums_over_slab(keep, arrived))
            mirrors.append(self.mirrored(owns[-1]))
        return owns, mirrors, mixed

    def spread_over_slab(self, owns, mirrors):
        plan = self.plan
        totals = []
        sums = [own + self.mirrored(mirror) for own, mirror in zip(owns, mirrors)]
        for mine in sums:
            mine = tie(mine, *totals[-1:])
            arrived = [self.across(mine, "slab", j) for j in range(1, plan.s)]
            total = (1, 2, plan.rt, plan.lp)
            totals.append(call(
                partial(join_kernel, plan), "join", 1, [scalar()] + [whole(mine)] * plan.s,
                whole_shape(total), shaped(*total), [pltpu.VMEM((plan.s, *mine.shape), f32)], 2,
            )(self.slab_index, mine, *arrived))
        return totals

    def spread_chunks(self, owns, mirrors):
        plan = self.plan
        totals = self.spread_over_slab(owns, mirrors)
        sent, arrived = [], []
        for total in totals:
            sent.append(tie(total, *arrived[-1:]))
            arrived.append(self.across(sent[-1], "chan", plan.ch // 2) if plan.ch > 2 else sent[-1])

        def take(n, before):
            total, other = sent[n], tie(arrived[n], *(before or sent[1:]))
            bit = plan.ch // 2
            while bit > 1:
                upper = (self.chan // bit) % 2 == 1
                total = jnp.stack([jnp.where(upper, other, total), jnp.where(upper, total, other)], axis=1)
                total = total.reshape((-1,) + total.shape[2:])
                bit //= 2
                other = self.across(total, "chan", bit)
            return total, other

        return take


def local(inputs, cotangent, spectral, local_weight, bias_vector):
    nx, ny, channels, nz = inputs.shape
    wb, wk = spectral.shape[0], spectral.shape[1]
    plan = Plan(nx, ny, nz, channels, wb, wk, spectral.shape[4] // channels, lax.axis_size("slab"), lax.axis_size("chan"))
    program = Program(plan)
    values = jnp.transpose(inputs, (0, 2, 1, 3))
    slopes = jnp.transpose(cotangent, (0, 2, 1, 3))
    weights = jnp.transpose(spectral, (0, 2, 3, 1, 4))

    owns, mirrors, linear = program.gather_chunks(
        lambda n, before: program.analyse(n, before, values),
        lambda before: program.linear(before, values, local_weight.T, bias_vector),
    )
    modes, owns, mirrors = program.mix([linear], owns, mirrors, weights)

    take = program.spread_chunks(owns, mirrors)
    filled = []

    def middle(n, before):
        own, other = take(n, filled[2:])
        output, gradient, keep, send = program.middle(n, before, filled[:2], own, other, linear, slopes)
        filled[:] = [output, gradient, keep]
        return keep, send

    owns, mirrors, mixed = program.gather_chunks(
        middle, lambda before: program.linear(before, filled[1], local_weight, jnp.zeros_like(bias_vector))
    )
    output = filled[0]
    grad_spectral, owns, mirrors = program.mix_back([mixed], owns, mirrors, weights, modes)
    grad_spectral = tie(jnp.transpose(grad_spectral, (0, 3, 2, 1, 4)), owns[0])

    take = program.spread_chunks(owns, mirrors)
    made = []
    for n in range(plan.chunks):
        own, other = take(n, made)
        made = program.synthesise(n, [grad_spectral], made, own, other, mixed)
    (grad_inputs,) = made
    return (
        jnp.transpose(output, (0, 2, 1, 3)),
        jnp.transpose(grad_inputs, (0, 2, 1, 3)),
        jnp.transpose(grad_spectral, (0, 1, 3, 2, 4)),
    )


def solution(mesh):
    in_specs = (
        P(("groups", "slab"), "chan", None, None),
        P(("groups", "slab"), "chan", None, None),
        P("slab", "chan", None, None, None),
        P(),
        P(),
    )
    out_specs = (
        P(("groups", "slab"), "chan", None, None),
        P(("groups", "slab"), "chan", None, None),
        P(("groups", "slab"), "chan", None, None, None),
    )
    return jax.shard_map(local, mesh=mesh, in_specs=in_specs, out_specs=out_specs, check_vma=False)
```

```python
from functools import partial
import math

import jax
import jax.numpy as jnp
import ml_dtypes
import numpy as np
from jax import lax
from jax.experimental import pallas as pl
from jax.experimental.pallas import tpu as pltpu
from jax.sharding import PartitionSpec as P

f32 = jnp.float32
bf16 = jnp.bfloat16
root_half = 0.7071067811865476
inv_root_two_pi = 0.3989422804014327
VMEM_LIMIT = 60 * 1024 * 1024
NT = (((1,), (1,)), ((), ()))
TN = (((0,), (0,)), ((), ()))


def round_up(value, unit):
    return -(-value // unit) * unit


class Plan:
    def __init__(self, nx, ny, nz, channels, wb, wk, mx, slab_count, chan_count):
        self.nx, self.ny, self.nz, self.c = nx, ny, nz, channels
        self.wb, self.wk, self.mx = wb, wk, mx
        self.s, self.ch = slab_count, chan_count
        self.half = chan_count // 2
        self.na = mx // 2 + 1
        self.span = (wb + 1) * self.na
        self.lw = slab_count * self.span
        self.lp = round_up(self.lw, 128)
        self.ll = round_up(2 * self.span, 128)
        self.mk = self.half * wk
        self.rc = round_up(2 * self.mk + 2 * self.half, 8)
        self.chunks = 2
        self.cc = channels
        self.w = (wk // 2, wk - wk // 2)
        self.rts = (round_up(channels * self.w[0], 8), round_up(channels * (self.w[1] + 1), 8))
        self.xb = math.gcd(8, nx)
        self.blk = self.xb * ny
        self.rows = self.cc * wk
        self.bb = math.gcd(2, wb)
        self.lb = math.gcd(4, nx)
        self.batch = max(d for d in range(1, 6) if self.cc % d == 0)
        self.full_x, self.full_y = nx * slab_count, ny * chan_count

    def segments(self, c):
        w0, w1 = self.w
        main = lambda first: lambda h, kind: kind * self.mk + h * self.wk + first
        return (
            (0, c * w0, w0, main(0)),
            (1, c * w1, w1, main(w0)),
            (1, self.c * w1 + c, 1, lambda h, kind: 2 * self.mk + kind * self.half + h),
        )

    def starts(self):
        kept = self.wb * self.s
        return [g * self.wb - (kept if 2 * g >= self.s else 0) for g in range(self.s)]

    def columns(self):
        b = np.concatenate([np.repeat(np.arange(st, st + self.wb + 1), self.na) for st in self.starts()])
        a = np.tile(np.arange(self.na), self.s * (self.wb + 1))
        return a, b

    def plane_table(self):
        a, b = self.columns()
        x = np.repeat(np.arange(self.nx), self.ny)[:, None]
        y = np.tile(np.arange(self.ny), self.nx)[:, None]
        total = self.full_x * self.full_y
        phase = (a * x * self.full_y + b * y * self.full_x) % total * (2.0 * np.pi / total)
        table = np.zeros((self.nx * self.ny, 2 * self.lp))
        scale = 1.0 / math.sqrt(total)
        table[:, : self.lw] = np.cos(phase) * scale
        table[:, self.lp : self.lp + self.lw] = -np.sin(phase) * scale
        high, low = (t.reshape(self.nx // self.xb, 1, self.blk, 2 * self.lp) for t in halves(table))
        return np.concatenate([high, high, low], 1).reshape(-1, 3 * self.blk, 2 * self.lp)

    def turns(self):
        a, b = self.columns()
        x = (np.arange(self.s) * self.nx)[:, None, None]
        y = (np.arange(self.ch) * self.ny)[None, :, None]
        total = self.full_x * self.full_y
        phase = (a * x * self.full_y + b * y * self.full_x) % total * (2.0 * np.pi / total)
        table = np.zeros((self.s, self.ch, 2, self.lp), np.float32)
        table[:, :, 0, : self.lw] = np.cos(phase)
        table[:, :, 1, : self.lw] = np.sin(phase)
        return table

    def depth_rows(self):
        main = np.arange(self.mk)
        edge = (np.arange(self.half) + 1) * self.wk
        z = np.arange(self.nz)
        scale = 1.0 / math.sqrt(self.nz)
        angle = lambda k: (k[:, None] * z) % self.nz * (2.0 * np.pi / self.nz)
        rows = [np.cos(angle(main)), np.sin(angle(main)), np.cos(angle(edge)), np.sin(angle(edge))]
        table = np.zeros((self.rc, self.nz))
        table[: 2 * self.mk + 2 * self.half] = np.concatenate(rows) * scale
        return halves(table)

    def depth_forward(self):
        high, low = self.depth_rows()
        return np.concatenate(
            [np.concatenate([high, high], 1), np.concatenate([low, np.zeros_like(low)], 1)], 0
        )

    def depth_inverse(self):
        high, low = self.depth_rows()
        table = np.zeros((round_up(3 * self.rc, 16), self.nz), ml_dtypes.bfloat16)
        table[: 3 * self.rc] = np.concatenate([high, high, low], 0)
        return table

    def selections(self):
        quarters = 128 // self.mx
        own = np.zeros((self.wb, 2, self.ll, 2, quarters, self.mx), np.float32)
        for b in range(self.wb):
            for r in range(2):
                for a in range(self.mx):
                    if a < self.mx // 2:
                        own[b, 0, r * self.span + b * self.na + a, r, :, a] = 1.0
                    else:
                        spot = r * self.span + (self.wb - b) * self.na + self.mx - a
                        own[b, 1, spot, r, :, a] = 1.0 - 2.0 * r
        own = own.reshape(self.wb, 2 * self.ll, 256)
        back = np.swapaxes(own, 1, 2)
        return own.astype(ml_dtypes.bfloat16), np.ascontiguousarray(back).astype(ml_dtypes.bfloat16)

    def orders(self, chunk):
        w0, w1 = self.w
        table = np.zeros((2, self.rows, self.rts[chunk]), np.float32)
        for c in range(self.c):
            for k in range(self.wk):
                for upper, index in enumerate((k, self.wk - k)):
                    if index < w0:
                        here, spot = 0, c * w0 + index
                    elif index < self.wk:
                        here, spot = 1, c * w1 + index - w0
                    else:
                        here, spot = 1, self.c * w1 + c
                    if here == chunk:
                        table[upper, c * self.wk + k, spot] = 1.0
        return table.astype(ml_dtypes.bfloat16)


def halves(table):
    high = table.astype(np.float32).astype(ml_dtypes.bfloat16)
    low = (table - high.astype(np.float64)).astype(np.float32).astype(ml_dtypes.bfloat16)
    return high, low


def dot(left, right, numbers=(((1,), (0,)), ((), ()))):
    return lax.dot_general(left, right, numbers, preferred_element_type=f32)


def split(value):
    high = value.astype(bf16)
    return high, (value - high.astype(f32)).astype(bf16)


def moved(value, chosen, left=False):
    first, second = split(value)
    if left:
        return dot(chosen, first) + dot(chosen, second)
    rows = value.shape[0]
    if rows % 16:
        return dot(first, chosen) + dot(second, chosen)
    both = dot(jnp.concatenate([first, second], axis=0), chosen)
    return both[:rows] + both[rows:]


def depth_analysis(plan, table_ref, values):
    rows = []
    for value in values:
        high, low = split(value)
        rows.append(jnp.concatenate([high, low], axis=1))
    both = dot(table_ref[...], jnp.concatenate(rows, axis=0), NT)
    lines = both[: plan.rc] + both[plan.rc :]
    return [lines[:, j * plan.blk : (j + 1) * plan.blk] for j in range(len(values))]


def depth_synthesis(plan, table_ref, rows):
    high = rows.astype(bf16).astype(f32)
    parts = [high, rows - high, high]
    extra = table_ref.shape[0] - 3 * plan.rc
    if extra:
        parts.append(jnp.zeros((extra, rows.shape[1]), f32))
    return dot(jnp.concatenate(parts, axis=0).astype(bf16), table_ref[...], TN)


def plane_analysis(plan, step, lines_ref, plane_ref, total_ref):
    high, low = split(lines_ref[...].reshape(plan.cc * plan.rc, plan.blk))
    rows = jnp.concatenate([high, low, high], axis=1)
    for start in range(0, 2 * plan.lp, 256):
        size = min(256, 2 * plan.lp - start)
        columns = pl.ds(start, size)
        part = dot(rows, plane_ref[0, :, columns]).reshape(plan.cc, plan.rc, size)

        @pl.when(step == 0)
        def _():
            total_ref[:, :, columns] = part

        @pl.when(step > 0)
        def _():
            total_ref[:, :, columns] += part


def plane_synthesis(plan, high_rows, low_rows, plane_ref, lines_ref):
    high_table, low_table = plane_ref[0, : plan.blk], plane_ref[0, 2 * plan.blk :]
    lines = (
        dot(high_rows[...], high_table, NT)
        + dot(low_rows[...], high_table, NT)
        + dot(high_rows[...], low_table, NT)
    )
    lines_ref[...] = lines.reshape(plan.cc, plan.rc, plan.blk)


def emit_modes(plan, flag_ref, turn_ref, total_ref, keep_refs, send_refs):
    lp, half = plan.lp, plan.half
    odd = flag_ref[0] == 1
    cosine, sine = turn_ref[0:1, :], turn_ref[1:2, :]
    for c in range(plan.c):
        real, imag = total_ref[c, :, :lp], total_ref[c, :, lp:]
        real, imag = real * cosine + imag * sine, imag * cosine - real * sine
        for m, base, size, place in plan.segments(c):
            made = []
            for g in range(plan.ch):
                h = g if g < half else plan.ch - 1 - g
                even, odd_rows = (slice(place(h, kind), place(h, kind) + size) for kind in (0, 1))
                if g < half:
                    made.append((real[even] + imag[odd_rows], imag[even] - real[odd_rows]))
                else:
                    made.append((real[even] - imag[odd_rows], imag[even] + real[odd_rows]))
            for pair in range(half):
                for r in range(2):
                    low, high = made[2 * pair][r], made[2 * pair + 1][r]
                    keep_refs[m][pair, r, base : base + size, :] = jnp.where(odd, high, low)
                    send_refs[m][pair, r, base : base + size, :] = jnp.where(odd, low, high)
    for m, used in enumerate((plan.c * plan.w[0], plan.c * (plan.w[1] + 1))):
        if used < plan.rts[m]:
            blank = jnp.zeros((half, 2, plan.rts[m] - used, lp), f32)
            keep_refs[m][:, :, used:, :] = blank
            send_refs[m][:, :, used:, :] = blank


def take_modes(plan, flag_ref, turn_ref, own_refs, other_refs, total_ref, high_rows, low_rows):
    lp, half = plan.lp, plan.half
    odd = flag_ref[0] == 1
    cosine, sine = turn_ref[0:1, :], turn_ref[1:2, :]

    def group(m, g, r, rows):
        own, other = own_refs[m][g // 2, r, rows, :], other_refs[m][g // 2, r, rows, :]
        return jnp.where(odd, own, other) if g % 2 else jnp.where(odd, other, own)

    for c in range(plan.c):
        for m, base, size, place in plan.segments(c):
            rows = slice(base, base + size)
            for h in range(half):
                plus = [group(m, h, r, rows) for r in range(2)]
                minus = [group(m, plan.ch - 1 - h, r, rows) for r in range(2)]
                real, imag = plus[0] + minus[0], plus[1] + minus[1]
                here = slice(place(h, 0), place(h, 0) + size)
                total_ref[c, here, :lp] = real * cosine - imag * sine
                total_ref[c, here, lp:] = imag * cosine + real * sine
                real, imag = plus[0] - minus[0], plus[1] - minus[1]
                here = slice(place(h, 1), place(h, 1) + size)
                total_ref[c, here, :lp] = -(imag * cosine + real * sine)
                total_ref[c, here, lp:] = real * cosine - imag * sine
        used = 2 * plan.mk + 2 * half
        if used < plan.rc:
            total_ref[c, used:, :] = jnp.zeros((plan.rc - used, 2 * lp), f32)
    high, low = split(total_ref[...].reshape(plan.c * plan.rc, 2 * lp))
    high_rows[...] = high
    low_rows[...] = low


def analyse_kernel(plan, flag_ref, values_ref, plane_ref, depth_ref, turn_ref, *refs):
    keep_refs, send_refs, (lines_ref, total_ref) = refs[:2], refs[2:4], refs[4:]
    step = pl.program_id(0)

    @pl.loop(0, plan.cc, step=plan.batch)
    def _(c):
        values = [values_ref[:, c + j].reshape(plan.blk, plan.nz) for j in range(plan.batch)]
        for j, lines in enumerate(depth_analysis(plan, depth_ref, values)):
            lines_ref[c + j] = lines

    plane_analysis(plan, step, lines_ref, plane_ref, total_ref)

    @pl.when(step == pl.num_programs(0) - 1)
    def _():
        emit_modes(plan, flag_ref, turn_ref, total_ref, keep_refs, send_refs)


def fields(plan, inverse_ref, lines_ref, first):
    lines = jnp.concatenate([lines_ref[first + j] for j in range(plan.batch)], axis=1)
    values = depth_synthesis(plan, inverse_ref, lines)
    return [values[j * plan.blk : (j + 1) * plan.blk] for j in range(plan.batch)]


def middle_kernel(plan, flag_ref, *refs):
    own_refs, other_refs, refs = refs[:2], refs[2:4], refs[4:]
    linear_ref, cotangent_ref, plane_ref, depth_ref, inverse_ref, turn_ref, output_ref, gradient_ref = refs[:8]
    keep_refs, send_refs, (lines_ref, back_ref, total_ref, high_rows, low_rows) = refs[8:10], refs[10:12], refs[12:]
    step = pl.program_id(0)

    @pl.when(step == 0)
    def _():
        take_modes(plan, flag_ref, turn_ref, own_refs, other_refs, total_ref, high_rows, low_rows)

    plane_synthesis(plan, high_rows, low_rows, plane_ref, lines_ref)
    shape = (plan.xb, plan.ny, plan.nz)

    @pl.loop(0, plan.cc, step=plan.batch)
    def _(first):
        gradients = []
        for j, field in enumerate(fields(plan, inverse_ref, lines_ref, first)):
            value = field + linear_ref[:, first + j].reshape(plan.blk, plan.nz)
            gate = 0.5 * (1.0 + lax.erf(value * root_half))
            slope = gate + value * jnp.exp(-0.5 * value * value) * inv_root_two_pi
            output_ref[:, first + j] = (value * gate).reshape(shape)
            gradients.append(cotangent_ref[:, first + j].reshape(plan.blk, plan.nz) * slope)
            gradient_ref[:, first + j] = gradients[-1].reshape(shape)
        for j, lines in enumerate(depth_analysis(plan, depth_ref, gradients)):
            back_ref[first + j] = lines

    plane_analysis(plan, step, back_ref, plane_ref, total_ref)

    @pl.when(step == pl.num_programs(0) - 1)
    def _():
        emit_modes(plan, flag_ref, turn_ref, total_ref, keep_refs, send_refs)


def synthesise_kernel(plan, flag_ref, *refs):
    own_refs, other_refs, refs = refs[:2], refs[2:4], refs[4:]
    linear_ref, plane_ref, inverse_ref, turn_ref, output_ref, lines_ref, total_ref, high_rows, low_rows = refs

    @pl.when(pl.program_id(0) == 0)
    def _():
        take_modes(plan, flag_ref, turn_ref, own_refs, other_refs, total_ref, high_rows, low_rows)

    plane_synthesis(plan, high_rows, low_rows, plane_ref, lines_ref)

    @pl.loop(0, plan.cc, step=plan.batch)
    def _(first):
        for j, field in enumerate(fields(plan, inverse_ref, lines_ref, first)):
            value = field + linear_ref[:, first + j].reshape(plan.blk, plan.nz)
            output_ref[:, first + j] = value.reshape(plan.xb, plan.ny, plan.nz)


def linear_kernel(plan, values_ref, weight_ref, bias_ref, output_ref):
    tiles = [(x, slice(t * 8, (t + 1) * 8)) for x in range(plan.lb) for t in range(plan.ny // 8)]
    values = [values_ref[x, :, t, :].reshape(plan.c * 8, plan.nz) for x, t in tiles]
    high, low = split(jnp.concatenate(values, axis=1))
    size = 8 * plan.c
    row, column = (lax.broadcasted_iota(jnp.int32, (size, plan.c), n) for n in (0, 1))
    repeat = (row // 8 == column).astype(f32)
    exact = partial(lax.dot_general, precision=lax.Precision.HIGHEST, preferred_element_type=f32)
    spread = exact(exact(repeat, weight_ref[...], (((1,), (0,)), ((), ()))), repeat, NT)
    row, column = (lax.broadcasted_iota(jnp.int32, (size, size), n) for n in (0, 1))
    high_matrix, low_matrix = split(jnp.where(row % 8 == column % 8, spread, 0.0))
    bias = exact(repeat, bias_ref[...], (((1,), (1,)), ((), ())))
    matrix = jnp.concatenate([high_matrix, high_matrix, low_matrix], axis=1)
    mixed = dot(matrix, jnp.concatenate([high, low, high], axis=0)) + bias
    for n, (x, t) in enumerate(tiles):
        output_ref[x, :, t, :] = mixed[:, n * plan.nz : (n + 1) * plan.nz].reshape(plan.c, 8, plan.nz)


def pick(plan, parts, chosen_ref, ordered_ref):
    @pl.when(pl.program_id(0) == 0)
    def _():
        for n in range(2):
            found = [moved(part[n][...], part[2][...], left=True) for part in parts]
            ordered_ref[:, n * plan.ll : (n + 1) * plan.ll] = sum(found[1:], found[0])

    return [moved(ordered_ref[...], chosen_ref[n]) for n in range(plan.bb)]


def give(plan, made_ref, order_ref, back_ref, own_ref, mirror_ref, sums_ref):
    part = moved(made_ref[0], back_ref[0])
    for n in range(1, plan.bb):
        part = part + moved(made_ref[n], back_ref[n])
    step = pl.program_id(0)

    @pl.when(step == 0)
    def _():
        sums_ref[...] = part

    @pl.when(step > 0)
    def _():
        sums_ref[...] += part

    @pl.when(step == pl.num_programs(0) - 1)
    def _():
        own_ref[...] = moved(sums_ref[:, : plan.ll], order_ref[...], left=True)
        mirror_ref[...] = moved(sums_ref[:, plan.ll :], order_ref[...], left=True)


def mix_kernel(
    plan, own_ref, mirror_ref, order_ref, disorder_ref, chosen_ref, back_ref, weight_ref,
    own_out, mirror_out, ordered_ref, made_ref, sums_ref,
):
    wk, quarters = plan.wk, 128 // plan.mx
    picked = pick(plan, [(own_ref, mirror_ref, order_ref)], chosen_ref, ordered_ref)
    place = lax.broadcasted_iota(jnp.int32, (wk, 128), 1) // plan.mx
    for n, modes in enumerate(picked):
        for t in range(plan.c // quarters):
            columns = slice(t * 128, (t + 1) * 128)
            real = imag = 0.0
            for i in range(plan.c):
                x_real, x_imag = modes[i * wk : (i + 1) * wk, :128], modes[i * wk : (i + 1) * wk, 128:]
                w_real, w_imag = weight_ref[n, 0, i, :, columns], weight_ref[n, 1, i, :, columns]
                real = real + (w_real * x_real - w_imag * x_imag)
                imag = imag + (w_real * x_imag + w_imag * x_real)
            for q in range(quarters):
                o = t * quarters + q
                made_ref[n, o * wk : (o + 1) * wk, :128] = jnp.where(place == q, real, 0.0)
                made_ref[n, o * wk : (o + 1) * wk, 128:] = jnp.where(place == q, imag, 0.0)
    give(plan, made_ref, disorder_ref, back_ref, own_out, mirror_out, sums_ref)


def along(plan, modes):
    wk, quarters = plan.wk, 128 // plan.mx
    place = lax.broadcasted_iota(jnp.int32, (wk, 128), 1) // plan.mx
    lined = []
    for t in range(plan.c // quarters):
        real = imag = 0.0
        for q in range(quarters):
            o = t * quarters + q
            real = jnp.where(place == q, modes[o * wk : (o + 1) * wk, :128], real)
            imag = jnp.where(place == q, modes[o * wk : (o + 1) * wk, 128:], imag)
        lined.append((slice(t * 128, (t + 1) * 128), real, imag))
    return lined


def mix_back_kernel(
    plan, own_ref, mirror_ref, order_ref, disorder_ref, chosen_ref, back_ref, weight_ref,
    own_out, mirror_out, ordered_ref, made_ref, sums_ref,
):
    wk = plan.wk
    for n, grads in enumerate(pick(plan, [(own_ref, mirror_ref, order_ref)], chosen_ref, ordered_ref)):
        lined = along(plan, grads)
        for i in range(plan.c):
            back_real = back_imag = 0.0
            for columns, real, imag in lined:
                w_real, w_imag = weight_ref[n, 0, i, :, columns], weight_ref[n, 1, i, :, columns]
                back_real = back_real + (w_real * real + w_imag * imag)
                back_imag = back_imag + (w_real * imag - w_imag * real)
            made_ref[n, i * wk : (i + 1) * wk, :128] = back_real
            made_ref[n, i * wk : (i + 1) * wk, 128:] = back_imag
    give(plan, made_ref, disorder_ref, back_ref, own_out, mirror_out, sums_ref)


def outer_kernel(plan, *refs):
    parts = [refs[:8][2 * m : 2 * m + 2] for m in range(4)]
    orders, chosen_ref, gradient_ref, mode_rows, grad_rows = refs[8:10], refs[10], refs[11], refs[12], refs[13]
    wk = plan.wk
    modes = pick(plan, [(*parts[m], orders[m]) for m in range(2)], chosen_ref, mode_rows)
    grads = pick(plan, [(*parts[2 + m], orders[m]) for m in range(2)], chosen_ref, grad_rows)
    for n in range(plan.bb):
        lined = along(plan, grads[n])
        for i in range(plan.c):
            rows = slice(i * wk, (i + 1) * wk)
            x_real, x_imag = modes[n][rows, :128], modes[n][rows, 128:]
            for columns, real, imag in lined:
                gradient_ref[n, 0, i, :, columns] = real * x_real + imag * x_imag
                gradient_ref[n, 1, i, :, columns] = imag * x_real - real * x_imag


def halve_kernel(flag_ref, keep_ref, arrived_ref, kept_ref, send_ref):
    odd = flag_ref[0] == 1
    for pair in range(kept_ref.shape[0]):
        low = keep_ref[2 * pair] + arrived_ref[2 * pair]
        high = keep_ref[2 * pair + 1] + arrived_ref[2 * pair + 1]
        kept_ref[pair] = jnp.where(odd, high, low)
        send_ref[pair] = jnp.where(odd, low, high)


def cut_kernel(plan, slab_ref, keep_ref, arrived_ref, *refs):
    out_refs, held_ref = refs[:-1], refs[-1]
    lane = lax.broadcasted_iota(jnp.int32, held_ref.shape[1:], 1)
    real = keep_ref[0, 0] + arrived_ref[0, 0]
    imag = keep_ref[0, 1] + arrived_ref[0, 1]
    for g in range(plan.s):
        first = pltpu.roll(real, (plan.lp - g * plan.span) % plan.lp, 1)[:, : plan.ll]
        second = pltpu.roll(imag, (plan.lp - g * plan.span + plan.span) % plan.lp, 1)[:, : plan.ll]
        held_ref[g] = jnp.where(lane < plan.span, first, jnp.where(lane < 2 * plan.span, second, 0.0))
    for j, out_ref in enumerate(out_refs):
        out_ref[...] = held_ref[slab_ref[0] ^ j]


def join_kernel(plan, slab_ref, *refs):
    piece_refs, total_ref, held_ref = refs[:-2], refs[-2], refs[-1]
    for j, piece_ref in enumerate(piece_refs):
        held_ref[j] = piece_ref[...]
    rows = held_ref.shape[1]
    lane = lax.broadcasted_iota(jnp.int32, (rows, plan.lp), 1)
    real = imag = jnp.zeros((rows, plan.lp), f32)
    blank = jnp.zeros((rows, plan.lp - plan.ll), f32)
    for g in range(plan.s):
        piece = jnp.concatenate([held_ref[slab_ref[0] ^ g], blank], axis=1)
        here = (lane >= g * plan.span) & (lane < (g + 1) * plan.span)
        real = jnp.where(here, pltpu.roll(piece, g * plan.span, 1), real)
        imag = jnp.where(here, pltpu.roll(piece, (g * plan.span - plan.span) % plan.lp, 1), imag)
    total_ref[0, 0] = real
    total_ref[0, 1] = imag


def whole(array):
    zeros = (0,) * array.ndim
    return pl.BlockSpec(array.shape, lambda i: zeros, pipeline_mode=pl.Buffered(1))


def whole_shape(shape):
    zeros = (0,) * len(shape)
    return pl.BlockSpec(shape, lambda i: zeros, pipeline_mode=pl.Buffered(1))


def leading(shape):
    rest = (0,) * (len(shape) - 1)
    return pl.BlockSpec(shape, lambda i: (i,) + rest)


def shaped(*shape):
    return jax.ShapeDtypeStruct(shape, f32)


def anywhere():
    return pl.BlockSpec(memory_space=pl.ANY)


def scalar():
    return pl.BlockSpec(memory_space=pltpu.SMEM)


def call(kernel, name, grid, in_specs, out_specs, out_shape, scratch, cost, before=(), aliases=None):
    skipped = len(before)
    run = pl.pallas_call(
        lambda *refs: kernel(*refs[skipped:]),
        grid=(grid,),
        in_specs=[anywhere()] * skipped + list(in_specs),
        out_specs=out_specs,
        out_shape=out_shape,
        scratch_shapes=scratch,
        name=name,
        input_output_aliases=aliases or {},
        compiler_params=pltpu.CompilerParams(vmem_limit_bytes=VMEM_LIMIT, dimension_semantics=("arbitrary",)),
        cost_estimate=pl.CostEstimate(flops=int(cost * 1.15e9), bytes_accessed=int(cost * 3.6e6), transcendentals=0),
    )
    return partial(run, *before)


def tie(value, *before):
    if not before:
        return value
    return pl.pallas_call(
        lambda *refs: None,
        in_specs=[anywhere()] * (1 + len(before)),
        out_specs=anywhere(),
        out_shape=jax.ShapeDtypeStruct(value.shape, value.dtype),
        input_output_aliases={0: 0},
        name="tie",
    )(value, *before)


class Program:
    def __init__(self, plan):
        self.plan = plan
        self.plane = jnp.asarray(plan.plane_table())
        self.depth = jnp.asarray(plan.depth_forward())
        self.inverse = jnp.asarray(plan.depth_inverse())
        slab, chan = lax.axis_index("slab"), lax.axis_index("chan")
        self.slab, self.chan = slab, chan
        turns = jnp.asarray(plan.turns())
        self.turn = lax.dynamic_index_in_dim(
            lax.dynamic_index_in_dim(turns, slab, 0, False), chan, 0, False
        )
        self.slab_index = slab.astype(jnp.int32).reshape(1)
        self.flag = (chan % 2).astype(jnp.int32).reshape(1)
        upper = (chan >= plan.half).astype(jnp.int32)
        tables = [plan.orders(m) for m in range(plan.chunks)]
        self.order = [lax.dynamic_index_in_dim(jnp.asarray(t), upper, 0, False) for t in tables]
        tables = [np.ascontiguousarray(np.swapaxes(t, 1, 2)) for t in tables]
        self.disorder = [lax.dynamic_index_in_dim(jnp.asarray(t), upper, 0, False) for t in tables]
        chosen, back = plan.selections()
        self.chosen, self.back = jnp.asarray(chosen), jnp.asarray(back)

    def half_shapes(self):
        plan = self.plan
        return [(plan.half, 2, rt, plan.lp) for rt in plan.rts]

    def field_spec(self):
        plan = self.plan
        return leading((plan.xb, plan.c, plan.ny, plan.nz))

    def table(self):
        plan = self.plan
        return leading((1, 3 * plan.blk, 2 * plan.lp))

    def lines(self):
        plan = self.plan
        return pltpu.VMEM((plan.cc, plan.rc, plan.blk), f32)

    def spectra(self):
        plan = self.plan
        rows = pltpu.VMEM((plan.cc * plan.rc, 2 * plan.lp), bf16)
        return [pltpu.VMEM((plan.cc, plan.rc, 2 * plan.lp), f32), rows, rows]

    def analyse(self, values):
        plan = self.plan
        halves = self.half_shapes()
        made = call(
            partial(analyse_kernel, plan), "analyse", plan.nx // plan.xb,
            [scalar(), self.field_spec(), self.table(), whole(self.depth), whole(self.turn)],
            [whole_shape(h) for h in halves * 2], [shaped(*h) for h in halves * 2],
            [self.lines(), self.spectra()[0]], 26,
        )(self.flag, values, self.plane, self.depth, self.turn)
        return made[:2], made[2:]

    def middle(self, owns, others, linear, cotangent):
        plan = self.plan
        halves = self.half_shapes()
        field, spec = shaped(plan.nx, plan.c, plan.ny, plan.nz), self.field_spec()
        modes = [whole_shape(h) for h in halves * 2]
        output, gradient, *made = call(
            partial(middle_kernel, plan), "middle", plan.nx // plan.xb,
            [scalar(), *modes, spec, spec, self.table(), whole(self.depth), whole(self.inverse), whole(self.turn)],
            [spec, spec, *modes], [field, field, *[shaped(*h) for h in halves * 2]],
            [self.lines(), self.lines(), *self.spectra()], 47,
        )(self.flag, *owns, *others, linear, cotangent, self.plane, self.depth, self.inverse, self.turn)
        return output, gradient, made[:2], made[2:]

    def synthesise(self, before, owns, others, linear):
        plan = self.plan
        spec = self.field_spec()
        return call(
            partial(synthesise_kernel, plan), "synthesise", plan.nx // plan.xb,
            [scalar(), *[whole_shape(h) for h in self.half_shapes() * 2], spec, self.table(),
             whole(self.inverse), whole(self.turn)],
            spec, shaped(plan.nx, plan.c, plan.ny, plan.nz),
            [self.lines(), *self.spectra()], 20, before,
        )(self.flag, *owns, *others, linear, self.plane, self.inverse, self.turn)

    def linear(self, before, values, matrix, bias):
        plan = self.plan
        bias = bias[None]
        spec = leading((plan.lb, plan.c, plan.ny, plan.nz))
        return call(
            partial(linear_kernel, plan), "linear", plan.nx // plan.lb,
            [spec, whole(matrix), whole(bias)],
            spec, shaped(plan.nx, plan.c, plan.ny, plan.nz), [],
            12, before,
        )(values, matrix, bias)

    def mix(self, kernel, name, chunk, before, own, mirror, weights):
        plan = self.plan
        modes = (plan.rts[chunk], plan.ll)
        order, disorder = self.order[chunk], self.disorder[chunk]
        ordered = pltpu.VMEM((plan.rows, 2 * plan.ll), f32)
        return call(
            partial(kernel, plan), name, plan.wb // plan.bb,
            [
                whole_shape(modes), whole_shape(modes), whole(order), whole(disorder),
                leading((plan.bb,) + self.chosen.shape[1:]), leading((plan.bb,) + self.back.shape[1:]),
                leading((plan.bb, *weights.shape[1:])),
            ],
            [whole_shape(modes)] * 2, [shaped(*modes)] * 2,
            [ordered, pltpu.VMEM((plan.bb, plan.rows, 256), f32), ordered], 9, before,
        )(own, mirror, order, disorder, self.chosen, self.back, weights)

    def outer(self, before, modes, grads, weights):
        plan = self.plan
        parts = [part for pair in (*modes, *grads) for part in pair]
        ordered = pltpu.VMEM((plan.rows, 2 * plan.ll), f32)
        out = leading((plan.bb, *weights.shape[1:]))
        return call(
            partial(outer_kernel, plan), "outer", plan.wb // plan.bb,
            [*[whole(p) for p in parts], *[whole(o) for o in self.order], leading((plan.bb,) + self.chosen.shape[1:])],
            out, shaped(*weights.shape), [ordered, ordered], 9, before,
        )(*parts, *self.order, self.chosen)

    def across(self, value, axis, bit):
        size = lax.axis_size(axis)
        return lax.ppermute(value, axis, [(i, i ^ bit) for i in range(size)])

    def mirrored(self, value):
        total = self.plan.s * self.plan.ch
        return lax.ppermute(value, ("slab", "chan"), [(i, total - 1 - i) for i in range(total)])

    def halve(self, keep, arrived, bit):
        mine = ((self.chan // bit) % 2).astype(jnp.int32).reshape(1)
        half = (keep.shape[0] // 2,) + keep.shape[1:]
        return call(
            halve_kernel, "halve", 1, [scalar(), whole(keep), whole(keep)], [whole_shape(half)] * 2,
            [shaped(*half)] * 2, [], 2,
        )(mine, keep, arrived)

    def sums_over_chan(self, keep, arrived, before):
        bit, sent = 2, arrived
        while bit < self.plan.ch:
            keep, sent = self.halve(keep, arrived, bit)
            arrived = self.across(tie(sent, *before) if bit == 2 else sent, "chan", bit)
            bit *= 2
        return keep, sent, arrived

    def cut(self, keep, arrived):
        plan = self.plan
        size = (keep.shape[2], plan.ll)
        mine, *pieces = call(
            partial(cut_kernel, plan), "cut", 1, [scalar(), whole(keep), whole(keep)],
            [whole_shape(size)] * plan.s, [shaped(*size)] * plan.s, [pltpu.VMEM((plan.s, *size), f32)], 2,
        )(self.slab_index, keep, arrived)
        return mine, pieces

    def join(self, mine, arrived):
        plan = self.plan
        total = (1, 2, mine.shape[0], plan.lp)
        return call(
            partial(join_kernel, plan), "join", 1, [scalar()] + [whole(mine)] * plan.s,
            whole_shape(total), shaped(*total), [pltpu.VMEM((plan.s, *mine.shape), f32)], 2,
        )(self.slab_index, mine, *arrived)

    def exchange(self, keeps, sends, linear, mix, outer=None):
        plan = self.plan
        first = [self.across(send, "chan", 1) for send in sends]
        keep0, sent0, came0 = self.sums_over_chan(keeps[0], first[0], [])
        extra = linear([sent0, first[1]])
        came0 = tie(came0, extra)
        keep1, sent1, came1 = self.sums_over_chan(keeps[1], first[1], [came0])

        mine, pieces = self.cut(keep0, came0)
        for j, piece in enumerate(pieces):
            mine = mine + self.across(piece, "slab", j + 1)
        own0 = mine
        mirror0 = self.mirrored(own0)
        mine, pieces = self.cut(keep1, tie(came1, own0))
        arrived = [self.across(piece, "slab", j + 1) for j, piece in enumerate(pieces)]
        out0, back0 = mix(0, [mine], own0, mirror0)
        for piece in [tie(arrived[0], out0)] + arrived[1:]:
            mine = mine + piece
        own1 = mine
        mirror1 = self.mirrored(own1)

        full0 = out0 + self.mirrored(back0)
        arrived = [self.across(full0, "slab", j) for j in range(1, plan.s)]
        out1, back1 = mix(1, [full0], own1, mirror1)
        full1 = out1 + self.mirrored(back1)
        total0 = self.join(full0, [tie(arrived[0], back1)] + arrived[1:])
        came0 = self.across(total0, "chan", plan.ch // 2)
        full1 = tie(full1, total0)
        arrived = [self.across(full1, "slab", j) for j in range(1, plan.s)]
        made = None
        if outer is not None:
            made = outer([total0], ((own0, mirror0), (own1, mirror1)))
            came0 = tie(came0, made)
        total1 = tie(self.join(full1, arrived), came0)
        came1 = self.across(total1, "chan", plan.ch // 2)
        if outer is not None:
            made = tie(jnp.transpose(made, (0, 3, 2, 1, 4)), total1)
            came1 = tie(came1, made)

        owns, others = [], []
        for total, other in ((total0, came0), (total1, came1)):
            bit = plan.ch // 2
            while bit > 1:
                upper = (self.chan // bit) % 2 == 1
                total = jnp.stack([jnp.where(upper, other, total), jnp.where(upper, total, other)], axis=1)
                total = total.reshape((-1,) + total.shape[2:])
                bit //= 2
                other = self.across(total, "chan", bit)
            owns.append(total)
            others.append(other)
        return owns, others, extra, made, ((own0, mirror0), (own1, mirror1))


def local(inputs, cotangent, spectral, local_weight, bias_vector):
    nx, ny, channels, nz = inputs.shape
    wb, wk = spectral.shape[0], spectral.shape[1]
    plan = Plan(nx, ny, nz, channels, wb, wk, spectral.shape[4] // channels, lax.axis_size("slab"), lax.axis_size("chan"))
    program = Program(plan)
    values = jnp.transpose(inputs, (0, 2, 1, 3))
    slopes = jnp.transpose(cotangent, (0, 2, 1, 3))
    weights = jnp.transpose(spectral, (0, 2, 3, 1, 4))

    keeps, sends = program.analyse(values)
    owns, others, linear, _, modes = program.exchange(
        keeps, sends,
        lambda before: program.linear(before, values, local_weight.T, bias_vector),
        lambda m, before, own, mirror: program.mix(mix_kernel, "mix", m, before, own, mirror, weights),
    )
    output, gradient, keeps, sends = program.middle(owns, others, linear, slopes)
    owns, others, linear, grad_spectral, _ = program.exchange(
        keeps, sends,
        lambda before: program.linear(before, gradient, local_weight, jnp.zeros_like(bias_vector)),
        lambda m, before, own, mirror: program.mix(mix_back_kernel, "mix_back", m, before, own, mirror, weights),
        lambda before, grads: program.outer(before, modes, grads, weights),
    )
    grad_inputs = program.synthesise([], owns, others, linear)
    return (
        jnp.transpose(output, (0, 2, 1, 3)),
        jnp.transpose(grad_inputs, (0, 2, 1, 3)),
        jnp.transpose(grad_spectral, (0, 1, 3, 2, 4)),
    )


def solution(mesh):
    in_specs = (
        P(("groups", "slab"), "chan", None, None),
        P(("groups", "slab"), "chan", None, None),
        P("slab", "chan", None, None, None),
        P(),
        P(),
    )
    out_specs = (
        P(("groups", "slab"), "chan", None, None),
        P(("groups", "slab"), "chan", None, None),
        P(("groups", "slab"), "chan", None, None, None),
    )
    return jax.shard_map(local, mesh=mesh, in_specs=in_specs, out_specs=out_specs, check_vma=False)
```

```python
from functools import partial
import math

import jax
import jax.numpy as jnp
import ml_dtypes
import numpy as np
from jax import lax
from jax.experimental import pallas as pl
from jax.experimental.pallas import tpu as pltpu
from jax.sharding import PartitionSpec as P

f32 = jnp.float32
bf16 = jnp.bfloat16
root_half = 0.7071067811865476
inv_root_two_pi = 0.3989422804014327
VMEM_LIMIT = 64 * 1024 * 1024
NT = (((1,), (1,)), ((), ()))
TN = (((0,), (0,)), ((), ()))


def round_up(value, unit):
    return -(-value // unit) * unit


class Plan:
    def __init__(self, nx, ny, nz, channels, wb, wk, mx, slab_count, chan_count):
        self.nx, self.ny, self.nz, self.c = nx, ny, nz, channels
        self.wb, self.wk, self.mx = wb, wk, mx
        self.s, self.ch = slab_count, chan_count
        self.half = chan_count // 2
        self.na = mx // 2 + 1
        self.span = (wb + 1) * self.na
        self.lw = slab_count * self.span
        self.lp = round_up(self.lw, 128)
        self.ll = round_up(2 * self.span, 128)
        self.mk = self.half * wk
        self.rc = round_up(2 * self.mk + 2 * self.half, 8)
        self.chunks = 2
        self.cc = channels
        self.w = (wk // 2, wk - wk // 2)
        self.rts = (round_up(channels * self.w[0], 8), round_up(channels * (self.w[1] + 1), 8))
        self.xb = math.gcd(8, nx)
        self.blk = self.xb * ny
        self.rows = self.cc * wk
        self.tall = round_up(self.rows, 16)
        self.bb = math.gcd(2, wb)
        self.lb = math.gcd(4, nx)
        self.batch = max(d for d in range(1, 6) if self.cc % d == 0)
        self.full_x, self.full_y = nx * slab_count, ny * chan_count

    def segments(self, c):
        w0, w1 = self.w
        main = lambda first: lambda h, kind: kind * self.mk + h * self.wk + first
        return (
            (0, c * w0, w0, main(0)),
            (1, c * w1, w1, main(w0)),
            (1, self.c * w1 + c, 1, lambda h, kind: 2 * self.mk + kind * self.half + h),
        )

    def starts(self):
        kept = self.wb * self.s
        return [g * self.wb - (kept if 2 * g >= self.s else 0) for g in range(self.s)]

    def columns(self):
        b = np.concatenate([np.repeat(np.arange(st, st + self.wb + 1), self.na) for st in self.starts()])
        a = np.tile(np.arange(self.na), self.s * (self.wb + 1))
        return a, b

    def plane_table(self):
        a, b = self.columns()
        x = np.repeat(np.arange(self.nx), self.ny)[:, None]
        y = np.tile(np.arange(self.ny), self.nx)[:, None]
        total = self.full_x * self.full_y
        phase = (a * x * self.full_y + b * y * self.full_x) % total * (2.0 * np.pi / total)
        table = np.zeros((self.nx * self.ny, 2 * self.lp))
        scale = 1.0 / math.sqrt(total)
        table[:, : self.lw] = np.cos(phase) * scale
        table[:, self.lp : self.lp + self.lw] = -np.sin(phase) * scale
        high, low = (t.reshape(self.nx // self.xb, 1, self.blk, 2 * self.lp) for t in halves(table))
        return np.concatenate([high, high, low], 1).reshape(-1, 3 * self.blk, 2 * self.lp)

    def turns(self):
        a, b = self.columns()
        x = (np.arange(self.s) * self.nx)[:, None, None]
        y = (np.arange(self.ch) * self.ny)[None, :, None]
        total = self.full_x * self.full_y
        phase = (a * x * self.full_y + b * y * self.full_x) % total * (2.0 * np.pi / total)
        table = np.zeros((self.s, self.ch, 2, self.lp), np.float32)
        table[:, :, 0, : self.lw] = np.cos(phase)
        table[:, :, 1, : self.lw] = np.sin(phase)
        return table

    def depth_rows(self):
        main = np.arange(self.mk)
        edge = (np.arange(self.half) + 1) * self.wk
        z = np.arange(self.nz)
        scale = 1.0 / math.sqrt(self.nz)
        angle = lambda k: (k[:, None] * z) % self.nz * (2.0 * np.pi / self.nz)
        rows = [np.cos(angle(main)), np.sin(angle(main)), np.cos(angle(edge)), np.sin(angle(edge))]
        table = np.zeros((self.rc, self.nz))
        table[: 2 * self.mk + 2 * self.half] = np.concatenate(rows) * scale
        return halves(table)

    def depth_forward(self):
        high, low = self.depth_rows()
        return np.concatenate(
            [np.concatenate([high, high], 1), np.concatenate([low, np.zeros_like(low)], 1)], 0
        )

    def depth_inverse(self):
        high, low = self.depth_rows()
        table = np.zeros((round_up(3 * self.rc, 16), self.nz), ml_dtypes.bfloat16)
        table[: 3 * self.rc] = np.concatenate([high, high, low], 0)
        return table

    def selections(self):
        quarters = 128 // self.mx
        own = np.zeros((self.wb, 2, self.ll, 2, quarters, self.mx), np.float32)
        for b in range(self.wb):
            for r in range(2):
                for a in range(self.mx):
                    if a < self.mx // 2:
                        own[b, 0, r * self.span + b * self.na + a, r, :, a] = 1.0
                    else:
                        spot = r * self.span + (self.wb - b) * self.na + self.mx - a
                        own[b, 1, spot, r, :, a] = 1.0 - 2.0 * r
        own = own.reshape(self.wb, 2 * self.ll, 256)
        back = np.swapaxes(own, 1, 2)
        return own.astype(ml_dtypes.bfloat16), np.ascontiguousarray(back).astype(ml_dtypes.bfloat16)

    def orders(self, chunk):
        w0, w1 = self.w
        table = np.zeros((2, self.rows, self.rts[chunk]), np.float32)
        for c in range(self.c):
            for k in range(self.wk):
                for upper, index in enumerate((k, self.wk - k)):
                    if index < w0:
                        here, spot = 0, c * w0 + index
                    elif index < self.wk:
                        here, spot = 1, c * w1 + index - w0
                    else:
                        here, spot = 1, self.c * w1 + c
                    if here == chunk:
                        table[upper, c * self.wk + k, spot] = 1.0
        return table.astype(ml_dtypes.bfloat16)


def halves(table):
    high = table.astype(np.float32).astype(ml_dtypes.bfloat16)
    low = (table - high.astype(np.float64)).astype(np.float32).astype(ml_dtypes.bfloat16)
    return high, low


def dot(left, right, numbers=(((1,), (0,)), ((), ()))):
    return lax.dot_general(left, right, numbers, preferred_element_type=f32)


def split(value):
    high = value.astype(bf16)
    return high, (value - high.astype(f32)).astype(bf16)


def moved(value, chosen, left=False):
    first, second = split(value)
    if left:
        return dot(chosen, first) + dot(chosen, second)
    rows = value.shape[0]
    if rows % 16:
        return dot(first, chosen) + dot(second, chosen)
    both = dot(jnp.concatenate([first, second], axis=0), chosen)
    return both[:rows] + both[rows:]


def depth_analysis(plan, table_ref, values):
    rows = []
    for value in values:
        high, low = split(value)
        rows.append(jnp.concatenate([high, low], axis=1))
    both = dot(table_ref[...], jnp.concatenate(rows, axis=0), NT)
    lines = both[: plan.rc] + both[plan.rc :]
    return [lines[:, j * plan.blk : (j + 1) * plan.blk] for j in range(len(values))]


def depth_synthesis(plan, table_ref, rows):
    high = rows.astype(bf16).astype(f32)
    parts = [high, rows - high, high]
    extra = table_ref.shape[0] - 3 * plan.rc
    if extra:
        parts.append(jnp.zeros((extra, rows.shape[1]), f32))
    return dot(jnp.concatenate(parts, axis=0).astype(bf16), table_ref[...], TN)


def plane_analysis(plan, step, lines_ref, plane_ref, total_ref):
    high, low = split(lines_ref[...].reshape(plan.cc * plan.rc, plan.blk))
    rows = jnp.concatenate([high, low, high], axis=1)
    for start in range(0, 2 * plan.lp, 256):
        size = min(256, 2 * plan.lp - start)
        columns = pl.ds(start, size)
        part = dot(rows, plane_ref[0, :, columns]).reshape(plan.cc, plan.rc, size)

        @pl.when(step == 0)
        def _():
            total_ref[:, :, columns] = part

        @pl.when(step > 0)
        def _():
            total_ref[:, :, columns] += part


def plane_synthesis(plan, high_rows, low_rows, plane_ref, lines_ref):
    high_table, low_table = plane_ref[0, : plan.blk], plane_ref[0, 2 * plan.blk :]
    lines = (
        dot(high_rows[...], high_table, NT)
        + dot(low_rows[...], high_table, NT)
        + dot(high_rows[...], low_table, NT)
    )
    lines_ref[...] = lines.reshape(plan.cc, plan.rc, plan.blk)


def emit_modes(plan, flag_ref, turn_ref, total_ref, keep_refs, send_refs):
    lp, half = plan.lp, plan.half
    odd = flag_ref[0] == 1
    cosine, sine = turn_ref[0:1, :], turn_ref[1:2, :]
    for c in range(plan.c):
        real, imag = total_ref[c, :, :lp], total_ref[c, :, lp:]
        real, imag = real * cosine + imag * sine, imag * cosine - real * sine
        for m, base, size, place in plan.segments(c):
            made = []
            for g in range(plan.ch):
                h = g if g < half else plan.ch - 1 - g
                even, odd_rows = (slice(place(h, kind), place(h, kind) + size) for kind in (0, 1))
                if g < half:
                    made.append((real[even] + imag[odd_rows], imag[even] - real[odd_rows]))
                else:
                    made.append((real[even] - imag[odd_rows], imag[even] + real[odd_rows]))
            for pair in range(half):
                for r in range(2):
                    low, high = made[2 * pair][r], made[2 * pair + 1][r]
                    keep_refs[m][pair, r, base : base + size, :] = jnp.where(odd, high, low)
                    send_refs[m][pair, r, base : base + size, :] = jnp.where(odd, low, high)
    for m, used in enumerate((plan.c * plan.w[0], plan.c * (plan.w[1] + 1))):
        if used < plan.rts[m]:
            blank = jnp.zeros((half, 2, plan.rts[m] - used, lp), f32)
            keep_refs[m][:, :, used:, :] = blank
            send_refs[m][:, :, used:, :] = blank


def take_modes(plan, flag_ref, turn_ref, own_refs, other_refs, total_ref, high_rows, low_rows):
    lp, half = plan.lp, plan.half
    odd = flag_ref[0] == 1
    cosine, sine = turn_ref[0:1, :], turn_ref[1:2, :]

    def group(m, g, r, rows):
        own, other = own_refs[m][g // 2, r, rows, :], other_refs[m][g // 2, r, rows, :]
        return jnp.where(odd, own, other) if g % 2 else jnp.where(odd, other, own)

    for c in range(plan.c):
        for m, base, size, place in plan.segments(c):
            rows = slice(base, base + size)
            for h in range(half):
                plus = [group(m, h, r, rows) for r in range(2)]
                minus = [group(m, plan.ch - 1 - h, r, rows) for r in range(2)]
                real, imag = plus[0] + minus[0], plus[1] + minus[1]
                here = slice(place(h, 0), place(h, 0) + size)
                total_ref[c, here, :lp] = real * cosine - imag * sine
                total_ref[c, here, lp:] = imag * cosine + real * sine
                real, imag = plus[0] - minus[0], plus[1] - minus[1]
                here = slice(place(h, 1), place(h, 1) + size)
                total_ref[c, here, :lp] = -(imag * cosine + real * sine)
                total_ref[c, here, lp:] = real * cosine - imag * sine
        used = 2 * plan.mk + 2 * half
        if used < plan.rc:
            total_ref[c, used:, :] = jnp.zeros((plan.rc - used, 2 * lp), f32)
    high, low = split(total_ref[...].reshape(plan.c * plan.rc, 2 * lp))
    high_rows[...] = high
    low_rows[...] = low


def analyse_kernel(plan, flag_ref, values_ref, plane_ref, depth_ref, turn_ref, *refs):
    keep_refs, send_refs, (lines_ref, total_ref) = refs[:2], refs[2:4], refs[4:]
    step = pl.program_id(0)

    @pl.loop(0, plan.cc, step=plan.batch)
    def _(c):
        values = [values_ref[:, c + j].reshape(plan.blk, plan.nz) for j in range(plan.batch)]
        for j, lines in enumerate(depth_analysis(plan, depth_ref, values)):
            lines_ref[c + j] = lines

    plane_analysis(plan, step, lines_ref, plane_ref, total_ref)

    @pl.when(step == pl.num_programs(0) - 1)
    def _():
        emit_modes(plan, flag_ref, turn_ref, total_ref, keep_refs, send_refs)


def fields(plan, inverse_ref, lines_ref, first):
    lines = jnp.concatenate([lines_ref[first + j] for j in range(plan.batch)], axis=1)
    values = depth_synthesis(plan, inverse_ref, lines)
    return [values[j * plan.blk : (j + 1) * plan.blk] for j in range(plan.batch)]


def middle_kernel(plan, flag_ref, *refs):
    own_refs, other_refs, refs = refs[:2], refs[2:4], refs[4:]
    linear_ref, cotangent_ref, plane_ref, depth_ref, inverse_ref, turn_ref, output_ref, gradient_ref = refs[:8]
    keep_refs, send_refs, (lines_ref, back_ref, total_ref, high_rows, low_rows) = refs[8:10], refs[10:12], refs[12:]
    step = pl.program_id(0)

    @pl.when(step == 0)
    def _():
        take_modes(plan, flag_ref, turn_ref, own_refs, other_refs, total_ref, high_rows, low_rows)

    plane_synthesis(plan, high_rows, low_rows, plane_ref, lines_ref)
    shape = (plan.xb, plan.ny, plan.nz)

    @pl.loop(0, plan.cc, step=plan.batch)
    def _(first):
        gradients = []
        for j, field in enumerate(fields(plan, inverse_ref, lines_ref, first)):
            value = field + linear_ref[:, first + j].reshape(plan.blk, plan.nz)
            gate = 0.5 * (1.0 + lax.erf(value * root_half))
            slope = gate + value * jnp.exp(-0.5 * value * value) * inv_root_two_pi
            output_ref[:, first + j] = (value * gate).reshape(shape)
            gradients.append(cotangent_ref[:, first + j].reshape(plan.blk, plan.nz) * slope)
            gradient_ref[:, first + j] = gradients[-1].reshape(shape)
        for j, lines in enumerate(depth_analysis(plan, depth_ref, gradients)):
            back_ref[first + j] = lines

    plane_analysis(plan, step, back_ref, plane_ref, total_ref)

    @pl.when(step == pl.num_programs(0) - 1)
    def _():
        emit_modes(plan, flag_ref, turn_ref, total_ref, keep_refs, send_refs)


def synthesise_kernel(plan, flag_ref, *refs):
    own_refs, other_refs, refs = refs[:2], refs[2:4], refs[4:]
    linear_ref, plane_ref, inverse_ref, turn_ref, output_ref, lines_ref, total_ref, high_rows, low_rows = refs

    @pl.when(pl.program_id(0) == 0)
    def _():
        take_modes(plan, flag_ref, turn_ref, own_refs, other_refs, total_ref, high_rows, low_rows)

    plane_synthesis(plan, high_rows, low_rows, plane_ref, lines_ref)

    @pl.loop(0, plan.cc, step=plan.batch)
    def _(first):
        for j, field in enumerate(fields(plan, inverse_ref, lines_ref, first)):
            value = field + linear_ref[:, first + j].reshape(plan.blk, plan.nz)
            output_ref[:, first + j] = value.reshape(plan.xb, plan.ny, plan.nz)


def linear_kernel(plan, values_ref, weight_ref, bias_ref, output_ref):
    tiles = [(x, slice(t * 8, (t + 1) * 8)) for x in range(plan.lb) for t in range(plan.ny // 8)]
    values = [values_ref[x, :, t, :].reshape(plan.c * 8, plan.nz) for x, t in tiles]
    high, low = split(jnp.concatenate(values, axis=1))
    size = 8 * plan.c
    row, column = (lax.broadcasted_iota(jnp.int32, (size, plan.c), n) for n in (0, 1))
    repeat = (row // 8 == column).astype(f32)
    exact = partial(lax.dot_general, precision=lax.Precision.HIGHEST, preferred_element_type=f32)
    spread = exact(exact(repeat, weight_ref[...], (((1,), (0,)), ((), ()))), repeat, NT)
    row, column = (lax.broadcasted_iota(jnp.int32, (size, size), n) for n in (0, 1))
    high_matrix, low_matrix = split(jnp.where(row % 8 == column % 8, spread, 0.0))
    bias = exact(repeat, bias_ref[...], (((1,), (1,)), ((), ())))
    matrix = jnp.concatenate([high_matrix, high_matrix, low_matrix], axis=1)
    mixed = dot(matrix, jnp.concatenate([high, low, high], axis=0)) + bias
    for n, (x, t) in enumerate(tiles):
        output_ref[x, :, t, :] = mixed[:, n * plan.nz : (n + 1) * plan.nz].reshape(plan.c, 8, plan.nz)


def pick(plan, parts, chosen_ref, ordered_ref):
    @pl.when(pl.program_id(0) == 0)
    def _():
        for n in range(2):
            found = [moved(part[n][...], part[2][...], left=True) for part in parts]
            high, low = split(sum(found[1:], found[0]))
            ordered_ref[: plan.rows, n * plan.ll : (n + 1) * plan.ll] = high
            ordered_ref[plan.tall : plan.tall + plan.rows, n * plan.ll : (n + 1) * plan.ll] = low

    both = [dot(ordered_ref[...], chosen_ref[n]) for n in range(plan.bb)]
    return [b[: plan.rows] + b[plan.tall : plan.tall + plan.rows] for b in both]


def give(plan, made_ref, order_ref, back_ref, own_ref, mirror_ref, sums_ref):
    part = moved(made_ref[0], back_ref[0])
    for n in range(1, plan.bb):
        part = part + moved(made_ref[n], back_ref[n])
    step = pl.program_id(0)

    @pl.when(step == 0)
    def _():
        sums_ref[...] = part

    @pl.when(step > 0)
    def _():
        sums_ref[...] += part

    @pl.when(step == pl.num_programs(0) - 1)
    def _():
        own_ref[...] = moved(sums_ref[:, : plan.ll], order_ref[...], left=True)
        mirror_ref[...] = moved(sums_ref[:, plan.ll :], order_ref[...], left=True)


def mix_kernel(
    plan, own_ref, mirror_ref, order_ref, disorder_ref, chosen_ref, back_ref, weight_ref,
    own_out, mirror_out, ordered_ref, made_ref, sums_ref,
):
    wk, quarters = plan.wk, 128 // plan.mx
    picked = pick(plan, [(own_ref, mirror_ref, order_ref)], chosen_ref, ordered_ref)
    place = lax.broadcasted_iota(jnp.int32, (wk, 128), 1) // plan.mx
    for n, modes in enumerate(picked):
        for t in range(plan.c // quarters):
            columns = slice(t * 128, (t + 1) * 128)
            real = imag = 0.0
            for i in range(plan.c):
                x_real, x_imag = modes[i * wk : (i + 1) * wk, :128], modes[i * wk : (i + 1) * wk, 128:]
                w_real, w_imag = weight_ref[n, 0, i, :, columns], weight_ref[n, 1, i, :, columns]
                real = real + (w_real * x_real - w_imag * x_imag)
                imag = imag + (w_real * x_imag + w_imag * x_real)
            for q in range(quarters):
                o = t * quarters + q
                made_ref[n, o * wk : (o + 1) * wk, :128] = jnp.where(place == q, real, 0.0)
                made_ref[n, o * wk : (o + 1) * wk, 128:] = jnp.where(place == q, imag, 0.0)
    give(plan, made_ref, disorder_ref, back_ref, own_out, mirror_out, sums_ref)


def along(plan, modes):
    wk, quarters = plan.wk, 128 // plan.mx
    place = lax.broadcasted_iota(jnp.int32, (wk, 128), 1) // plan.mx
    lined = []
    for t in range(plan.c // quarters):
        real = imag = 0.0
        for q in range(quarters):
            o = t * quarters + q
            real = jnp.where(place == q, modes[o * wk : (o + 1) * wk, :128], real)
            imag = jnp.where(place == q, modes[o * wk : (o + 1) * wk, 128:], imag)
        lined.append((slice(t * 128, (t + 1) * 128), real, imag))
    return lined


def mix_back_kernel(
    plan, own_ref, mirror_ref, order_ref, disorder_ref, chosen_ref, back_ref, weight_ref,
    own_out, mirror_out, ordered_ref, made_ref, sums_ref,
):
    wk = plan.wk
    for n, grads in enumerate(pick(plan, [(own_ref, mirror_ref, order_ref)], chosen_ref, ordered_ref)):
        lined = along(plan, grads)
        for i in range(plan.c):
            back_real = back_imag = 0.0
            for columns, real, imag in lined:
                w_real, w_imag = weight_ref[n, 0, i, :, columns], weight_ref[n, 1, i, :, columns]
                back_real = back_real + (w_real * real + w_imag * imag)
                back_imag = back_imag + (w_real * imag - w_imag * real)
            made_ref[n, i * wk : (i + 1) * wk, :128] = back_real
            made_ref[n, i * wk : (i + 1) * wk, 128:] = back_imag
    give(plan, made_ref, disorder_ref, back_ref, own_out, mirror_out, sums_ref)


def outer_kernel(plan, *refs):
    parts = [refs[:8][2 * m : 2 * m + 2] for m in range(4)]
    orders, chosen_ref, gradient_ref, mode_rows, grad_rows = refs[8:10], refs[10], refs[11], refs[12], refs[13]
    wk = plan.wk
    modes = pick(plan, [(*parts[m], orders[m]) for m in range(2)], chosen_ref, mode_rows)
    grads = pick(plan, [(*parts[2 + m], orders[m]) for m in range(2)], chosen_ref, grad_rows)
    for n in range(plan.bb):
        lined = along(plan, grads[n])
        for i in range(plan.c):
            rows = slice(i * wk, (i + 1) * wk)
            x_real, x_imag = modes[n][rows, :128], modes[n][rows, 128:]
            for columns, real, imag in lined:
                gradient_ref[n, 0, i, :, columns] = real * x_real + imag * x_imag
                gradient_ref[n, 1, i, :, columns] = imag * x_real - real * x_imag


def halve_kernel(flag_ref, keep_ref, arrived_ref, kept_ref, send_ref):
    odd = flag_ref[0] == 1
    for pair in range(kept_ref.shape[0]):
        low = keep_ref[2 * pair] + arrived_ref[2 * pair]
        high = keep_ref[2 * pair + 1] + arrived_ref[2 * pair + 1]
        kept_ref[pair] = jnp.where(odd, high, low)
        send_ref[pair] = jnp.where(odd, low, high)


def send_kernel(place_ref, keep_ref, arrived_ref, send_ref):
    send_ref[...] = keep_ref[...] + arrived_ref[...]


def cut_kernel(plan, place_ref, keep_ref, arrived_ref, came_ref, *refs):
    out_refs, held_ref = refs[:-1], refs[-1]
    lane = lax.broadcasted_iota(jnp.int32, held_ref.shape[1:], 1)
    real = keep_ref[0, 0] + arrived_ref[0, 0] + came_ref[0, 0]
    imag = keep_ref[0, 1] + arrived_ref[0, 1] + came_ref[0, 1]
    for g in range(plan.s):
        first = pltpu.roll(real, (plan.lp - g * plan.span) % plan.lp, 1)[:, : plan.ll]
        second = pltpu.roll(imag, (plan.lp - g * plan.span + plan.span) % plan.lp, 1)[:, : plan.ll]
        held_ref[g] = jnp.where(lane < plan.span, first, jnp.where(lane < 2 * plan.span, second, 0.0))
    for j, out_ref in enumerate(out_refs):
        out_ref[...] = held_ref[place_ref[0] ^ j]


def join_kernel(plan, slab_ref, *refs):
    piece_refs, total_ref, held_ref = refs[:-2], refs[-2], refs[-1]
    for j, piece_ref in enumerate(piece_refs):
        held_ref[j] = piece_ref[...]
    rows = held_ref.shape[1]
    lane = lax.broadcasted_iota(jnp.int32, (rows, plan.lp), 1)
    real = imag = jnp.zeros((rows, plan.lp), f32)
    blank = jnp.zeros((rows, plan.lp - plan.ll), f32)
    for g in range(plan.s):
        piece = jnp.concatenate([held_ref[slab_ref[0] ^ g], blank], axis=1)
        here = (lane >= g * plan.span) & (lane < (g + 1) * plan.span)
        real = jnp.where(here, pltpu.roll(piece, g * plan.span, 1), real)
        imag = jnp.where(here, pltpu.roll(piece, (g * plan.span - plan.span) % plan.lp, 1), imag)
    total_ref[0, 0] = real
    total_ref[0, 1] = imag


def whole(array):
    zeros = (0,) * array.ndim
    return pl.BlockSpec(array.shape, lambda i: zeros, pipeline_mode=pl.Buffered(1))


def whole_shape(shape):
    zeros = (0,) * len(shape)
    return pl.BlockSpec(shape, lambda i: zeros, pipeline_mode=pl.Buffered(1))


def leading(shape):
    rest = (0,) * (len(shape) - 1)
    return pl.BlockSpec(shape, lambda i: (i,) + rest)


def shaped(*shape):
    return jax.ShapeDtypeStruct(shape, f32)


def anywhere():
    return pl.BlockSpec(memory_space=pl.ANY)


def scalar():
    return pl.BlockSpec(memory_space=pltpu.SMEM)


def call(kernel, name, grid, in_specs, out_specs, out_shape, scratch, cost, before=(), aliases=None):
    skipped = len(before)
    run = pl.pallas_call(
        lambda *refs: kernel(*refs[skipped:]),
        grid=(grid,),
        in_specs=[anywhere()] * skipped + list(in_specs),
        out_specs=out_specs,
        out_shape=out_shape,
        scratch_shapes=scratch,
        name=name,
        input_output_aliases=aliases or {},
        compiler_params=pltpu.CompilerParams(vmem_limit_bytes=VMEM_LIMIT, dimension_semantics=("arbitrary",)),
        cost_estimate=pl.CostEstimate(flops=int(cost * 1.15e9), bytes_accessed=int(cost * 3.6e6), transcendentals=0),
    )
    return partial(run, *before)


def tie(value, *before):
    if not before:
        return value
    return pl.pallas_call(
        lambda *refs: None,
        in_specs=[anywhere()] * (1 + len(before)),
        out_specs=anywhere(),
        out_shape=jax.ShapeDtypeStruct(value.shape, value.dtype),
        input_output_aliases={0: 0},
        name="tie",
    )(value, *before)


class Program:
    def __init__(self, plan):
        self.plan = plan
        self.plane = jnp.asarray(plan.plane_table())
        self.depth = jnp.asarray(plan.depth_forward())
        self.inverse = jnp.asarray(plan.depth_inverse())
        slab, chan = lax.axis_index("slab"), lax.axis_index("chan")
        self.slab, self.chan = slab, chan
        turns = jnp.asarray(plan.turns())
        self.turn = lax.dynamic_index_in_dim(
            lax.dynamic_index_in_dim(turns, slab, 0, False), chan, 0, False
        )
        self.slab_index = slab.astype(jnp.int32).reshape(1)
        self.flag = (chan % 2).astype(jnp.int32).reshape(1)
        upper = (chan >= plan.half).astype(jnp.int32)
        tables = [plan.orders(m) for m in range(plan.chunks)]
        self.order = [lax.dynamic_index_in_dim(jnp.asarray(t), upper, 0, False) for t in tables]
        tables = [np.ascontiguousarray(np.swapaxes(t, 1, 2)) for t in tables]
        self.disorder = [lax.dynamic_index_in_dim(jnp.asarray(t), upper, 0, False) for t in tables]
        chosen, back = plan.selections()
        self.chosen, self.back = jnp.asarray(chosen), jnp.asarray(back)

    def half_shapes(self):
        plan = self.plan
        return [(plan.half, 2, rt, plan.lp) for rt in plan.rts]

    def field_spec(self):
        plan = self.plan
        return leading((plan.xb, plan.c, plan.ny, plan.nz))

    def table(self):
        plan = self.plan
        return leading((1, 3 * plan.blk, 2 * plan.lp))

    def lines(self):
        plan = self.plan
        return pltpu.VMEM((plan.cc, plan.rc, plan.blk), f32)

    def spectra(self):
        plan = self.plan
        rows = pltpu.VMEM((plan.cc * plan.rc, 2 * plan.lp), bf16)
        return [pltpu.VMEM((plan.cc, plan.rc, 2 * plan.lp), f32), rows, rows]

    def analyse(self, values):
        plan = self.plan
        halves = self.half_shapes()
        made = call(
            partial(analyse_kernel, plan), "analyse", plan.nx // plan.xb,
            [scalar(), self.field_spec(), self.table(), whole(self.depth), whole(self.turn)],
            [whole_shape(h) for h in halves * 2], [shaped(*h) for h in halves * 2],
            [self.lines(), self.spectra()[0]], 26,
        )(self.flag, values, self.plane, self.depth, self.turn)
        return made[:2], made[2:]

    def middle(self, owns, others, linear, cotangent):
        plan = self.plan
        halves = self.half_shapes()
        field, spec = shaped(plan.nx, plan.c, plan.ny, plan.nz), self.field_spec()
        modes = [whole_shape(h) for h in halves * 2]
        output, gradient, *made = call(
            partial(middle_kernel, plan), "middle", plan.nx // plan.xb,
            [scalar(), *modes, spec, spec, self.table(), whole(self.depth), whole(self.inverse), whole(self.turn)],
            [spec, spec, *modes], [field, field, *[shaped(*h) for h in halves * 2]],
            [self.lines(), self.lines(), *self.spectra()], 47,
        )(self.flag, *owns, *others, linear, cotangent, self.plane, self.depth, self.inverse, self.turn)
        return output, gradient, made[:2], made[2:]

    def synthesise(self, before, owns, others, linear):
        plan = self.plan
        spec = self.field_spec()
        return call(
            partial(synthesise_kernel, plan), "synthesise", plan.nx // plan.xb,
            [scalar(), *[whole_shape(h) for h in self.half_shapes() * 2], spec, self.table(),
             whole(self.inverse), whole(self.turn)],
            spec, shaped(plan.nx, plan.c, plan.ny, plan.nz),
            [self.lines(), *self.spectra()], 20, before,
        )(self.flag, *owns, *others, linear, self.plane, self.inverse, self.turn)

    def linear(self, before, values, matrix, bias):
        plan = self.plan
        bias = bias[None]
        spec = leading((plan.lb, plan.c, plan.ny, plan.nz))
        return call(
            partial(linear_kernel, plan), "linear", plan.nx // plan.lb,
            [spec, whole(matrix), whole(bias)],
            spec, shaped(plan.nx, plan.c, plan.ny, plan.nz), [],
            12, before,
        )(values, matrix, bias)

    def mix(self, kernel, name, chunk, before, own, mirror, weights):
        plan = self.plan
        modes = (plan.rts[chunk], plan.ll)
        order, disorder = self.order[chunk], self.disorder[chunk]
        ordered = pltpu.VMEM((2 * plan.tall, 2 * plan.ll), bf16)
        return call(
            partial(kernel, plan), name, plan.wb // plan.bb,
            [
                whole_shape(modes), whole_shape(modes), whole(order), whole(disorder),
                leading((plan.bb,) + self.chosen.shape[1:]), leading((plan.bb,) + self.back.shape[1:]),
                leading((plan.bb, *weights.shape[1:])),
            ],
            [whole_shape(modes)] * 2, [shaped(*modes)] * 2,
            [ordered, pltpu.VMEM((plan.bb, plan.rows, 256), f32), pltpu.VMEM((plan.rows, 2 * plan.ll), f32)], 9, before,
        )(own, mirror, order, disorder, self.chosen, self.back, weights)

    def outer(self, before, modes, grads, weights):
        plan = self.plan
        parts = [part for pair in (*modes, *grads) for part in pair]
        ordered = pltpu.VMEM((2 * plan.tall, 2 * plan.ll), bf16)
        out = leading((plan.bb, *weights.shape[1:]))
        return call(
            partial(outer_kernel, plan), "outer", plan.wb // plan.bb,
            [*[whole(p) for p in parts], *[whole(o) for o in self.order], leading((plan.bb,) + self.chosen.shape[1:])],
            out, shaped(*weights.shape), [ordered, ordered], 9, before,
        )(*parts, *self.order, self.chosen)

    def across(self, value, axis, bit):
        size = lax.axis_size(axis)
        return lax.ppermute(value, axis, [(i, i ^ bit) for i in range(size)])

    def mirrored(self, value):
        total = self.plan.s * self.plan.ch
        return lax.ppermute(value, ("slab", "chan"), [(i, total - 1 - i) for i in range(total)])

    def chosen_half(self, kernel, name, grid, in_specs, out_specs, out_shape, scratch, arrays):
        place = jnp.stack([self.slab, self.chan // (self.plan.ch // 2)]).astype(jnp.int32)
        return pl.pallas_call(
            kernel,
            grid_spec=pltpu.PrefetchScalarGridSpec(
                num_scalar_prefetch=1, grid=grid, in_specs=in_specs, out_specs=out_specs, scratch_shapes=scratch
            ),
            out_shape=out_shape,
            name=name,
            compiler_params=pltpu.CompilerParams(vmem_limit_bytes=VMEM_LIMIT, dimension_semantics=("arbitrary",)),
            cost_estimate=pl.CostEstimate(flops=10**9, bytes_accessed=4 * 10**6, transcendentals=0),
        )(place, *arrays)

    def sent_half(self, keep, arrived):
        block = (1, 1) + keep.shape[2:]
        spec = pl.BlockSpec(block, lambda r, place: (1 - place[1], r, 0, 0))
        return self.chosen_half(
            send_kernel, "send", (2,), [spec, spec], pl.BlockSpec(block, lambda r, place: (0, r, 0, 0)),
            shaped(1, *keep.shape[1:]), [], (keep, arrived),
        )

    def halve(self, keep, arrived, bit):
        mine = ((self.chan // bit) % 2).astype(jnp.int32).reshape(1)
        half = (keep.shape[0] // 2,) + keep.shape[1:]
        return call(
            halve_kernel, "halve", 1, [scalar(), whole(keep), whole(keep)], [whole_shape(half)] * 2,
            [shaped(*half)] * 2, [], 2,
        )(mine, keep, arrived)

    def sums_over_chan(self, keep, arrived, before):
        bit = 2
        while 2 * bit < self.plan.ch:
            keep, sent = self.halve(keep, arrived, bit)
            arrived = self.across(sent, "chan", bit)
            bit *= 2
        sent = tie(self.sent_half(keep, arrived), *before)
        return (keep, arrived), sent, self.across(sent, "chan", bit)

    def cut(self, kept, came):
        plan = self.plan
        size = (came.shape[2], plan.ll)
        block = (1,) + came.shape[1:]
        spec = pl.BlockSpec(block, lambda i, place: (place[1], 0, 0, 0))
        mine, *pieces = self.chosen_half(
            partial(cut_kernel, plan), "cut", (1,), [spec, spec, pl.BlockSpec(block, lambda i, place: (0, 0, 0, 0))],
            [pl.BlockSpec(size, lambda i, place: (0, 0))] * plan.s, [shaped(*size)] * plan.s,
            [pltpu.VMEM((plan.s, *size), f32)], (*kept, came),
        )
        return mine, pieces

    def join(self, mine, arrived):
        plan = self.plan
        total = (1, 2, mine.shape[0], plan.lp)
        return call(
            partial(join_kernel, plan), "join", 1, [scalar()] + [whole(mine)] * plan.s,
            whole_shape(total), shaped(*total), [pltpu.VMEM((plan.s, *mine.shape), f32)], 2,
        )(self.slab_index, mine, *arrived)

    def exchange(self, keeps, sends, linear, mix, outer=None):
        plan = self.plan
        first = [self.across(send, "chan", 1) for send in sends]
        keep0, sent0, came0 = self.sums_over_chan(keeps[0], first[0], [])
        extra = linear([sent0, first[1]])
        came0 = tie(came0, extra)
        keep1, sent1, came1 = self.sums_over_chan(keeps[1], first[1], [came0])

        mine, pieces = self.cut(keep0, came0)
        for j, piece in enumerate(pieces):
            mine = mine + self.across(piece, "slab", j + 1)
        own0 = mine
        mirror0 = self.mirrored(own0)
        mine, pieces = self.cut(keep1, tie(came1, own0))
        arrived = [self.across(piece, "slab", j + 1) for j, piece in enumerate(pieces)]
        out0, back0 = mix(0, [mine], own0, mirror0)
        for piece in [tie(arrived[0], out0)] + arrived[1:]:
            mine = mine + piece
        own1 = mine
        mirror1 = self.mirrored(own1)

        full0 = out0 + self.mirrored(back0)
        arrived = [self.across(full0, "slab", j) for j in range(1, plan.s)]
        out1, back1 = mix(1, [full0], own1, mirror1)
        full1 = out1 + self.mirrored(back1)
        total0 = self.join(full0, [tie(arrived[0], back1)] + arrived[1:])
        came0 = self.across(total0, "chan", plan.ch // 2)
        full1 = tie(full1, total0)
        arrived = [self.across(full1, "slab", j) for j in range(1, plan.s)]
        made = None
        if outer is not None:
            made = outer([total0], ((own0, mirror0), (own1, mirror1)))
            came0 = tie(came0, made)
        total1 = tie(self.join(full1, arrived), came0)
        came1 = self.across(total1, "chan", plan.ch // 2)
        if outer is not None:
            made = tie(jnp.transpose(made, (0, 3, 2, 1, 4)), total1)
            came1 = tie(came1, made)

        owns, others = [], []
        for total, other in ((total0, came0), (total1, came1)):
            bit = plan.ch // 2
            while bit > 1:
                upper = (self.chan // bit) % 2 == 1
                total = jnp.stack([jnp.where(upper, other, total), jnp.where(upper, total, other)], axis=1)
                total = total.reshape((-1,) + total.shape[2:])
                bit //= 2
                other = self.across(total, "chan", bit)
            owns.append(total)
            others.append(other)
        return owns, others, extra, made, ((own0, mirror0), (own1, mirror1))


def local(inputs, cotangent, spectral, local_weight, bias_vector):
    nx, ny, channels, nz = inputs.shape
    wb, wk = spectral.shape[0], spectral.shape[1]
    plan = Plan(nx, ny, nz, channels, wb, wk, spectral.shape[4] // channels, lax.axis_size("slab"), lax.axis_size("chan"))
    program = Program(plan)
    values = jnp.transpose(inputs, (0, 2, 1, 3))
    slopes = jnp.transpose(cotangent, (0, 2, 1, 3))
    weights = jnp.transpose(spectral, (0, 2, 3, 1, 4))

    keeps, sends = program.analyse(values)
    owns, others, linear, _, modes = program.exchange(
        keeps, sends,
        lambda before: program.linear(before, values, local_weight.T, bias_vector),
        lambda m, before, own, mirror: program.mix(mix_kernel, "mix", m, before, own, mirror, weights),
    )
    output, gradient, keeps, sends = program.middle(owns, others, linear, slopes)
    owns, others, linear, grad_spectral, _ = program.exchange(
        keeps, sends,
        lambda before: program.linear(before, gradient, local_weight, jnp.zeros_like(bias_vector)),
        lambda m, before, own, mirror: program.mix(mix_back_kernel, "mix_back", m, before, own, mirror, weights),
        lambda before, grads: program.outer(before, modes, grads, weights),
    )
    grad_inputs = program.synthesise([], owns, others, linear)
    return (
        jnp.transpose(output, (0, 2, 1, 3)),
        jnp.transpose(grad_inputs, (0, 2, 1, 3)),
        jnp.transpose(grad_spectral, (0, 1, 3, 2, 4)),
    )


def solution(mesh):
    in_specs = (
        P(("groups", "slab"), "chan", None, None),
        P(("groups", "slab"), "chan", None, None),
        P("slab", "chan", None, None, None),
        P(),
        P(),
    )
    out_specs = (
        P(("groups", "slab"), "chan", None, None),
        P(("groups", "slab"), "chan", None, None),
        P(("groups", "slab"), "chan", None, None, None),
    )
    return jax.shard_map(local, mesh=mesh, in_specs=in_specs, out_specs=out_specs, check_vma=False)
```

```python
from functools import partial
import math

import jax
import jax.numpy as jnp
import ml_dtypes
import numpy as np
from jax import lax
from jax.experimental import pallas as pl
from jax.experimental.pallas import tpu as pltpu
from jax.sharding import PartitionSpec as P

f32 = jnp.float32
bf16 = jnp.bfloat16
root_half = 0.7071067811865476
inv_root_two_pi = 0.3989422804014327
VMEM_LIMIT = 64 * 1024 * 1024
NT = (((1,), (1,)), ((), ()))
TN = (((0,), (0,)), ((), ()))


def round_up(value, unit):
    return -(-value // unit) * unit


class Plan:
    def __init__(self, nx, ny, nz, channels, wb, wk, mx, slab_count, chan_count):
        self.nx, self.ny, self.nz, self.c = nx, ny, nz, channels
        self.wb, self.wk, self.mx = wb, wk, mx
        self.s, self.ch = slab_count, chan_count
        self.half = chan_count // 2
        self.na = mx // 2 + 1
        self.span = (wb + 1) * self.na
        self.lw = slab_count * self.span
        self.lp = round_up(self.lw, 128)
        self.ll = round_up(2 * self.span, 128)
        self.mk = self.half * wk
        self.rc = round_up(2 * self.mk + 2 * self.half, 8)
        self.chunks = 2
        self.cc = channels
        self.w = (wk // 2, wk - wk // 2)
        self.rts = (round_up(channels * self.w[0], 8), round_up(channels * (self.w[1] + 1), 8))
        self.xb = math.gcd(8, nx)
        self.blk = self.xb * ny
        self.rows = self.cc * wk
        self.tall = round_up(self.rows, 16)
        self.bb = math.gcd(2, wb)
        self.lb = math.gcd(4, nx // 2)
        self.batch = max(d for d in range(1, 6) if self.cc % d == 0)
        self.full_x, self.full_y = nx * slab_count, ny * chan_count

    def segments(self, c):
        w0, w1 = self.w
        main = lambda first: lambda h, kind: kind * self.mk + h * self.wk + first
        return (
            (0, c * w0, w0, main(0)),
            (1, c * w1, w1, main(w0)),
            (1, self.c * w1 + c, 1, lambda h, kind: 2 * self.mk + kind * self.half + h),
        )

    def starts(self):
        kept = self.wb * self.s
        return [g * self.wb - (kept if 2 * g >= self.s else 0) for g in range(self.s)]

    def columns(self):
        b = np.concatenate([np.repeat(np.arange(st, st + self.wb + 1), self.na) for st in self.starts()])
        a = np.tile(np.arange(self.na), self.s * (self.wb + 1))
        return a, b

    def plane_table(self):
        a, b = self.columns()
        x = np.repeat(np.arange(self.nx), self.ny)[:, None]
        y = np.tile(np.arange(self.ny), self.nx)[:, None]
        total = self.full_x * self.full_y
        phase = (a * x * self.full_y + b * y * self.full_x) % total * (2.0 * np.pi / total)
        table = np.zeros((self.nx * self.ny, 2 * self.lp))
        scale = 1.0 / math.sqrt(total)
        table[:, : self.lw] = np.cos(phase) * scale
        table[:, self.lp : self.lp + self.lw] = -np.sin(phase) * scale
        high, low = (t.reshape(self.nx // self.xb, 1, self.blk, 2 * self.lp) for t in halves(table))
        return np.concatenate([high, high, low], 1).reshape(-1, 3 * self.blk, 2 * self.lp)

    def turns(self):
        a, b = self.columns()
        x = (np.arange(self.s) * self.nx)[:, None, None]
        y = (np.arange(self.ch) * self.ny)[None, :, None]
        total = self.full_x * self.full_y
        phase = (a * x * self.full_y + b * y * self.full_x) % total * (2.0 * np.pi / total)
        table = np.zeros((self.s, self.ch, 2, self.lp), np.float32)
        table[:, :, 0, : self.lw] = np.cos(phase)
        table[:, :, 1, : self.lw] = np.sin(phase)
        return table

    def depth_rows(self):
        main = np.arange(self.mk)
        edge = (np.arange(self.half) + 1) * self.wk
        z = np.arange(self.nz)
        scale = 1.0 / math.sqrt(self.nz)
        angle = lambda k: (k[:, None] * z) % self.nz * (2.0 * np.pi / self.nz)
        rows = [np.cos(angle(main)), np.sin(angle(main)), np.cos(angle(edge)), np.sin(angle(edge))]
        table = np.zeros((self.rc, self.nz))
        table[: 2 * self.mk + 2 * self.half] = np.concatenate(rows) * scale
        return halves(table)

    def depth_forward(self):
        high, low = self.depth_rows()
        return np.concatenate(
            [np.concatenate([high, high], 1), np.concatenate([low, np.zeros_like(low)], 1)], 0
        )

    def depth_inverse(self):
        high, low = self.depth_rows()
        table = np.zeros((round_up(3 * self.rc, 16), self.nz), ml_dtypes.bfloat16)
        table[: 3 * self.rc] = np.concatenate([high, high, low], 0)
        return table

    def selections(self):
        quarters = 128 // self.mx
        own = np.zeros((self.wb, 2, self.ll, 2, quarters, self.mx), np.float32)
        for b in range(self.wb):
            for r in range(2):
                for a in range(self.mx):
                    if a < self.mx // 2:
                        own[b, 0, r * self.span + b * self.na + a, r, :, a] = 1.0
                    else:
                        spot = r * self.span + (self.wb - b) * self.na + self.mx - a
                        own[b, 1, spot, r, :, a] = 1.0 - 2.0 * r
        own = own.reshape(self.wb, 2 * self.ll, 256)
        back = np.swapaxes(own, 1, 2)
        return own.astype(ml_dtypes.bfloat16), np.ascontiguousarray(back).astype(ml_dtypes.bfloat16)

    def orders(self, chunk):
        w0, w1 = self.w
        table = np.zeros((2, self.rows, self.rts[chunk]), np.float32)
        for c in range(self.c):
            for k in range(self.wk):
                for upper, index in enumerate((k, self.wk - k)):
                    if index < w0:
                        here, spot = 0, c * w0 + index
                    elif index < self.wk:
                        here, spot = 1, c * w1 + index - w0
                    else:
                        here, spot = 1, self.c * w1 + c
                    if here == chunk:
                        table[upper, c * self.wk + k, spot] = 1.0
        return table.astype(ml_dtypes.bfloat16)


def halves(table):
    high = table.astype(np.float32).astype(ml_dtypes.bfloat16)
    low = (table - high.astype(np.float64)).astype(np.float32).astype(ml_dtypes.bfloat16)
    return high, low


def dot(left, right, numbers=(((1,), (0,)), ((), ()))):
    return lax.dot_general(left, right, numbers, preferred_element_type=f32)


def split(value):
    high = value.astype(bf16)
    return high, (value - high.astype(f32)).astype(bf16)


def moved(value, chosen, left=False):
    first, second = split(value)
    if left:
        return dot(chosen, first) + dot(chosen, second)
    rows = value.shape[0]
    if rows % 16:
        return dot(first, chosen) + dot(second, chosen)
    both = dot(jnp.concatenate([first, second], axis=0), chosen)
    return both[:rows] + both[rows:]


def depth_analysis(plan, table_ref, values):
    rows = []
    for value in values:
        high, low = split(value)
        rows.append(jnp.concatenate([high, low], axis=1))
    both = dot(table_ref[...], jnp.concatenate(rows, axis=0), NT)
    lines = both[: plan.rc] + both[plan.rc :]
    return [lines[:, j * plan.blk : (j + 1) * plan.blk] for j in range(len(values))]


def depth_synthesis(plan, table_ref, rows):
    high = rows.astype(bf16).astype(f32)
    parts = [high, rows - high, high]
    extra = table_ref.shape[0] - 3 * plan.rc
    if extra:
        parts.append(jnp.zeros((extra, rows.shape[1]), f32))
    return dot(jnp.concatenate(parts, axis=0).astype(bf16), table_ref[...], TN)


def plane_analysis(plan, step, lines_ref, plane_ref, total_ref):
    high, low = split(lines_ref[...].reshape(plan.cc * plan.rc, plan.blk))
    rows = jnp.concatenate([high, low, high], axis=1)
    for start in range(0, 2 * plan.lp, 256):
        size = min(256, 2 * plan.lp - start)
        columns = pl.ds(start, size)
        part = dot(rows, plane_ref[0, :, columns]).reshape(plan.cc, plan.rc, size)

        @pl.when(step == 0)
        def _():
            total_ref[:, :, columns] = part

        @pl.when(step > 0)
        def _():
            total_ref[:, :, columns] += part


def plane_synthesis(plan, high_rows, low_rows, plane_ref, lines_ref):
    high_table, low_table = plane_ref[0, : plan.blk], plane_ref[0, 2 * plan.blk :]
    lines = (
        dot(high_rows[...], high_table, NT)
        + dot(low_rows[...], high_table, NT)
        + dot(high_rows[...], low_table, NT)
    )
    lines_ref[...] = lines.reshape(plan.cc, plan.rc, plan.blk)


def emit_modes(plan, flag_ref, turn_ref, total_ref, keep_refs, send_refs):
    lp, half = plan.lp, plan.half
    odd = flag_ref[0] == 1
    cosine, sine = turn_ref[0:1, :], turn_ref[1:2, :]
    for c in range(plan.c):
        real, imag = total_ref[c, :, :lp], total_ref[c, :, lp:]
        real, imag = real * cosine + imag * sine, imag * cosine - real * sine
        for m, base, size, place in plan.segments(c):
            made = []
            for g in range(plan.ch):
                h = g if g < half else plan.ch - 1 - g
                even, odd_rows = (slice(place(h, kind), place(h, kind) + size) for kind in (0, 1))
                if g < half:
                    made.append((real[even] + imag[odd_rows], imag[even] - real[odd_rows]))
                else:
                    made.append((real[even] - imag[odd_rows], imag[even] + real[odd_rows]))
            for pair in range(half):
                for r in range(2):
                    low, high = made[2 * pair][r], made[2 * pair + 1][r]
                    keep_refs[m][pair, r, base : base + size, :] = jnp.where(odd, high, low)
                    send_refs[m][pair, r, base : base + size, :] = jnp.where(odd, low, high)
    for m, used in enumerate((plan.c * plan.w[0], plan.c * (plan.w[1] + 1))):
        if used < plan.rts[m]:
            blank = jnp.zeros((half, 2, plan.rts[m] - used, lp), f32)
            keep_refs[m][:, :, used:, :] = blank
            send_refs[m][:, :, used:, :] = blank


def take_modes(plan, flag_ref, turn_ref, own_refs, other_refs, total_ref, high_rows, low_rows):
    lp, half = plan.lp, plan.half
    odd = flag_ref[0] == 1
    cosine, sine = turn_ref[0:1, :], turn_ref[1:2, :]

    def group(m, g, r, rows):
        own, other = own_refs[m][g // 2, r, rows, :], other_refs[m][g // 2, r, rows, :]
        return jnp.where(odd, own, other) if g % 2 else jnp.where(odd, other, own)

    for c in range(plan.c):
        for m, base, size, place in plan.segments(c):
            rows = slice(base, base + size)
            for h in range(half):
                plus = [group(m, h, r, rows) for r in range(2)]
                minus = [group(m, plan.ch - 1 - h, r, rows) for r in range(2)]
                real, imag = plus[0] + minus[0], plus[1] + minus[1]
                here = slice(place(h, 0), place(h, 0) + size)
                total_ref[c, here, :lp] = real * cosine - imag * sine
                total_ref[c, here, lp:] = imag * cosine + real * sine
                real, imag = plus[0] - minus[0], plus[1] - minus[1]
                here = slice(place(h, 1), place(h, 1) + size)
                total_ref[c, here, :lp] = -(imag * cosine + real * sine)
                total_ref[c, here, lp:] = real * cosine - imag * sine
        used = 2 * plan.mk + 2 * half
        if used < plan.rc:
            total_ref[c, used:, :] = jnp.zeros((plan.rc - used, 2 * lp), f32)
    high, low = split(total_ref[...].reshape(plan.c * plan.rc, 2 * lp))
    high_rows[...] = high
    low_rows[...] = low


def analyse_kernel(plan, flag_ref, values_ref, plane_ref, depth_ref, turn_ref, *refs):
    keep_refs, send_refs, (lines_ref, total_ref) = refs[:2], refs[2:4], refs[4:]
    step = pl.program_id(0)

    @pl.loop(0, plan.cc, step=plan.batch)
    def _(c):
        values = [values_ref[:, c + j].reshape(plan.blk, plan.nz) for j in range(plan.batch)]
        for j, lines in enumerate(depth_analysis(plan, depth_ref, values)):
            lines_ref[c + j] = lines

    plane_analysis(plan, step, lines_ref, plane_ref, total_ref)

    @pl.when(step == pl.num_programs(0) - 1)
    def _():
        emit_modes(plan, flag_ref, turn_ref, total_ref, keep_refs, send_refs)


def fields(plan, inverse_ref, lines_ref, first):
    lines = jnp.concatenate([lines_ref[first + j] for j in range(plan.batch)], axis=1)
    values = depth_synthesis(plan, inverse_ref, lines)
    return [values[j * plan.blk : (j + 1) * plan.blk] for j in range(plan.batch)]


def middle_kernel(plan, flag_ref, *refs):
    own_refs, other_refs, refs = refs[:2], refs[2:4], refs[4:]
    linear_ref, cotangent_ref, plane_ref, depth_ref, inverse_ref, turn_ref, output_ref, gradient_ref = refs[:8]
    keep_refs, send_refs, (lines_ref, back_ref, total_ref, high_rows, low_rows) = refs[8:10], refs[10:12], refs[12:]
    step = pl.program_id(0)

    @pl.when(step == 0)
    def _():
        take_modes(plan, flag_ref, turn_ref, own_refs, other_refs, total_ref, high_rows, low_rows)

    plane_synthesis(plan, high_rows, low_rows, plane_ref, lines_ref)
    shape = (plan.xb, plan.ny, plan.nz)

    @pl.loop(0, plan.cc, step=plan.batch)
    def _(first):
        gradients = []
        for j, field in enumerate(fields(plan, inverse_ref, lines_ref, first)):
            value = field + linear_ref[:, first + j].reshape(plan.blk, plan.nz)
            gate = 0.5 * (1.0 + lax.erf(value * root_half))
            slope = gate + value * jnp.exp(-0.5 * value * value) * inv_root_two_pi
            output_ref[:, first + j] = (value * gate).reshape(shape)
            gradients.append(cotangent_ref[:, first + j].reshape(plan.blk, plan.nz) * slope)
            gradient_ref[:, first + j] = gradients[-1].reshape(shape)
        for j, lines in enumerate(depth_analysis(plan, depth_ref, gradients)):
            back_ref[first + j] = lines

    plane_analysis(plan, step, back_ref, plane_ref, total_ref)

    @pl.when(step == pl.num_programs(0) - 1)
    def _():
        emit_modes(plan, flag_ref, turn_ref, total_ref, keep_refs, send_refs)


def synthesise_kernel(plan, flag_ref, *refs):
    own_refs, other_refs, refs = refs[:2], refs[2:4], refs[4:]
    linear_ref, plane_ref, inverse_ref, turn_ref, output_ref, lines_ref, total_ref, high_rows, low_rows = refs

    @pl.when(pl.program_id(0) == 0)
    def _():
        take_modes(plan, flag_ref, turn_ref, own_refs, other_refs, total_ref, high_rows, low_rows)

    plane_synthesis(plan, high_rows, low_rows, plane_ref, lines_ref)

    @pl.loop(0, plan.cc, step=plan.batch)
    def _(first):
        for j, field in enumerate(fields(plan, inverse_ref, lines_ref, first)):
            value = field + linear_ref[:, first + j].reshape(plan.blk, plan.nz)
            output_ref[:, first + j] = value.reshape(plan.xb, plan.ny, plan.nz)


def linear_kernel(plan, values_ref, weight_ref, bias_ref, output_ref):
    tiles = [(x, slice(t * 8, (t + 1) * 8)) for x in range(plan.lb) for t in range(plan.ny // 8)]
    values = [values_ref[x, :, t, :].reshape(plan.c * 8, plan.nz) for x, t in tiles]
    high, low = split(jnp.concatenate(values, axis=1))
    size = 8 * plan.c
    row, column = (lax.broadcasted_iota(jnp.int32, (size, plan.c), n) for n in (0, 1))
    repeat = (row // 8 == column).astype(f32)
    exact = partial(lax.dot_general, precision=lax.Precision.HIGHEST, preferred_element_type=f32)
    spread = exact(exact(repeat, weight_ref[...], (((1,), (0,)), ((), ()))), repeat, NT)
    row, column = (lax.broadcasted_iota(jnp.int32, (size, size), n) for n in (0, 1))
    high_matrix, low_matrix = split(jnp.where(row % 8 == column % 8, spread, 0.0))
    bias = exact(repeat, bias_ref[...], (((1,), (1,)), ((), ())))
    matrix = jnp.concatenate([high_matrix, high_matrix, low_matrix], axis=1)
    mixed = dot(matrix, jnp.concatenate([high, low, high], axis=0)) + bias
    for n, (x, t) in enumerate(tiles):
        output_ref[x, :, t, :] = mixed[:, n * plan.nz : (n + 1) * plan.nz].reshape(plan.c, 8, plan.nz)


def pick(plan, upper_ref, parts, chosen_ref, ordered_ref):
    @pl.when(pl.program_id(0) == 0)
    def _():
        for n in range(2):
            found = [moved(part[n][...], part[2][upper_ref[0]], left=True) for part in parts]
            high, low = split(sum(found[1:], found[0]))
            ordered_ref[: plan.rows, n * plan.ll : (n + 1) * plan.ll] = high
            ordered_ref[plan.tall : plan.tall + plan.rows, n * plan.ll : (n + 1) * plan.ll] = low

    both = [dot(ordered_ref[...], chosen_ref[n]) for n in range(plan.bb)]
    return [b[: plan.rows] + b[plan.tall : plan.tall + plan.rows] for b in both]


def give(plan, upper_ref, made_ref, order_ref, back_ref, own_ref, mirror_ref, sums_ref):
    part = moved(made_ref[0], back_ref[0])
    for n in range(1, plan.bb):
        part = part + moved(made_ref[n], back_ref[n])
    step = pl.program_id(0)

    @pl.when(step == 0)
    def _():
        sums_ref[...] = part

    @pl.when(step > 0)
    def _():
        sums_ref[...] += part

    @pl.when(step == pl.num_programs(0) - 1)
    def _():
        own_ref[...] = moved(sums_ref[:, : plan.ll], order_ref[upper_ref[0]], left=True)
        mirror_ref[...] = moved(sums_ref[:, plan.ll :], order_ref[upper_ref[0]], left=True)


def mix_kernel(
    plan, upper_ref, own_ref, mirror_ref, order_ref, disorder_ref, chosen_ref, back_ref, weight_ref,
    own_out, mirror_out, ordered_ref, made_ref, sums_ref,
):
    wk, quarters = plan.wk, 128 // plan.mx
    picked = pick(plan, upper_ref, [(own_ref, mirror_ref, order_ref)], chosen_ref, ordered_ref)
    place = lax.broadcasted_iota(jnp.int32, (wk, 128), 1) // plan.mx
    for n, modes in enumerate(picked):
        for t in range(plan.c // quarters):
            columns = slice(t * 128, (t + 1) * 128)
            real = imag = 0.0
            for i in range(plan.c):
                x_real, x_imag = modes[i * wk : (i + 1) * wk, :128], modes[i * wk : (i + 1) * wk, 128:]
                w_real, w_imag = weight_ref[n, 0, i, :, columns], weight_ref[n, 1, i, :, columns]
                real = real + (w_real * x_real - w_imag * x_imag)
                imag = imag + (w_real * x_imag + w_imag * x_real)
            for q in range(quarters):
                o = t * quarters + q
                made_ref[n, o * wk : (o + 1) * wk, :128] = jnp.where(place == q, real, 0.0)
                made_ref[n, o * wk : (o + 1) * wk, 128:] = jnp.where(place == q, imag, 0.0)
    give(plan, upper_ref, made_ref, disorder_ref, back_ref, own_out, mirror_out, sums_ref)


def along(plan, modes):
    wk, quarters = plan.wk, 128 // plan.mx
    place = lax.broadcasted_iota(jnp.int32, (wk, 128), 1) // plan.mx
    lined = []
    for t in range(plan.c // quarters):
        real = imag = 0.0
        for q in range(quarters):
            o = t * quarters + q
            real = jnp.where(place == q, modes[o * wk : (o + 1) * wk, :128], real)
            imag = jnp.where(place == q, modes[o * wk : (o + 1) * wk, 128:], imag)
        lined.append((slice(t * 128, (t + 1) * 128), real, imag))
    return lined


def mix_back_kernel(
    plan, upper_ref, own_ref, mirror_ref, order_ref, disorder_ref, chosen_ref, back_ref, weight_ref,
    own_out, mirror_out, ordered_ref, made_ref, sums_ref,
):
    wk = plan.wk
    for n, grads in enumerate(pick(plan, upper_ref, [(own_ref, mirror_ref, order_ref)], chosen_ref, ordered_ref)):
        lined = along(plan, grads)
        for i in range(plan.c):
            back_real = back_imag = 0.0
            for columns, real, imag in lined:
                w_real, w_imag = weight_ref[n, 0, i, :, columns], weight_ref[n, 1, i, :, columns]
                back_real = back_real + (w_real * real + w_imag * imag)
                back_imag = back_imag + (w_real * imag - w_imag * real)
            made_ref[n, i * wk : (i + 1) * wk, :128] = back_real
            made_ref[n, i * wk : (i + 1) * wk, 128:] = back_imag
    give(plan, upper_ref, made_ref, disorder_ref, back_ref, own_out, mirror_out, sums_ref)


def outer_kernel(plan, upper_ref, *refs):
    parts = [refs[:8][2 * m : 2 * m + 2] for m in range(4)]
    orders, chosen_ref, gradient_ref, mode_rows, grad_rows = refs[8:10], refs[10], refs[11], refs[12], refs[13]
    wk = plan.wk
    modes = pick(plan, upper_ref, [(*parts[m], orders[m]) for m in range(2)], chosen_ref, mode_rows)
    grads = pick(plan, upper_ref, [(*parts[2 + m], orders[m]) for m in range(2)], chosen_ref, grad_rows)
    for n in range(plan.bb):
        lined = along(plan, grads[n])
        for i in range(plan.c):
            rows = slice(i * wk, (i + 1) * wk)
            x_real, x_imag = modes[n][rows, :128], modes[n][rows, 128:]
            for columns, real, imag in lined:
                gradient_ref[n, 0, i, :, columns] = real * x_real + imag * x_imag
                gradient_ref[n, 1, i, :, columns] = imag * x_real - real * x_imag


def halve_kernel(flag_ref, keep_ref, arrived_ref, kept_ref, send_ref):
    odd = flag_ref[0] == 1
    for pair in range(kept_ref.shape[0]):
        low = keep_ref[2 * pair] + arrived_ref[2 * pair]
        high = keep_ref[2 * pair + 1] + arrived_ref[2 * pair + 1]
        kept_ref[pair] = jnp.where(odd, high, low)
        send_ref[pair] = jnp.where(odd, low, high)


def cut_kernel(plan, place_ref, keep_ref, arrived_ref, came_ref, *refs):
    out_refs, held_ref = refs[:-1], refs[-1]
    lane = lax.broadcasted_iota(jnp.int32, held_ref.shape[1:], 1)
    real = keep_ref[0, 0] + arrived_ref[0, 0] + came_ref[0, 0]
    imag = keep_ref[0, 1] + arrived_ref[0, 1] + came_ref[0, 1]
    for g in range(plan.s):
        first = pltpu.roll(real, (plan.lp - g * plan.span) % plan.lp, 1)[:, : plan.ll]
        second = pltpu.roll(imag, (plan.lp - g * plan.span + plan.span) % plan.lp, 1)[:, : plan.ll]
        held_ref[g] = jnp.where(lane < plan.span, first, jnp.where(lane < 2 * plan.span, second, 0.0))
    for j, out_ref in enumerate(out_refs):
        out_ref[...] = held_ref[place_ref[0] ^ j]


def join_kernel(plan, slab_ref, *refs):
    piece_refs, total_ref, held_ref = refs[:-2], refs[-2], refs[-1]
    for j, piece_ref in enumerate(piece_refs):
        held_ref[j] = piece_ref[...]
    rows = held_ref.shape[1]
    lane = lax.broadcasted_iota(jnp.int32, (rows, plan.lp), 1)
    real = imag = jnp.zeros((rows, plan.lp), f32)
    blank = jnp.zeros((rows, plan.lp - plan.ll), f32)
    for g in range(plan.s):
        piece = jnp.concatenate([held_ref[slab_ref[0] ^ g], blank], axis=1)
        here = (lane >= g * plan.span) & (lane < (g + 1) * plan.span)
        real = jnp.where(here, pltpu.roll(piece, g * plan.span, 1), real)
        imag = jnp.where(here, pltpu.roll(piece, (g * plan.span - plan.span) % plan.lp, 1), imag)
    total_ref[0, 0] = real
    total_ref[0, 1] = imag


def whole(array):
    zeros = (0,) * array.ndim
    return pl.BlockSpec(array.shape, lambda i: zeros, pipeline_mode=pl.Buffered(1))


def whole_shape(shape):
    zeros = (0,) * len(shape)
    return pl.BlockSpec(shape, lambda i: zeros, pipeline_mode=pl.Buffered(1))


def leading(shape):
    rest = (0,) * (len(shape) - 1)
    return pl.BlockSpec(shape, lambda i: (i,) + rest)


def shaped(*shape):
    return jax.ShapeDtypeStruct(shape, f32)


def anywhere():
    return pl.BlockSpec(memory_space=pl.ANY)


def scalar():
    return pl.BlockSpec(memory_space=pltpu.SMEM)


def call(kernel, name, grid, in_specs, out_specs, out_shape, scratch, cost, before=(), aliases=None):
    skipped = len(before)
    run = pl.pallas_call(
        lambda *refs: kernel(*refs[skipped:]),
        grid=(grid,),
        in_specs=[anywhere()] * skipped + list(in_specs),
        out_specs=out_specs,
        out_shape=out_shape,
        scratch_shapes=scratch,
        name=name,
        input_output_aliases=aliases or {},
        compiler_params=pltpu.CompilerParams(vmem_limit_bytes=VMEM_LIMIT, dimension_semantics=("arbitrary",)),
        cost_estimate=pl.CostEstimate(flops=int(cost * 1.15e9), bytes_accessed=int(cost * 3.6e6), transcendentals=0),
    )
    return partial(run, *before)


def tie(value, *before):
    if not before:
        return value
    return pl.pallas_call(
        lambda *refs: None,
        in_specs=[anywhere()] * (1 + len(before)),
        out_specs=anywhere(),
        out_shape=jax.ShapeDtypeStruct(value.shape, value.dtype),
        input_output_aliases={0: 0},
        name="tie",
    )(value, *before)


class Program:
    def __init__(self, plan):
        self.plan = plan
        self.plane = jnp.asarray(plan.plane_table())
        self.depth = jnp.asarray(plan.depth_forward())
        self.inverse = jnp.asarray(plan.depth_inverse())
        slab, chan = lax.axis_index("slab"), lax.axis_index("chan")
        self.slab, self.chan = slab, chan
        turns = jnp.asarray(plan.turns())
        self.turn = lax.dynamic_index_in_dim(
            lax.dynamic_index_in_dim(turns, slab, 0, False), chan, 0, False
        )
        self.slab_index = slab.astype(jnp.int32).reshape(1)
        self.flag = (chan % 2).astype(jnp.int32).reshape(1)
        self.upper = (chan >= plan.half).astype(jnp.int32).reshape(1)
        tables = [plan.orders(m) for m in range(plan.chunks)]
        self.order = [jnp.asarray(t) for t in tables]
        self.disorder = [jnp.asarray(np.ascontiguousarray(np.swapaxes(t, 1, 2))) for t in tables]
        chosen, back = plan.selections()
        self.chosen, self.back = jnp.asarray(chosen), jnp.asarray(back)

    def half_shapes(self):
        plan = self.plan
        return [(plan.half, 2, rt, plan.lp) for rt in plan.rts]

    def field_spec(self):
        plan = self.plan
        return leading((plan.xb, plan.c, plan.ny, plan.nz))

    def table(self):
        plan = self.plan
        return leading((1, 3 * plan.blk, 2 * plan.lp))

    def lines(self):
        plan = self.plan
        return pltpu.VMEM((plan.cc, plan.rc, plan.blk), f32)

    def spectra(self):
        plan = self.plan
        rows = pltpu.VMEM((plan.cc * plan.rc, 2 * plan.lp), bf16)
        return [pltpu.VMEM((plan.cc, plan.rc, 2 * plan.lp), f32), rows, rows]

    def analyse(self, values):
        plan = self.plan
        halves = self.half_shapes()
        made = call(
            partial(analyse_kernel, plan), "analyse", plan.nx // plan.xb,
            [scalar(), self.field_spec(), self.table(), whole(self.depth), whole(self.turn)],
            [whole_shape(h) for h in halves * 2], [shaped(*h) for h in halves * 2],
            [self.lines(), self.spectra()[0]], 26,
        )(self.flag, values, self.plane, self.depth, self.turn)
        return made[:2], made[2:]

    def middle(self, owns, others, linear, cotangent):
        plan = self.plan
        halves = self.half_shapes()
        field, spec = shaped(plan.nx, plan.c, plan.ny, plan.nz), self.field_spec()
        modes = [whole_shape(h) for h in halves * 2]
        output, gradient, *made = call(
            partial(middle_kernel, plan), "middle", plan.nx // plan.xb,
            [scalar(), *modes, spec, spec, self.table(), whole(self.depth), whole(self.inverse), whole(self.turn)],
            [spec, spec, *modes], [field, field, *[shaped(*h) for h in halves * 2]],
            [self.lines(), self.lines(), *self.spectra()], 47,
        )(self.flag, *owns, *others, linear, cotangent, self.plane, self.depth, self.inverse, self.turn)
        return output, gradient, made[:2], made[2:]

    def synthesise(self, before, owns, others, linear):
        plan = self.plan
        spec = self.field_spec()
        return call(
            partial(synthesise_kernel, plan), "synthesise", plan.nx // plan.xb,
            [scalar(), *[whole_shape(h) for h in self.half_shapes() * 2], spec, self.table(),
             whole(self.inverse), whole(self.turn)],
            spec, shaped(plan.nx, plan.c, plan.ny, plan.nz),
            [self.lines(), *self.spectra()], 20, before,
        )(self.flag, *owns, *others, linear, self.plane, self.inverse, self.turn)

    def linear(self, half, before, filled, values, matrix, bias):
        plan = self.plan
        bias = bias[None]
        steps = plan.nx // plan.lb // 2
        spec = pl.BlockSpec((plan.lb, plan.c, plan.ny, plan.nz), lambda i: (i + half * steps, 0, 0, 0))
        return call(
            partial(linear_kernel, plan), "linear", steps,
            [spec, whole(matrix), whole(bias)],
            spec, shaped(plan.nx, plan.c, plan.ny, plan.nz), [], 7, (*filled, *before), {0: 0} if filled else None,
        )(values, matrix, bias)

    def mix(self, kernel, name, chunk, before, own, mirror, weights):
        plan = self.plan
        modes = (plan.rts[chunk], plan.ll)
        order, disorder = self.order[chunk], self.disorder[chunk]
        ordered = pltpu.VMEM((2 * plan.tall, 2 * plan.ll), bf16)
        return call(
            partial(kernel, plan), name, plan.wb // plan.bb,
            [
                scalar(), whole_shape(modes), whole_shape(modes), whole(order), whole(disorder),
                leading((plan.bb,) + self.chosen.shape[1:]), leading((plan.bb,) + self.back.shape[1:]),
                leading((plan.bb, *weights.shape[1:])),
            ],
            [whole_shape(modes)] * 2, [shaped(*modes)] * 2,
            [ordered, pltpu.VMEM((plan.bb, plan.rows, 256), f32), pltpu.VMEM((plan.rows, 2 * plan.ll), f32)], 9, before,
        )(self.upper, own, mirror, order, disorder, self.chosen, self.back, weights)

    def outer(self, before, modes, grads, weights):
        plan = self.plan
        parts = [part for pair in (*modes, *grads) for part in pair]
        ordered = pltpu.VMEM((2 * plan.tall, 2 * plan.ll), bf16)
        out = leading((plan.bb, *weights.shape[1:]))
        return call(
            partial(outer_kernel, plan), "outer", plan.wb // plan.bb,
            [scalar(), *[whole(p) for p in parts], *[whole(o) for o in self.order], leading((plan.bb,) + self.chosen.shape[1:])],
            out, shaped(*weights.shape), [ordered, ordered], 9, before,
        )(self.upper, *parts, *self.order, self.chosen)

    def across(self, value, axis, bit):
        size = lax.axis_size(axis)
        return lax.ppermute(value, axis, [(i, i ^ bit) for i in range(size)])

    def mirrored(self, value):
        total = self.plan.s * self.plan.ch
        return lax.ppermute(value, ("slab", "chan"), [(i, total - 1 - i) for i in range(total)])

    def chosen_half(self, kernel, name, grid, in_specs, out_specs, out_shape, scratch, arrays):
        place = jnp.stack([self.slab, self.chan // (self.plan.ch // 2)]).astype(jnp.int32)
        return pl.pallas_call(
            kernel,
            grid_spec=pltpu.PrefetchScalarGridSpec(
                num_scalar_prefetch=1, grid=grid, in_specs=in_specs, out_specs=out_specs, scratch_shapes=scratch
            ),
            out_shape=out_shape,
            name=name,
            compiler_params=pltpu.CompilerParams(vmem_limit_bytes=VMEM_LIMIT, dimension_semantics=("arbitrary",)),
            cost_estimate=pl.CostEstimate(flops=10**9, bytes_accessed=4 * 10**6, transcendentals=0),
        )(place, *arrays)

    def sent_half(self, keep, arrived):
        other = 1 - self.chan // (self.plan.ch // 2)
        return lax.dynamic_index_in_dim(keep, other, 0) + lax.dynamic_index_in_dim(arrived, other, 0)

    def halve(self, keep, arrived, bit):
        mine = ((self.chan // bit) % 2).astype(jnp.int32).reshape(1)
        half = (keep.shape[0] // 2,) + keep.shape[1:]
        return call(
            halve_kernel, "halve", 1, [scalar(), whole(keep), whole(keep)], [whole_shape(half)] * 2,
            [shaped(*half)] * 2, [], 2,
        )(mine, keep, arrived)

    def sums_over_chan(self, keep, arrived, before):
        bit = 2
        while 2 * bit < self.plan.ch:
            keep, sent = self.halve(keep, arrived, bit)
            arrived = self.across(sent, "chan", bit)
            bit *= 2
        sent = tie(self.sent_half(keep, arrived), *before)
        return (keep, arrived), sent, self.across(sent, "chan", bit)

    def cut(self, kept, came):
        plan = self.plan
        size = (came.shape[2], plan.ll)
        block = (1,) + came.shape[1:]
        spec = pl.BlockSpec(block, lambda i, place: (place[1], 0, 0, 0))
        mine, *pieces = self.chosen_half(
            partial(cut_kernel, plan), "cut", (1,), [spec, spec, pl.BlockSpec(block, lambda i, place: (0, 0, 0, 0))],
            [pl.BlockSpec(size, lambda i, place: (0, 0))] * plan.s, [shaped(*size)] * plan.s,
            [pltpu.VMEM((plan.s, *size), f32)], (*kept, came),
        )
        return mine, pieces

    def join(self, mine, arrived):
        plan = self.plan
        total = (1, 2, mine.shape[0], plan.lp)
        return call(
            partial(join_kernel, plan), "join", 1, [scalar()] + [whole(mine)] * plan.s,
            whole_shape(total), shaped(*total), [pltpu.VMEM((plan.s, *mine.shape), f32)], 2,
        )(self.slab_index, mine, *arrived)

    def exchange(self, keeps, sends, mix, fillers):
        def fill(n, value, *before):
            return tie(value, fillers[n](before)) if fillers[n] else value

        plan = self.plan
        first = [self.across(send, "chan", 1) for send in sends]
        keep0, sent0, came0 = self.sums_over_chan(keeps[0], first[0], [])
        came0 = fill(0, came0, sent0, first[1])
        keep1, sent1, came1 = self.sums_over_chan(keeps[1], first[1], [came0])

        mine, pieces = self.cut(keep0, came0)
        arrived = [self.across(piece, "slab", j + 1) for j, piece in enumerate(pieces)]
        for piece in [fill(1, arrived[0], mine, sent1)] + arrived[1:]:
            mine = mine + piece
        own0 = mine
        mirror0 = self.mirrored(own0)
        mine, pieces = self.cut(keep1, tie(came1, own0))
        arrived = [self.across(piece, "slab", j + 1) for j, piece in enumerate(pieces)]
        out0, back0 = mix(0, [mine], own0, mirror0)
        for piece in [tie(arrived[0], out0)] + arrived[1:]:
            mine = mine + piece
        own1 = mine
        mirror1 = self.mirrored(own1)

        full0 = out0 + self.mirrored(back0)
        arrived = [self.across(full0, "slab", j) for j in range(1, plan.s)]
        out1, back1 = mix(1, [full0], own1, mirror1)
        full1 = out1 + self.mirrored(back1)
        total0 = self.join(full0, [tie(arrived[0], back1)] + arrived[1:])
        came0 = self.across(total0, "chan", plan.ch // 2)
        full1 = tie(full1, total0)
        arrived = [self.across(full1, "slab", j) for j in range(1, plan.s)]
        modes = ((own0, mirror0), (own1, mirror1))
        if fillers[2]:
            came0 = tie(came0, fillers[2]([total0], modes))
        total1 = tie(self.join(full1, arrived), came0)
        came1 = self.across(total1, "chan", plan.ch // 2)
        came1 = fill(3, came1, total1)

        owns, others = [], []
        for total, other in ((total0, came0), (total1, came1)):
            bit = plan.ch // 2
            while bit > 1:
                upper = (self.chan // bit) % 2 == 1
                total = jnp.stack([jnp.where(upper, other, total), jnp.where(upper, total, other)], axis=1)
                total = total.reshape((-1,) + total.shape[2:])
                bit //= 2
                other = self.across(total, "chan", bit)
            owns.append(total)
            others.append(other)
        return owns, others, modes


def local(inputs, cotangent, spectral, local_weight, bias_vector):
    nx, ny, channels, nz = inputs.shape
    wb, wk = spectral.shape[0], spectral.shape[1]
    plan = Plan(nx, ny, nz, channels, wb, wk, spectral.shape[4] // channels, lax.axis_size("slab"), lax.axis_size("chan"))
    program = Program(plan)
    values = jnp.transpose(inputs, (0, 2, 1, 3))
    slopes = jnp.transpose(cotangent, (0, 2, 1, 3))
    weights = jnp.transpose(spectral, (0, 2, 3, 1, 4))

    held = {}

    def relaid(before):
        held["weights"] = tie(weights, *before)
        return held["weights"]

    def linear(half, name, values, matrix, bias):
        def run(before):
            filled = [held[name]] if half else []
            held[name] = program.linear(half, before, filled, values, matrix, bias)
            return held[name]

        return run

    def mix(kernel, name):
        return lambda m, before, own, mirror: program.mix(kernel, name, m, before, own, mirror, held["weights"])

    keeps, sends = program.analyse(values)
    there = [linear(half, "linear", values, local_weight.T, bias_vector) for half in range(2)]
    owns, others, modes = program.exchange(keeps, sends, mix(mix_kernel, "mix"), (relaid, there[0], None, there[1]))
    output, gradient, keeps, sends = program.middle(owns, others, held["linear"], slopes)

    def outer(before, grads):
        held["outer"] = program.outer(before, modes, grads, weights)
        return held["outer"]

    def placed(before):
        held["outer"] = tie(jnp.transpose(held["outer"], (0, 3, 2, 1, 4)), *before)
        return held["outer"]

    back = [linear(half, "back", gradient, local_weight, jnp.zeros_like(bias_vector)) for half in range(2)]
    owns, others, _ = program.exchange(
        keeps, sends, mix(mix_back_kernel, "mix_back"), (back[0], back[1], outer, placed)
    )
    grad_inputs = program.synthesise([], owns, others, held["back"])
    grad_spectral = held["outer"]
    return (
        jnp.transpose(output, (0, 2, 1, 3)),
        jnp.transpose(grad_inputs, (0, 2, 1, 3)),
        jnp.transpose(grad_spectral, (0, 1, 3, 2, 4)),
    )


def solution(mesh):
    in_specs = (
        P(("groups", "slab"), "chan", None, None),
        P(("groups", "slab"), "chan", None, None),
        P("slab", "chan", None, None, None),
        P(),
        P(),
    )
    out_specs = (
        P(("groups", "slab"), "chan", None, None),
        P(("groups", "slab"), "chan", None, None),
        P(("groups", "slab"), "chan", None, None, None),
    )
    return jax.shard_map(local, mesh=mesh, in_specs=in_specs, out_specs=out_specs, check_vma=False)
```

```python
from functools import partial
import math

import jax
import jax.numpy as jnp
import ml_dtypes
import numpy as np
from jax import lax
from jax.experimental import pallas as pl
from jax.experimental.pallas import tpu as pltpu
from jax.sharding import PartitionSpec as P

f32 = jnp.float32
bf16 = jnp.bfloat16
root_half = 0.7071067811865476
inv_root_two_pi = 0.3989422804014327
VMEM_LIMIT = 64 * 1024 * 1024
NT = (((1,), (1,)), ((), ()))
TN = (((0,), (0,)), ((), ()))


def round_up(value, unit):
    return -(-value // unit) * unit


class Plan:
    def __init__(self, nx, ny, nz, channels, wb, wk, mx, slab_count, chan_count):
        self.nx, self.ny, self.nz, self.c = nx, ny, nz, channels
        self.wb, self.wk, self.mx = wb, wk, mx
        self.s, self.ch = slab_count, chan_count
        self.half = chan_count // 2
        self.na = mx // 2 + 1
        self.span = (wb + 1) * self.na
        self.lw = slab_count * self.span
        self.lp = round_up(self.lw, 128)
        self.ll = round_up(2 * self.span, 128)
        self.mk = self.half * wk
        self.rc = round_up(2 * self.mk + 2 * self.half, 8)
        self.chunks = 2
        self.cc = channels
        self.w = (wk // 2, wk - wk // 2)
        self.rts = (round_up(channels * self.w[0], 8), round_up(channels * (self.w[1] + 1), 8))
        self.xb = math.gcd(8, nx)
        self.blk = self.xb * ny
        self.rows = self.cc * wk
        self.tall = round_up(self.rows, 16)
        self.bb = math.gcd(2, wb)
        self.lb = math.gcd(4, nx // 2)
        self.batch = max(d for d in range(1, 6) if self.cc % d == 0)
        self.full_x, self.full_y = nx * slab_count, ny * chan_count

    def segments(self, c):
        w0, w1 = self.w
        main = lambda first: lambda h, kind: kind * self.mk + h * self.wk + first
        return (
            (0, c * w0, w0, main(0)),
            (1, c * w1, w1, main(w0)),
            (1, self.c * w1 + c, 1, lambda h, kind: 2 * self.mk + kind * self.half + h),
        )

    def starts(self):
        kept = self.wb * self.s
        return [g * self.wb - (kept if 2 * g >= self.s else 0) for g in range(self.s)]

    def columns(self):
        b = np.concatenate([np.repeat(np.arange(st, st + self.wb + 1), self.na) for st in self.starts()])
        a = np.tile(np.arange(self.na), self.s * (self.wb + 1))
        return a, b

    def plane_table(self):
        a, b = self.columns()
        x = np.repeat(np.arange(self.nx), self.ny)[:, None]
        y = np.tile(np.arange(self.ny), self.nx)[:, None]
        total = self.full_x * self.full_y
        phase = (a * x * self.full_y + b * y * self.full_x) % total * (2.0 * np.pi / total)
        table = np.zeros((self.nx * self.ny, 2 * self.lp))
        scale = 1.0 / math.sqrt(total)
        table[:, : self.lw] = np.cos(phase) * scale
        table[:, self.lp : self.lp + self.lw] = -np.sin(phase) * scale
        high, low = (t.reshape(self.nx // self.xb, 1, self.blk, 2 * self.lp) for t in halves(table))
        return np.concatenate([high, high, low], 1).reshape(-1, 3 * self.blk, 2 * self.lp)

    def turns(self):
        a, b = self.columns()
        x = (np.arange(self.s) * self.nx)[:, None, None]
        y = (np.arange(self.ch) * self.ny)[None, :, None]
        total = self.full_x * self.full_y
        phase = (a * x * self.full_y + b * y * self.full_x) % total * (2.0 * np.pi / total)
        table = np.zeros((self.s, self.ch, 2, self.lp), np.float32)
        table[:, :, 0, : self.lw] = np.cos(phase)
        table[:, :, 1, : self.lw] = np.sin(phase)
        return table

    def depth_rows(self):
        main = np.arange(self.mk)
        edge = (np.arange(self.half) + 1) * self.wk
        z = np.arange(self.nz)
        scale = 1.0 / math.sqrt(self.nz)
        angle = lambda k: (k[:, None] * z) % self.nz * (2.0 * np.pi / self.nz)
        rows = [np.cos(angle(main)), np.sin(angle(main)), np.cos(angle(edge)), np.sin(angle(edge))]
        table = np.zeros((self.rc, self.nz))
        table[: 2 * self.mk + 2 * self.half] = np.concatenate(rows) * scale
        return halves(table)

    def depth_forward(self):
        high, low = self.depth_rows()
        return np.concatenate(
            [np.concatenate([high, high], 1), np.concatenate([low, np.zeros_like(low)], 1)], 0
        )

    def depth_inverse(self):
        high, low = self.depth_rows()
        table = np.zeros((round_up(3 * self.rc, 16), self.nz), ml_dtypes.bfloat16)
        table[: 3 * self.rc] = np.concatenate([high, high, low], 0)
        return table

    def selections(self):
        quarters = 128 // self.mx
        own = np.zeros((self.wb, 2, self.ll, 2, quarters, self.mx), np.float32)
        for b in range(self.wb):
            for r in range(2):
                for a in range(self.mx):
                    if a < self.mx // 2:
                        own[b, 0, r * self.span + b * self.na + a, r, :, a] = 1.0
                    else:
                        spot = r * self.span + (self.wb - b) * self.na + self.mx - a
                        own[b, 1, spot, r, :, a] = 1.0 - 2.0 * r
        own = own.reshape(self.wb, 2 * self.ll, 256)
        back = np.swapaxes(own, 1, 2)
        return own.astype(ml_dtypes.bfloat16), np.ascontiguousarray(back).astype(ml_dtypes.bfloat16)

    def orders(self, chunk):
        w0, w1 = self.w
        table = np.zeros((2, self.rows, self.rts[chunk]), np.float32)
        for c in range(self.c):
            for k in range(self.wk):
                for upper, index in enumerate((k, self.wk - k)):
                    if index < w0:
                        here, spot = 0, c * w0 + index
                    elif index < self.wk:
                        here, spot = 1, c * w1 + index - w0
                    else:
                        here, spot = 1, self.c * w1 + c
                    if here == chunk:
                        table[upper, c * self.wk + k, spot] = 1.0
        return table.astype(ml_dtypes.bfloat16)


def halves(table):
    high = table.astype(np.float32).astype(ml_dtypes.bfloat16)
    low = (table - high.astype(np.float64)).astype(np.float32).astype(ml_dtypes.bfloat16)
    return high, low


def dot(left, right, numbers=(((1,), (0,)), ((), ()))):
    return lax.dot_general(left, right, numbers, preferred_element_type=f32)


def split(value):
    high = value.astype(bf16)
    return high, (value - high.astype(f32)).astype(bf16)


def moved(value, chosen, left=False):
    first, second = split(value)
    if left:
        return dot(chosen, first) + dot(chosen, second)
    rows = value.shape[0]
    if rows % 16:
        return dot(first, chosen) + dot(second, chosen)
    both = dot(jnp.concatenate([first, second], axis=0), chosen)
    return both[:rows] + both[rows:]


def depth_analysis(plan, table_ref, values):
    rows = []
    for value in values:
        high, low = split(value)
        rows.append(jnp.concatenate([high, low], axis=1))
    both = dot(table_ref[...], jnp.concatenate(rows, axis=0), NT)
    lines = both[: plan.rc] + both[plan.rc :]
    return [lines[:, j * plan.blk : (j + 1) * plan.blk] for j in range(len(values))]


def depth_synthesis(plan, table_ref, rows):
    high = rows.astype(bf16).astype(f32)
    parts = [high, rows - high, high]
    extra = table_ref.shape[0] - 3 * plan.rc
    if extra:
        parts.append(jnp.zeros((extra, rows.shape[1]), f32))
    return dot(jnp.concatenate(parts, axis=0).astype(bf16), table_ref[...], TN)


def plane_analysis(plan, step, lines_ref, plane_ref, total_ref):
    high, low = split(lines_ref[...].reshape(plan.cc * plan.rc, plan.blk))
    rows = jnp.concatenate([high, low, high], axis=1)
    for start in range(0, 2 * plan.lp, 256):
        size = min(256, 2 * plan.lp - start)
        columns = pl.ds(start, size)
        part = dot(rows, plane_ref[0, :, columns]).reshape(plan.cc, plan.rc, size)

        @pl.when(step == 0)
        def _():
            total_ref[:, :, columns] = part

        @pl.when(step > 0)
        def _():
            total_ref[:, :, columns] += part


def plane_synthesis(plan, high_rows, low_rows, plane_ref, lines_ref):
    high_table, low_table = plane_ref[0, : plan.blk], plane_ref[0, 2 * plan.blk :]
    lines = (
        dot(high_rows[...], high_table, NT)
        + dot(low_rows[...], high_table, NT)
        + dot(high_rows[...], low_table, NT)
    )
    lines_ref[...] = lines.reshape(plan.cc, plan.rc, plan.blk)


def emit_modes(plan, flag_ref, turn_ref, total_ref, keep_refs, send_refs):
    lp, half = plan.lp, plan.half
    odd = flag_ref[0] == 1
    cosine, sine = turn_ref[0:1, :], turn_ref[1:2, :]
    for c in range(plan.c):
        real, imag = total_ref[c, :, :lp], total_ref[c, :, lp:]
        real, imag = real * cosine + imag * sine, imag * cosine - real * sine
        for m, base, size, place in plan.segments(c):
            made = []
            for g in range(plan.ch):
                h = g if g < half else plan.ch - 1 - g
                even, odd_rows = (slice(place(h, kind), place(h, kind) + size) for kind in (0, 1))
                if g < half:
                    made.append((real[even] + imag[odd_rows], imag[even] - real[odd_rows]))
                else:
                    made.append((real[even] - imag[odd_rows], imag[even] + real[odd_rows]))
            for pair in range(half):
                for r in range(2):
                    low, high = made[2 * pair][r], made[2 * pair + 1][r]
                    keep_refs[m][pair, r, base : base + size, :] = jnp.where(odd, high, low)
                    send_refs[m][pair, r, base : base + size, :] = jnp.where(odd, low, high)
    for m, used in enumerate((plan.c * plan.w[0], plan.c * (plan.w[1] + 1))):
        if used < plan.rts[m]:
            blank = jnp.zeros((half, 2, plan.rts[m] - used, lp), f32)
            keep_refs[m][:, :, used:, :] = blank
            send_refs[m][:, :, used:, :] = blank


def take_modes(plan, flag_ref, turn_ref, group_refs, total_ref, high_rows, low_rows):
    lp, half = plan.lp, plan.half
    odd, upper = flag_ref[0] == 1, flag_ref[1] == 1
    cosine, sine = turn_ref[0:1, :], turn_ref[1:2, :]

    def group(m, g, r, rows):
        here, there, core_here, core_there = (ref[g // 4, r, rows, :] for ref in group_refs[m])
        first, second = ((here, there), (core_here, core_there)) if g % 2 else ((core_here, core_there), (here, there))
        held, came = (jnp.where(odd, a, b) for a, b in zip(first, second))
        return jnp.where(upper, held, came) if g // 2 % 2 else jnp.where(upper, came, held)

    for c in range(plan.c):
        for m, base, size, place in plan.segments(c):
            rows = slice(base, base + size)
            for h in range(half):
                plus = [group(m, h, r, rows) for r in range(2)]
                minus = [group(m, plan.ch - 1 - h, r, rows) for r in range(2)]
                real, imag = plus[0] + minus[0], plus[1] + minus[1]
                here = slice(place(h, 0), place(h, 0) + size)
                total_ref[c, here, :lp] = real * cosine - imag * sine
                total_ref[c, here, lp:] = imag * cosine + real * sine
                real, imag = plus[0] - minus[0], plus[1] - minus[1]
                here = slice(place(h, 1), place(h, 1) + size)
                total_ref[c, here, :lp] = -(imag * cosine + real * sine)
                total_ref[c, here, lp:] = real * cosine - imag * sine
        used = 2 * plan.mk + 2 * half
        if used < plan.rc:
            total_ref[c, used:, :] = jnp.zeros((plan.rc - used, 2 * lp), f32)
    high, low = split(total_ref[...].reshape(plan.c * plan.rc, 2 * lp))
    high_rows[...] = high
    low_rows[...] = low


def analyse_kernel(plan, flag_ref, values_ref, plane_ref, depth_ref, turn_ref, *refs):
    keep_refs, send_refs, (lines_ref, total_ref) = refs[:2], refs[2:4], refs[4:]
    step = pl.program_id(0)

    @pl.loop(0, plan.cc, step=plan.batch)
    def _(c):
        values = [values_ref[:, c + j].reshape(plan.blk, plan.nz) for j in range(plan.batch)]
        for j, lines in enumerate(depth_analysis(plan, depth_ref, values)):
            lines_ref[c + j] = lines

    plane_analysis(plan, step, lines_ref, plane_ref, total_ref)

    @pl.when(step == pl.num_programs(0) - 1)
    def _():
        emit_modes(plan, flag_ref, turn_ref, total_ref, keep_refs, send_refs)


def fields(plan, inverse_ref, lines_ref, first):
    lines = jnp.concatenate([lines_ref[first + j] for j in range(plan.batch)], axis=1)
    values = depth_synthesis(plan, inverse_ref, lines)
    return [values[j * plan.blk : (j + 1) * plan.blk] for j in range(plan.batch)]


def middle_kernel(plan, flag_ref, *refs):
    group_refs, refs = (refs[:4], refs[4:8]), refs[8:]
    linear_ref, cotangent_ref, plane_ref, depth_ref, inverse_ref, turn_ref, output_ref, gradient_ref = refs[:8]
    keep_refs, send_refs, (lines_ref, back_ref, total_ref, high_rows, low_rows) = refs[8:10], refs[10:12], refs[12:]
    step = pl.program_id(0)

    @pl.when(step == 0)
    def _():
        take_modes(plan, flag_ref, turn_ref, group_refs, total_ref, high_rows, low_rows)

    plane_synthesis(plan, high_rows, low_rows, plane_ref, lines_ref)
    shape = (plan.xb, plan.ny, plan.nz)

    @pl.loop(0, plan.cc, step=plan.batch)
    def _(first):
        gradients = []
        for j, field in enumerate(fields(plan, inverse_ref, lines_ref, first)):
            value = field + linear_ref[:, first + j].reshape(plan.blk, plan.nz)
            gate = 0.5 * (1.0 + lax.erf(value * root_half))
            slope = gate + value * jnp.exp(-0.5 * value * value) * inv_root_two_pi
            output_ref[:, first + j] = (value * gate).reshape(shape)
            gradients.append(cotangent_ref[:, first + j].reshape(plan.blk, plan.nz) * slope)
            gradient_ref[:, first + j] = gradients[-1].reshape(shape)
        for j, lines in enumerate(depth_analysis(plan, depth_ref, gradients)):
            back_ref[first + j] = lines

    plane_analysis(plan, step, back_ref, plane_ref, total_ref)

    @pl.when(step == pl.num_programs(0) - 1)
    def _():
        emit_modes(plan, flag_ref, turn_ref, total_ref, keep_refs, send_refs)


def synthesise_kernel(plan, flag_ref, *refs):
    group_refs, refs = (refs[:4], refs[4:8]), refs[8:]
    linear_ref, plane_ref, inverse_ref, turn_ref, output_ref, lines_ref, total_ref, high_rows, low_rows = refs

    @pl.when(pl.program_id(0) == 0)
    def _():
        take_modes(plan, flag_ref, turn_ref, group_refs, total_ref, high_rows, low_rows)

    plane_synthesis(plan, high_rows, low_rows, plane_ref, lines_ref)

    @pl.loop(0, plan.cc, step=plan.batch)
    def _(first):
        for j, field in enumerate(fields(plan, inverse_ref, lines_ref, first)):
            value = field + linear_ref[:, first + j].reshape(plan.blk, plan.nz)
            output_ref[:, first + j] = value.reshape(plan.xb, plan.ny, plan.nz)


def linear_kernel(plan, values_ref, weight_ref, bias_ref, output_ref):
    tiles = [(x, slice(t * 8, (t + 1) * 8)) for x in range(plan.lb) for t in range(plan.ny // 8)]
    values = [values_ref[x, :, t, :].reshape(plan.c * 8, plan.nz) for x, t in tiles]
    high, low = split(jnp.concatenate(values, axis=1))
    size = 8 * plan.c
    row, column = (lax.broadcasted_iota(jnp.int32, (size, plan.c), n) for n in (0, 1))
    repeat = (row // 8 == column).astype(f32)
    exact = partial(lax.dot_general, precision=lax.Precision.HIGHEST, preferred_element_type=f32)
    spread = exact(exact(repeat, weight_ref[...], (((1,), (0,)), ((), ()))), repeat, NT)
    row, column = (lax.broadcasted_iota(jnp.int32, (size, size), n) for n in (0, 1))
    high_matrix, low_matrix = split(jnp.where(row % 8 == column % 8, spread, 0.0))
    bias = exact(repeat, bias_ref[...], (((1,), (1,)), ((), ())))
    matrix = jnp.concatenate([high_matrix, high_matrix, low_matrix], axis=1)
    mixed = dot(matrix, jnp.concatenate([high, low, high], axis=0)) + bias
    for n, (x, t) in enumerate(tiles):
        output_ref[x, :, t, :] = mixed[:, n * plan.nz : (n + 1) * plan.nz].reshape(plan.c, 8, plan.nz)


def pick(plan, upper_ref, parts, chosen_ref, ordered_ref):
    @pl.when(pl.program_id(0) == 0)
    def _():
        for n in range(2):
            found = [moved(part[n][...], part[2][upper_ref[0]], left=True) for part in parts]
            high, low = split(sum(found[1:], found[0]))
            ordered_ref[: plan.rows, n * plan.ll : (n + 1) * plan.ll] = high
            ordered_ref[plan.tall : plan.tall + plan.rows, n * plan.ll : (n + 1) * plan.ll] = low

    both = [dot(ordered_ref[...], chosen_ref[n]) for n in range(plan.bb)]
    return [b[: plan.rows] + b[plan.tall : plan.tall + plan.rows] for b in both]


def give(plan, upper_ref, made_ref, order_ref, back_ref, own_ref, mirror_ref, sums_ref):
    part = moved(made_ref[0], back_ref[0])
    for n in range(1, plan.bb):
        part = part + moved(made_ref[n], back_ref[n])
    step = pl.program_id(0)

    @pl.when(step == 0)
    def _():
        sums_ref[...] = part

    @pl.when(step > 0)
    def _():
        sums_ref[...] += part

    @pl.when(step == pl.num_programs(0) - 1)
    def _():
        own_ref[...] = moved(sums_ref[:, : plan.ll], order_ref[upper_ref[0]], left=True)
        mirror_ref[...] = moved(sums_ref[:, plan.ll :], order_ref[upper_ref[0]], left=True)


def mix_kernel(
    plan, upper_ref, own_ref, mirror_ref, order_ref, disorder_ref, chosen_ref, back_ref, weight_ref,
    own_out, mirror_out, ordered_ref, made_ref, sums_ref,
):
    wk, quarters = plan.wk, 128 // plan.mx
    picked = pick(plan, upper_ref, [(own_ref, mirror_ref, order_ref)], chosen_ref, ordered_ref)
    place = lax.broadcasted_iota(jnp.int32, (wk, 128), 1) // plan.mx
    for n, modes in enumerate(picked):
        for t in range(plan.c // quarters):
            columns = slice(t * 128, (t + 1) * 128)
            real = imag = 0.0
            for i in range(plan.c):
                x_real, x_imag = modes[i * wk : (i + 1) * wk, :128], modes[i * wk : (i + 1) * wk, 128:]
                w_real, w_imag = weight_ref[n, 0, i, :, columns], weight_ref[n, 1, i, :, columns]
                real = real + (w_real * x_real - w_imag * x_imag)
                imag = imag + (w_real * x_imag + w_imag * x_real)
            for q in range(quarters):
                o = t * quarters + q
                made_ref[n, o * wk : (o + 1) * wk, :128] = jnp.where(place == q, real, 0.0)
                made_ref[n, o * wk : (o + 1) * wk, 128:] = jnp.where(place == q, imag, 0.0)
    give(plan, upper_ref, made_ref, disorder_ref, back_ref, own_out, mirror_out, sums_ref)


def along(plan, modes):
    wk, quarters = plan.wk, 128 // plan.mx
    place = lax.broadcasted_iota(jnp.int32, (wk, 128), 1) // plan.mx
    lined = []
    for t in range(plan.c // quarters):
        real = imag = 0.0
        for q in range(quarters):
            o = t * quarters + q
            real = jnp.where(place == q, modes[o * wk : (o + 1) * wk, :128], real)
            imag = jnp.where(place == q, modes[o * wk : (o + 1) * wk, 128:], imag)
        lined.append((slice(t * 128, (t + 1) * 128), real, imag))
    return lined


def mix_back_kernel(
    plan, upper_ref, own_ref, mirror_ref, order_ref, disorder_ref, chosen_ref, back_ref, weight_ref,
    own_out, mirror_out, ordered_ref, made_ref, sums_ref,
):
    wk = plan.wk
    for n, grads in enumerate(pick(plan, upper_ref, [(own_ref, mirror_ref, order_ref)], chosen_ref, ordered_ref)):
        lined = along(plan, grads)
        for i in range(plan.c):
            back_real = back_imag = 0.0
            for columns, real, imag in lined:
                w_real, w_imag = weight_ref[n, 0, i, :, columns], weight_ref[n, 1, i, :, columns]
                back_real = back_real + (w_real * real + w_imag * imag)
                back_imag = back_imag + (w_real * imag - w_imag * real)
            made_ref[n, i * wk : (i + 1) * wk, :128] = back_real
            made_ref[n, i * wk : (i + 1) * wk, 128:] = back_imag
    give(plan, upper_ref, made_ref, disorder_ref, back_ref, own_out, mirror_out, sums_ref)


def outer_kernel(plan, upper_ref, *refs):
    parts = [refs[:8][2 * m : 2 * m + 2] for m in range(4)]
    orders, chosen_ref, gradient_ref, mode_rows, grad_rows = refs[8:10], refs[10], refs[11], refs[12], refs[13]
    wk = plan.wk
    modes = pick(plan, upper_ref, [(*parts[m], orders[m]) for m in range(2)], chosen_ref, mode_rows)
    grads = pick(plan, upper_ref, [(*parts[2 + m], orders[m]) for m in range(2)], chosen_ref, grad_rows)
    for n in range(plan.bb):
        lined = along(plan, grads[n])
        for i in range(plan.c):
            rows = slice(i * wk, (i + 1) * wk)
            x_real, x_imag = modes[n][rows, :128], modes[n][rows, 128:]
            for columns, real, imag in lined:
                gradient_ref[n, 0, i, :, columns] = real * x_real + imag * x_imag
                gradient_ref[n, 1, i, :, columns] = imag * x_real - real * x_imag


def halve_kernel(flag_ref, keep_ref, arrived_ref, kept_ref, send_ref):
    odd = flag_ref[0] == 1
    for pair in range(kept_ref.shape[0]):
        low = keep_ref[2 * pair] + arrived_ref[2 * pair]
        high = keep_ref[2 * pair + 1] + arrived_ref[2 * pair + 1]
        kept_ref[pair] = jnp.where(odd, high, low)
        send_ref[pair] = jnp.where(odd, low, high)


def cut_kernel(plan, place_ref, keep_ref, arrived_ref, came_ref, *refs):
    out_refs, held_ref = refs[:-1], refs[-1]
    lane = lax.broadcasted_iota(jnp.int32, held_ref.shape[1:], 1)
    real = keep_ref[0, 0] + arrived_ref[0, 0] + came_ref[0, 0]
    imag = keep_ref[0, 1] + arrived_ref[0, 1] + came_ref[0, 1]
    for g in range(plan.s):
        first = pltpu.roll(real, (plan.lp - g * plan.span) % plan.lp, 1)[:, : plan.ll]
        second = pltpu.roll(imag, (plan.lp - g * plan.span + plan.span) % plan.lp, 1)[:, : plan.ll]
        held_ref[g] = jnp.where(lane < plan.span, first, jnp.where(lane < 2 * plan.span, second, 0.0))
    for j, out_ref in enumerate(out_refs):
        out_ref[...] = held_ref[place_ref[0] ^ j]


def join_kernel(plan, slab_ref, *refs):
    piece_refs, total_ref, held_ref = refs[:-2], refs[-2], refs[-1]
    for j, piece_ref in enumerate(piece_refs):
        held_ref[j] = piece_ref[...]
    rows = held_ref.shape[1]
    lane = lax.broadcasted_iota(jnp.int32, (rows, plan.lp), 1)
    real = imag = jnp.zeros((rows, plan.lp), f32)
    blank = jnp.zeros((rows, plan.lp - plan.ll), f32)
    for g in range(plan.s):
        piece = jnp.concatenate([held_ref[slab_ref[0] ^ g], blank], axis=1)
        here = (lane >= g * plan.span) & (lane < (g + 1) * plan.span)
        real = jnp.where(here, pltpu.roll(piece, g * plan.span, 1), real)
        imag = jnp.where(here, pltpu.roll(piece, (g * plan.span - plan.span) % plan.lp, 1), imag)
    total_ref[0, 0] = real
    total_ref[0, 1] = imag


def whole(array):
    zeros = (0,) * array.ndim
    return pl.BlockSpec(array.shape, lambda i: zeros, pipeline_mode=pl.Buffered(1))


def whole_shape(shape):
    zeros = (0,) * len(shape)
    return pl.BlockSpec(shape, lambda i: zeros, pipeline_mode=pl.Buffered(1))


def leading(shape):
    rest = (0,) * (len(shape) - 1)
    return pl.BlockSpec(shape, lambda i: (i,) + rest)


def shaped(*shape):
    return jax.ShapeDtypeStruct(shape, f32)


def anywhere():
    return pl.BlockSpec(memory_space=pl.ANY)


def scalar():
    return pl.BlockSpec(memory_space=pltpu.SMEM)


def call(kernel, name, grid, in_specs, out_specs, out_shape, scratch, cost, before=(), aliases=None):
    skipped = len(before)
    run = pl.pallas_call(
        lambda *refs: kernel(*refs[skipped:]),
        grid=(grid,),
        in_specs=[anywhere()] * skipped + list(in_specs),
        out_specs=out_specs,
        out_shape=out_shape,
        scratch_shapes=scratch,
        name=name,
        input_output_aliases=aliases or {},
        compiler_params=pltpu.CompilerParams(vmem_limit_bytes=VMEM_LIMIT, dimension_semantics=("arbitrary",)),
        cost_estimate=pl.CostEstimate(flops=int(cost * 1.15e9), bytes_accessed=int(cost * 3.6e6), transcendentals=0),
    )
    return partial(run, *before)


def tie(value, *before):
    if not before:
        return value
    return pl.pallas_call(
        lambda *refs: None,
        in_specs=[anywhere()] * (1 + len(before)),
        out_specs=anywhere(),
        out_shape=jax.ShapeDtypeStruct(value.shape, value.dtype),
        input_output_aliases={0: 0},
        name="tie",
    )(value, *before)


class Program:
    def __init__(self, plan):
        self.plan = plan
        self.plane = jnp.asarray(plan.plane_table())
        self.depth = jnp.asarray(plan.depth_forward())
        self.inverse = jnp.asarray(plan.depth_inverse())
        slab, chan = lax.axis_index("slab"), lax.axis_index("chan")
        self.slab, self.chan = slab, chan
        turns = jnp.asarray(plan.turns())
        self.turn = lax.dynamic_index_in_dim(
            lax.dynamic_index_in_dim(turns, slab, 0, False), chan, 0, False
        )
        self.slab_index = slab.astype(jnp.int32).reshape(1)
        self.flag = jnp.stack([chan % 2, chan // 2 % 2]).astype(jnp.int32)
        self.upper = (chan >= plan.half).astype(jnp.int32).reshape(1)
        tables = [plan.orders(m) for m in range(plan.chunks)]
        self.order = [jnp.asarray(t) for t in tables]
        self.disorder = [jnp.asarray(np.ascontiguousarray(np.swapaxes(t, 1, 2))) for t in tables]
        chosen, back = plan.selections()
        self.chosen, self.back = jnp.asarray(chosen), jnp.asarray(back)

    def half_shapes(self):
        plan = self.plan
        return [(plan.half, 2, rt, plan.lp) for rt in plan.rts]

    def field_spec(self):
        plan = self.plan
        return leading((plan.xb, plan.c, plan.ny, plan.nz))

    def table(self):
        plan = self.plan
        return leading((1, 3 * plan.blk, 2 * plan.lp))

    def lines(self):
        plan = self.plan
        return pltpu.VMEM((plan.cc, plan.rc, plan.blk), f32)

    def spectra(self):
        plan = self.plan
        rows = pltpu.VMEM((plan.cc * plan.rc, 2 * plan.lp), bf16)
        return [pltpu.VMEM((plan.cc, plan.rc, 2 * plan.lp), f32), rows, rows]

    def analyse(self, values):
        plan = self.plan
        halves = self.half_shapes()
        made = call(
            partial(analyse_kernel, plan), "analyse", plan.nx // plan.xb,
            [scalar(), self.field_spec(), self.table(), whole(self.depth), whole(self.turn)],
            [whole_shape(h) for h in halves * 2], [shaped(*h) for h in halves * 2],
            [self.lines(), self.spectra()[0]], 26,
        )(self.flag, values, self.plane, self.depth, self.turn)
        return made[:2], made[2:]

    def middle(self, groups, linear, cotangent):
        plan = self.plan
        halves = self.half_shapes()
        taken = [part for group in groups for part in group]
        field, spec = shaped(plan.nx, plan.c, plan.ny, plan.nz), self.field_spec()
        modes = [whole_shape(h) for h in halves * 2]
        output, gradient, *made = call(
            partial(middle_kernel, plan), "middle", plan.nx // plan.xb,
            [scalar(), *[whole(t) for t in taken], spec, spec, self.table(), whole(self.depth), whole(self.inverse), whole(self.turn)],
            [spec, spec, *modes], [field, field, *[shaped(*h) for h in halves * 2]],
            [self.lines(), self.lines(), *self.spectra()], 47,
        )(self.flag, *taken, linear, cotangent, self.plane, self.depth, self.inverse, self.turn)
        return output, gradient, made[:2], made[2:]

    def synthesise(self, before, groups, linear):
        plan = self.plan
        taken = [part for group in groups for part in group]
        spec = self.field_spec()
        return call(
            partial(synthesise_kernel, plan), "synthesise", plan.nx // plan.xb,
            [scalar(), *[whole(t) for t in taken], spec, self.table(),
             whole(self.inverse), whole(self.turn)],
            spec, shaped(plan.nx, plan.c, plan.ny, plan.nz),
            [self.lines(), *self.spectra()], 20, before,
        )(self.flag, *taken, linear, self.plane, self.inverse, self.turn)

    def linear(self, half, before, filled, values, matrix, bias):
        plan = self.plan
        bias = bias[None]
        steps = plan.nx // plan.lb // 2
        spec = pl.BlockSpec((plan.lb, plan.c, plan.ny, plan.nz), lambda i: (i + half * steps, 0, 0, 0))
        return call(
            partial(linear_kernel, plan), "linear", steps,
            [spec, whole(matrix), whole(bias)],
            spec, shaped(plan.nx, plan.c, plan.ny, plan.nz), [], 7, (*filled, *before), {0: 0} if filled else None,
        )(values, matrix, bias)

    def mix(self, kernel, name, chunk, before, own, mirror, weights):
        plan = self.plan
        modes = (plan.rts[chunk], plan.ll)
        order, disorder = self.order[chunk], self.disorder[chunk]
        ordered = pltpu.VMEM((2 * plan.tall, 2 * plan.ll), bf16)
        return call(
            partial(kernel, plan), name, plan.wb // plan.bb,
            [
                scalar(), whole_shape(modes), whole_shape(modes), whole(order), whole(disorder),
                leading((plan.bb,) + self.chosen.shape[1:]), leading((plan.bb,) + self.back.shape[1:]),
                leading((plan.bb, *weights.shape[1:])),
            ],
            [whole_shape(modes)] * 2, [shaped(*modes)] * 2,
            [ordered, pltpu.VMEM((plan.bb, plan.rows, 256), f32), pltpu.VMEM((plan.rows, 2 * plan.ll), f32)], 9, before,
        )(self.upper, own, mirror, order, disorder, self.chosen, self.back, weights)

    def outer(self, before, modes, grads, weights):
        plan = self.plan
        parts = [part for pair in (*modes, *grads) for part in pair]
        ordered = pltpu.VMEM((2 * plan.tall, 2 * plan.ll), bf16)
        out = leading((plan.bb, *weights.shape[1:]))
        return call(
            partial(outer_kernel, plan), "outer", plan.wb // plan.bb,
            [scalar(), *[whole(p) for p in parts], *[whole(o) for o in self.order], leading((plan.bb,) + self.chosen.shape[1:])],
            out, shaped(*weights.shape), [ordered, ordered], 9, before,
        )(self.upper, *parts, *self.order, self.chosen)

    def across(self, value, axis, bit):
        size = lax.axis_size(axis)
        return lax.ppermute(value, axis, [(i, i ^ bit) for i in range(size)])

    def mirrored(self, value):
        total = self.plan.s * self.plan.ch
        return lax.ppermute(value, ("slab", "chan"), [(i, total - 1 - i) for i in range(total)])

    def chosen_half(self, kernel, name, grid, in_specs, out_specs, out_shape, scratch, arrays):
        place = jnp.stack([self.slab, self.chan // (self.plan.ch // 2)]).astype(jnp.int32)
        return pl.pallas_call(
            kernel,
            grid_spec=pltpu.PrefetchScalarGridSpec(
                num_scalar_prefetch=1, grid=grid, in_specs=in_specs, out_specs=out_specs, scratch_shapes=scratch
            ),
            out_shape=out_shape,
            name=name,
            compiler_params=pltpu.CompilerParams(vmem_limit_bytes=VMEM_LIMIT, dimension_semantics=("arbitrary",)),
            cost_estimate=pl.CostEstimate(flops=10**9, bytes_accessed=4 * 10**6, transcendentals=0),
        )(place, *arrays)

    def sent_half(self, keep, arrived):
        other = 1 - self.chan // (self.plan.ch // 2)
        return lax.dynamic_index_in_dim(keep, other, 0) + lax.dynamic_index_in_dim(arrived, other, 0)

    def halve(self, keep, arrived, bit):
        mine = ((self.chan // bit) % 2).astype(jnp.int32).reshape(1)
        half = (keep.shape[0] // 2,) + keep.shape[1:]
        return call(
            halve_kernel, "halve", 1, [scalar(), whole(keep), whole(keep)], [whole_shape(half)] * 2,
            [shaped(*half)] * 2, [], 2,
        )(mine, keep, arrived)

    def sums_over_chan(self, keep, arrived, before):
        bit = 2
        while 2 * bit < self.plan.ch:
            keep, sent = self.halve(keep, arrived, bit)
            arrived = self.across(sent, "chan", bit)
            bit *= 2
        sent = tie(self.sent_half(keep, arrived), *before)
        return (keep, arrived), sent, self.across(sent, "chan", bit)

    def cut(self, kept, came):
        plan = self.plan
        size = (came.shape[2], plan.ll)
        block = (1,) + came.shape[1:]
        spec = pl.BlockSpec(block, lambda i, place: (place[1], 0, 0, 0))
        mine, *pieces = self.chosen_half(
            partial(cut_kernel, plan), "cut", (1,), [spec, spec, pl.BlockSpec(block, lambda i, place: (0, 0, 0, 0))],
            [pl.BlockSpec(size, lambda i, place: (0, 0))] * plan.s, [shaped(*size)] * plan.s,
            [pltpu.VMEM((plan.s, *size), f32)], (*kept, came),
        )
        return mine, pieces

    def join(self, mine, arrived):
        plan = self.plan
        total = (1, 2, mine.shape[0], plan.lp)
        return call(
            partial(join_kernel, plan), "join", 1, [scalar()] + [whole(mine)] * plan.s,
            whole_shape(total), shaped(*total), [pltpu.VMEM((plan.s, *mine.shape), f32)], 2,
        )(self.slab_index, mine, *arrived)

    def exchange(self, keeps, sends, mix, fillers):
        def fill(n, value, *before):
            return tie(value, fillers[n](before)) if fillers[n] else value

        plan = self.plan
        first = [self.across(send, "chan", 1) for send in sends]
        keep0, sent0, came0 = self.sums_over_chan(keeps[0], first[0], [])
        came0 = fill(0, came0, sent0, first[1])
        keep1, sent1, came1 = self.sums_over_chan(keeps[1], first[1], [came0])

        mine, pieces = self.cut(keep0, came0)
        arrived = [self.across(piece, "slab", j + 1) for j, piece in enumerate(pieces)]
        for piece in [fill(1, arrived[0], mine, sent1)] + arrived[1:]:
            mine = mine + piece
        own0 = mine
        mirror0 = self.mirrored(own0)
        mine, pieces = self.cut(keep1, tie(came1, own0))
        arrived = [self.across(piece, "slab", j + 1) for j, piece in enumerate(pieces)]
        out0, back0 = mix(0, [mine], own0, mirror0)
        full0 = out0 + self.mirrored(back0)
        for piece in [tie(arrived[0], full0)] + arrived[1:]:
            mine = mine + piece
        own1 = mine
        mirror1 = self.mirrored(own1)

        arrived = [self.across(full0, "slab", j) for j in range(1, plan.s)]
        out1, back1 = mix(1, [full0], own1, mirror1)
        full1 = out1 + self.mirrored(back1)
        total0 = self.join(full0, [tie(arrived[0], back1)] + arrived[1:])
        came0 = self.across(total0, "chan", plan.ch // 2)
        full1 = tie(full1, total0)
        arrived = [self.across(full1, "slab", j) for j in range(1, plan.s)]
        modes = ((own0, mirror0), (own1, mirror1))
        if fillers[2]:
            came0 = tie(came0, fillers[2]([total0], modes))
        total1 = tie(self.join(full1, arrived), came0)
        came1 = self.across(total1, "chan", plan.ch // 2)
        came1 = fill(3, came1, total1)

        groups = []
        for total, other in ((total0, came0), (total1, came1)):
            if groups:
                other = tie(other, *groups[0][2:])
            bit = plan.ch // 2
            while bit > 2:
                upper = (self.chan // bit) % 2 == 1
                total = jnp.stack([jnp.where(upper, other, total), jnp.where(upper, total, other)], axis=1)
                total = total.reshape((-1,) + total.shape[2:])
                bit //= 2
                other = self.across(total, "chan", bit)
            groups.append((total, other, self.across(total, "chan", 1), self.across(other, "chan", 1)))
        return groups, modes


def local(inputs, cotangent, spectral, local_weight, bias_vector):
    nx, ny, channels, nz = inputs.shape
    wb, wk = spectral.shape[0], spectral.shape[1]
    plan = Plan(nx, ny, nz, channels, wb, wk, spectral.shape[4] // channels, lax.axis_size("slab"), lax.axis_size("chan"))
    program = Program(plan)
    values = jnp.transpose(inputs, (0, 2, 1, 3))
    slopes = jnp.transpose(cotangent, (0, 2, 1, 3))
    weights = jnp.transpose(spectral, (0, 2, 3, 1, 4))

    held = {}

    def relaid(before):
        held["weights"] = tie(weights, *before)
        return held["weights"]

    def linear(half, name, values, matrix, bias):
        def run(before):
            filled = [held[name]] if half else []
            held[name] = program.linear(half, before, filled, values, matrix, bias)
            return held[name]

        return run

    def mix(kernel, name):
        return lambda m, before, own, mirror: program.mix(kernel, name, m, before, own, mirror, held["weights"])

    keeps, sends = program.analyse(values)
    there = [linear(half, "linear", values, local_weight.T, bias_vector) for half in range(2)]
    groups, modes = program.exchange(keeps, sends, mix(mix_kernel, "mix"), (relaid, there[0], None, there[1]))
    output, gradient, keeps, sends = program.middle(groups, held["linear"], slopes)

    def outer(before, grads):
        held["outer"] = program.outer(before, modes, grads, weights)
        return held["outer"]

    def placed(before):
        held["outer"] = tie(jnp.transpose(held["outer"], (0, 3, 2, 1, 4)), *before)
        return held["outer"]

    back = [linear(half, "back", gradient, local_weight, jnp.zeros_like(bias_vector)) for half in range(2)]
    groups, _ = program.exchange(
        keeps, sends, mix(mix_back_kernel, "mix_back"), (back[0], back[1], outer, placed)
    )
    grad_inputs = program.synthesise([], groups, held["back"])
    grad_spectral = held["outer"]
    return (
        jnp.transpose(output, (0, 2, 1, 3)),
        jnp.transpose(grad_inputs, (0, 2, 1, 3)),
        jnp.transpose(grad_spectral, (0, 1, 3, 2, 4)),
    )


def solution(mesh):
    in_specs = (
        P(("groups", "slab"), "chan", None, None),
        P(("groups", "slab"), "chan", None, None),
        P("slab", "chan", None, None, None),
        P(),
        P(),
    )
    out_specs = (
        P(("groups", "slab"), "chan", None, None),
        P(("groups", "slab"), "chan", None, None),
        P(("groups", "slab"), "chan", None, None, None),
    )
    return jax.shard_map(local, mesh=mesh, in_specs=in_specs, out_specs=out_specs, check_vma=False)
```

```python
from functools import partial
import math

import jax
import jax.numpy as jnp
import ml_dtypes
import numpy as np
from jax import lax
from jax.experimental import pallas as pl
from jax.experimental.pallas import tpu as pltpu
from jax.sharding import PartitionSpec as P

f32 = jnp.float32
bf16 = jnp.bfloat16
root_half = 0.7071067811865476
inv_root_two_pi = 0.3989422804014327
VMEM_LIMIT = 64 * 1024 * 1024
NT = (((1,), (1,)), ((), ()))
TN = (((0,), (0,)), ((), ()))


def round_up(value, unit):
    return -(-value // unit) * unit


class Plan:
    def __init__(self, nx, ny, nz, channels, wb, wk, mx, slab_count, chan_count):
        self.nx, self.ny, self.nz, self.c = nx, ny, nz, channels
        self.wb, self.wk, self.mx = wb, wk, mx
        self.s, self.ch = slab_count, chan_count
        self.half = chan_count // 2
        self.na = mx // 2 + 1
        self.span = (wb + 1) * self.na
        self.lw = slab_count * self.span
        self.lp = round_up(self.lw, 128)
        self.ll = round_up(2 * self.span, 128)
        self.mk = self.half * wk
        self.rc = round_up(2 * self.mk + 2 * self.half, 8)
        self.chunks = 2
        self.cc = channels
        self.w = (wk // 2, wk - wk // 2)
        self.rts = (round_up(channels * self.w[0], 8), round_up(channels * (self.w[1] + 1), 8))
        self.xb = math.gcd(8, nx)
        self.blk = self.xb * ny
        self.rows = self.cc * wk
        self.tall = round_up(self.rows, 16)
        self.bb = math.gcd(4, wb)
        self.lb = math.gcd(4, nx // 2)
        self.batch = max(d for d in range(1, 6) if self.cc % d == 0)
        self.full_x, self.full_y = nx * slab_count, ny * chan_count

    def segments(self, c):
        w0, w1 = self.w
        main = lambda first: lambda h, kind: kind * self.mk + h * self.wk + first
        return (
            (0, c * w0, w0, main(0)),
            (1, c * w1, w1, main(w0)),
            (1, self.c * w1 + c, 1, lambda h, kind: 2 * self.mk + kind * self.half + h),
        )

    def starts(self):
        kept = self.wb * self.s
        return [g * self.wb - (kept if 2 * g >= self.s else 0) for g in range(self.s)]

    def columns(self):
        b = np.concatenate([np.repeat(np.arange(st, st + self.wb + 1), self.na) for st in self.starts()])
        a = np.tile(np.arange(self.na), self.s * (self.wb + 1))
        return a, b

    def plane_table(self):
        a, b = self.columns()
        x = np.repeat(np.arange(self.nx), self.ny)[:, None]
        y = np.tile(np.arange(self.ny), self.nx)[:, None]
        total = self.full_x * self.full_y
        phase = (a * x * self.full_y + b * y * self.full_x) % total * (2.0 * np.pi / total)
        table = np.zeros((self.nx * self.ny, 2 * self.lp))
        scale = 1.0 / math.sqrt(total)
        table[:, : self.lw] = np.cos(phase) * scale
        table[:, self.lp : self.lp + self.lw] = -np.sin(phase) * scale
        high, low = (t.reshape(self.nx // self.xb, 1, self.blk, 2 * self.lp) for t in halves(table))
        return np.concatenate([high, high, low], 1).reshape(-1, 3 * self.blk, 2 * self.lp)

    def turns(self):
        a, b = self.columns()
        x = (np.arange(self.s) * self.nx)[:, None, None]
        y = (np.arange(self.ch) * self.ny)[None, :, None]
        total = self.full_x * self.full_y
        phase = (a * x * self.full_y + b * y * self.full_x) % total * (2.0 * np.pi / total)
        table = np.zeros((self.s, self.ch, 2, self.lp), np.float32)
        table[:, :, 0, : self.lw] = np.cos(phase)
        table[:, :, 1, : self.lw] = np.sin(phase)
        return table

    def depth_rows(self):
        main = np.arange(self.mk)
        edge = (np.arange(self.half) + 1) * self.wk
        z = np.arange(self.nz)
        scale = 1.0 / math.sqrt(self.nz)
        angle = lambda k: (k[:, None] * z) % self.nz * (2.0 * np.pi / self.nz)
        rows = [np.cos(angle(main)), np.sin(angle(main)), np.cos(angle(edge)), np.sin(angle(edge))]
        table = np.zeros((self.rc, self.nz))
        table[: 2 * self.mk + 2 * self.half] = np.concatenate(rows) * scale
        return halves(table)

    def depth_forward(self):
        high, low = self.depth_rows()
        return np.concatenate(
            [np.concatenate([high, high], 1), np.concatenate([low, np.zeros_like(low)], 1)], 0
        )

    def depth_inverse(self):
        high, low = self.depth_rows()
        table = np.zeros((round_up(3 * self.rc, 16), self.nz), ml_dtypes.bfloat16)
        table[: 3 * self.rc] = np.concatenate([high, high, low], 0)
        return table

    def selections(self):
        quarters = 128 // self.mx
        own = np.zeros((self.wb, 2, self.ll, 2, quarters, self.mx), np.float32)
        for b in range(self.wb):
            for r in range(2):
                for a in range(self.mx):
                    if a < self.mx // 2:
                        own[b, 0, r * self.span + b * self.na + a, r, :, a] = 1.0
                    else:
                        spot = r * self.span + (self.wb - b) * self.na + self.mx - a
                        own[b, 1, spot, r, :, a] = 1.0 - 2.0 * r
        own = own.reshape(self.wb, 2 * self.ll, 256)
        back = np.swapaxes(own, 1, 2)
        return own.astype(ml_dtypes.bfloat16), np.ascontiguousarray(back).astype(ml_dtypes.bfloat16)

    def orders(self, chunk):
        w0, w1 = self.w
        table = np.zeros((2, self.rows, self.rts[chunk]), np.float32)
        for c in range(self.c):
            for k in range(self.wk):
                for upper, index in enumerate((k, self.wk - k)):
                    if index < w0:
                        here, spot = 0, c * w0 + index
                    elif index < self.wk:
                        here, spot = 1, c * w1 + index - w0
                    else:
                        here, spot = 1, self.c * w1 + c
                    if here == chunk:
                        table[upper, c * self.wk + k, spot] = 1.0
        return table.astype(ml_dtypes.bfloat16)


def halves(table):
    high = table.astype(np.float32).astype(ml_dtypes.bfloat16)
    low = (table - high.astype(np.float64)).astype(np.float32).astype(ml_dtypes.bfloat16)
    return high, low


def dot(left, right, numbers=(((1,), (0,)), ((), ()))):
    return lax.dot_general(left, right, numbers, preferred_element_type=f32)


def split(value):
    high = value.astype(bf16)
    return high, (value - high.astype(f32)).astype(bf16)


def moved(value, chosen, left=False):
    first, second = split(value)
    if left:
        return dot(chosen, first) + dot(chosen, second)
    rows = value.shape[0]
    if rows % 16:
        return dot(first, chosen) + dot(second, chosen)
    both = dot(jnp.concatenate([first, second], axis=0), chosen)
    return both[:rows] + both[rows:]


def depth_analysis(plan, table_ref, values):
    rows = []
    for value in values:
        high, low = split(value)
        rows.append(jnp.concatenate([high, low], axis=1))
    both = dot(table_ref[...], jnp.concatenate(rows, axis=0), NT)
    lines = both[: plan.rc] + both[plan.rc :]
    return [lines[:, j * plan.blk : (j + 1) * plan.blk] for j in range(len(values))]


def depth_synthesis(plan, table_ref, rows):
    high = rows.astype(bf16).astype(f32)
    parts = [high, rows - high, high]
    extra = table_ref.shape[0] - 3 * plan.rc
    if extra:
        parts.append(jnp.zeros((extra, rows.shape[1]), f32))
    return dot(jnp.concatenate(parts, axis=0).astype(bf16), table_ref[...], TN)


def plane_analysis(plan, step, lines_ref, plane_ref, total_ref):
    high, low = split(lines_ref[...].reshape(plan.cc * plan.rc, plan.blk))
    rows = jnp.concatenate([high, low, high], axis=1)
    for start in range(0, 2 * plan.lp, 256):
        size = min(256, 2 * plan.lp - start)
        columns = pl.ds(start, size)
        part = dot(rows, plane_ref[0, :, columns]).reshape(plan.cc, plan.rc, size)

        @pl.when(step == 0)
        def _():
            total_ref[:, :, columns] = part

        @pl.when(step > 0)
        def _():
            total_ref[:, :, columns] += part


def plane_synthesis(plan, high_rows, low_rows, plane_ref, lines_ref):
    high_table, low_table = plane_ref[0, : plan.blk], plane_ref[0, 2 * plan.blk :]
    lines = (
        dot(high_rows[...], high_table, NT)
        + dot(low_rows[...], high_table, NT)
        + dot(high_rows[...], low_table, NT)
    )
    lines_ref[...] = lines.reshape(plan.cc, plan.rc, plan.blk)


def emit_modes(plan, flag_ref, turn_ref, total_ref, keep_refs, send_refs):
    lp, half = plan.lp, plan.half
    odd = flag_ref[0] == 1
    cosine, sine = turn_ref[flag_ref[2], 0:1, :], turn_ref[flag_ref[2], 1:2, :]
    for c in range(plan.c):
        real, imag = total_ref[c, :, :lp], total_ref[c, :, lp:]
        real, imag = real * cosine + imag * sine, imag * cosine - real * sine
        for m, base, size, place in plan.segments(c):
            made = []
            for g in range(plan.ch):
                h = g if g < half else plan.ch - 1 - g
                even, odd_rows = (slice(place(h, kind), place(h, kind) + size) for kind in (0, 1))
                if g < half:
                    made.append((real[even] + imag[odd_rows], imag[even] - real[odd_rows]))
                else:
                    made.append((real[even] - imag[odd_rows], imag[even] + real[odd_rows]))
            for pair in range(half):
                for r in range(2):
                    low, high = made[2 * pair][r], made[2 * pair + 1][r]
                    keep_refs[m][pair, r, base : base + size, :] = jnp.where(odd, high, low)
                    send_refs[m][pair, r, base : base + size, :] = jnp.where(odd, low, high)
    for m, used in enumerate((plan.c * plan.w[0], plan.c * (plan.w[1] + 1))):
        if used < plan.rts[m]:
            blank = jnp.zeros((half, 2, plan.rts[m] - used, lp), f32)
            keep_refs[m][:, :, used:, :] = blank
            send_refs[m][:, :, used:, :] = blank


def take_modes(plan, flag_ref, turn_ref, group_refs, total_ref, high_rows, low_rows):
    lp, half = plan.lp, plan.half
    odd, upper = flag_ref[0] == 1, flag_ref[1] == 1
    cosine, sine = turn_ref[flag_ref[2], 0:1, :], turn_ref[flag_ref[2], 1:2, :]

    def group(m, g, r, rows):
        here, there, core_here, core_there = (ref[g // 4, r, rows, :] for ref in group_refs[m])
        first, second = ((here, there), (core_here, core_there)) if g % 2 else ((core_here, core_there), (here, there))
        held, came = (jnp.where(odd, a, b) for a, b in zip(first, second))
        return jnp.where(upper, held, came) if g // 2 % 2 else jnp.where(upper, came, held)

    for c in range(plan.c):
        for m, base, size, place in plan.segments(c):
            rows = slice(base, base + size)
            for h in range(half):
                plus = [group(m, h, r, rows) for r in range(2)]
                minus = [group(m, plan.ch - 1 - h, r, rows) for r in range(2)]
                real, imag = plus[0] + minus[0], plus[1] + minus[1]
                here = slice(place(h, 0), place(h, 0) + size)
                total_ref[c, here, :lp] = real * cosine - imag * sine
                total_ref[c, here, lp:] = imag * cosine + real * sine
                real, imag = plus[0] - minus[0], plus[1] - minus[1]
                here = slice(place(h, 1), place(h, 1) + size)
                total_ref[c, here, :lp] = -(imag * cosine + real * sine)
                total_ref[c, here, lp:] = real * cosine - imag * sine
        used = 2 * plan.mk + 2 * half
        if used < plan.rc:
            total_ref[c, used:, :] = jnp.zeros((plan.rc - used, 2 * lp), f32)
    high, low = split(total_ref[...].reshape(plan.c * plan.rc, 2 * lp))
    high_rows[...] = high
    low_rows[...] = low


def analyse_kernel(plan, flag_ref, values_ref, plane_ref, depth_ref, turn_ref, *refs):
    keep_refs, send_refs, (lines_ref, total_ref) = refs[:2], refs[2:4], refs[4:]
    step = pl.program_id(0)

    @pl.loop(0, plan.cc, step=plan.batch)
    def _(c):
        values = [values_ref[:, c + j].reshape(plan.blk, plan.nz) for j in range(plan.batch)]
        for j, lines in enumerate(depth_analysis(plan, depth_ref, values)):
            lines_ref[c + j] = lines

    plane_analysis(plan, step, lines_ref, plane_ref, total_ref)

    @pl.when(step == pl.num_programs(0) - 1)
    def _():
        emit_modes(plan, flag_ref, turn_ref, total_ref, keep_refs, send_refs)


def fields(plan, inverse_ref, lines_ref, first):
    lines = jnp.concatenate([lines_ref[first + j] for j in range(plan.batch)], axis=1)
    values = depth_synthesis(plan, inverse_ref, lines)
    return [values[j * plan.blk : (j + 1) * plan.blk] for j in range(plan.batch)]


def middle_kernel(plan, flag_ref, *refs):
    group_refs, refs = (refs[:4], refs[4:8]), refs[8:]
    linear_ref, cotangent_ref, plane_ref, depth_ref, inverse_ref, turn_ref, output_ref, gradient_ref = refs[:8]
    keep_refs, send_refs, (lines_ref, back_ref, total_ref, high_rows, low_rows) = refs[8:10], refs[10:12], refs[12:]
    step = pl.program_id(0)

    @pl.when(step == 0)
    def _():
        take_modes(plan, flag_ref, turn_ref, group_refs, total_ref, high_rows, low_rows)

    plane_synthesis(plan, high_rows, low_rows, plane_ref, lines_ref)
    shape = (plan.xb, plan.ny, plan.nz)

    @pl.loop(0, plan.cc, step=plan.batch)
    def _(first):
        gradients = []
        for j, field in enumerate(fields(plan, inverse_ref, lines_ref, first)):
            value = field + linear_ref[:, first + j].reshape(plan.blk, plan.nz)
            gate = 0.5 * (1.0 + lax.erf(value * root_half))
            slope = gate + value * jnp.exp(-0.5 * value * value) * inv_root_two_pi
            output_ref[:, first + j] = (value * gate).reshape(shape)
            gradients.append(cotangent_ref[:, first + j].reshape(plan.blk, plan.nz) * slope)
            gradient_ref[:, first + j] = gradients[-1].reshape(shape)
        for j, lines in enumerate(depth_analysis(plan, depth_ref, gradients)):
            back_ref[first + j] = lines

    plane_analysis(plan, step, back_ref, plane_ref, total_ref)

    @pl.when(step == pl.num_programs(0) - 1)
    def _():
        emit_modes(plan, flag_ref, turn_ref, total_ref, keep_refs, send_refs)


def synthesise_kernel(plan, flag_ref, *refs):
    group_refs, refs = (refs[:4], refs[4:8]), refs[8:]
    linear_ref, plane_ref, inverse_ref, turn_ref, output_ref, lines_ref, total_ref, high_rows, low_rows = refs

    @pl.when(pl.program_id(0) == 0)
    def _():
        take_modes(plan, flag_ref, turn_ref, group_refs, total_ref, high_rows, low_rows)

    plane_synthesis(plan, high_rows, low_rows, plane_ref, lines_ref)

    @pl.loop(0, plan.cc, step=plan.batch)
    def _(first):
        for j, field in enumerate(fields(plan, inverse_ref, lines_ref, first)):
            value = field + linear_ref[:, first + j].reshape(plan.blk, plan.nz)
            output_ref[:, first + j] = value.reshape(plan.xb, plan.ny, plan.nz)


def linear_kernel(plan, values_ref, weight_ref, bias_ref, output_ref):
    tiles = [(x, slice(t * 8, (t + 1) * 8)) for x in range(plan.lb) for t in range(plan.ny // 8)]
    values = [values_ref[x, :, t, :].reshape(plan.c * 8, plan.nz) for x, t in tiles]
    high, low = split(jnp.concatenate(values, axis=1))
    size = 8 * plan.c
    row, column = (lax.broadcasted_iota(jnp.int32, (size, plan.c), n) for n in (0, 1))
    repeat = (row // 8 == column).astype(f32)
    exact = partial(lax.dot_general, precision=lax.Precision.HIGHEST, preferred_element_type=f32)
    spread = exact(exact(repeat, weight_ref[...], (((1,), (0,)), ((), ()))), repeat, NT)
    row, column = (lax.broadcasted_iota(jnp.int32, (size, size), n) for n in (0, 1))
    high_matrix, low_matrix = split(jnp.where(row % 8 == column % 8, spread, 0.0))
    bias = exact(repeat, bias_ref[...], (((1,), (1,)), ((), ())))
    matrix = jnp.concatenate([high_matrix, high_matrix, low_matrix], axis=1)
    mixed = dot(matrix, jnp.concatenate([high, low, high], axis=0)) + bias
    for n, (x, t) in enumerate(tiles):
        output_ref[x, :, t, :] = mixed[:, n * plan.nz : (n + 1) * plan.nz].reshape(plan.c, 8, plan.nz)


def pick(plan, upper_ref, parts, chosen_ref, ordered_ref):
    @pl.when(pl.program_id(0) == 0)
    def _():
        for n in range(2):
            found = [moved(part[n][...], part[2][upper_ref[0]], left=True) for part in parts]
            high, low = split(sum(found[1:], found[0]))
            ordered_ref[: plan.rows, n * plan.ll : (n + 1) * plan.ll] = high
            ordered_ref[plan.tall : plan.tall + plan.rows, n * plan.ll : (n + 1) * plan.ll] = low

    both = [dot(ordered_ref[...], chosen_ref[n]) for n in range(plan.bb)]
    return [b[: plan.rows] + b[plan.tall : plan.tall + plan.rows] for b in both]


def give(plan, upper_ref, made_ref, order_ref, back_ref, own_ref, mirror_ref, sums_ref):
    part = moved(made_ref[0], back_ref[0])
    for n in range(1, plan.bb):
        part = part + moved(made_ref[n], back_ref[n])
    step = pl.program_id(0)

    @pl.when(step == 0)
    def _():
        sums_ref[...] = part

    @pl.when(step > 0)
    def _():
        sums_ref[...] += part

    @pl.when(step == pl.num_programs(0) - 1)
    def _():
        own_ref[...] = moved(sums_ref[:, : plan.ll], order_ref[upper_ref[0]], left=True)
        mirror_ref[...] = moved(sums_ref[:, plan.ll :], order_ref[upper_ref[0]], left=True)


def mix_kernel(
    plan, upper_ref, own_ref, mirror_ref, order_ref, disorder_ref, chosen_ref, back_ref, weight_ref,
    own_out, mirror_out, ordered_ref, made_ref, sums_ref,
):
    wk, quarters = plan.wk, 128 // plan.mx
    picked = pick(plan, upper_ref, [(own_ref, mirror_ref, order_ref)], chosen_ref, ordered_ref)
    place = lax.broadcasted_iota(jnp.int32, (wk, 128), 1) // plan.mx
    for n, modes in enumerate(picked):
        for t in range(plan.c // quarters):
            columns = slice(t * 128, (t + 1) * 128)
            real = imag = 0.0
            for i in range(plan.c):
                x_real, x_imag = modes[i * wk : (i + 1) * wk, :128], modes[i * wk : (i + 1) * wk, 128:]
                w_real, w_imag = weight_ref[n, 0, i, :, columns], weight_ref[n, 1, i, :, columns]
                real = real + (w_real * x_real - w_imag * x_imag)
                imag = imag + (w_real * x_imag + w_imag * x_real)
            for q in range(quarters):
                o = t * quarters + q
                made_ref[n, o * wk : (o + 1) * wk, :128] = jnp.where(place == q, real, 0.0)
                made_ref[n, o * wk : (o + 1) * wk, 128:] = jnp.where(place == q, imag, 0.0)
    give(plan, upper_ref, made_ref, disorder_ref, back_ref, own_out, mirror_out, sums_ref)


def along(plan, modes):
    wk, quarters = plan.wk, 128 // plan.mx
    place = lax.broadcasted_iota(jnp.int32, (wk, 128), 1) // plan.mx
    lined = []
    for t in range(plan.c // quarters):
        real = imag = 0.0
        for q in range(quarters):
            o = t * quarters + q
            real = jnp.where(place == q, modes[o * wk : (o + 1) * wk, :128], real)
            imag = jnp.where(place == q, modes[o * wk : (o + 1) * wk, 128:], imag)
        lined.append((slice(t * 128, (t + 1) * 128), real, imag))
    return lined


def mix_back_kernel(
    plan, upper_ref, own_ref, mirror_ref, order_ref, disorder_ref, chosen_ref, back_ref, weight_ref,
    own_out, mirror_out, ordered_ref, made_ref, sums_ref,
):
    wk = plan.wk
    for n, grads in enumerate(pick(plan, upper_ref, [(own_ref, mirror_ref, order_ref)], chosen_ref, ordered_ref)):
        lined = along(plan, grads)
        for i in range(plan.c):
            back_real = back_imag = 0.0
            for columns, real, imag in lined:
                w_real, w_imag = weight_ref[n, 0, i, :, columns], weight_ref[n, 1, i, :, columns]
                back_real = back_real + (w_real * real + w_imag * imag)
                back_imag = back_imag + (w_real * imag - w_imag * real)
            made_ref[n, i * wk : (i + 1) * wk, :128] = back_real
            made_ref[n, i * wk : (i + 1) * wk, 128:] = back_imag
    give(plan, upper_ref, made_ref, disorder_ref, back_ref, own_out, mirror_out, sums_ref)


def outer_kernel(plan, upper_ref, *refs):
    parts = [refs[:8][2 * m : 2 * m + 2] for m in range(4)]
    orders, chosen_ref, gradient_ref, mode_rows, grad_rows = refs[8:10], refs[10], refs[11], refs[12], refs[13]
    wk = plan.wk
    modes = pick(plan, upper_ref, [(*parts[m], orders[m]) for m in range(2)], chosen_ref, mode_rows)
    grads = pick(plan, upper_ref, [(*parts[2 + m], orders[m]) for m in range(2)], chosen_ref, grad_rows)
    for n in range(plan.bb):
        lined = along(plan, grads[n])
        for i in range(plan.c):
            rows = slice(i * wk, (i + 1) * wk)
            x_real, x_imag = modes[n][rows, :128], modes[n][rows, 128:]
            for columns, real, imag in lined:
                gradient_ref[n, 0, i, :, columns] = real * x_real + imag * x_imag
                gradient_ref[n, 1, i, :, columns] = imag * x_real - real * x_imag


def halve_kernel(flag_ref, keep_ref, arrived_ref, kept_ref, send_ref):
    odd = flag_ref[0] == 1
    for pair in range(kept_ref.shape[0]):
        low = keep_ref[2 * pair] + arrived_ref[2 * pair]
        high = keep_ref[2 * pair + 1] + arrived_ref[2 * pair + 1]
        kept_ref[pair] = jnp.where(odd, high, low)
        send_ref[pair] = jnp.where(odd, low, high)


def cut_kernel(plan, place_ref, keep_ref, arrived_ref, came_ref, *refs):
    out_refs, held_ref = refs[:-1], refs[-1]
    lane = lax.broadcasted_iota(jnp.int32, held_ref.shape[1:], 1)
    real = keep_ref[0, 0] + arrived_ref[0, 0] + came_ref[0, 0]
    imag = keep_ref[0, 1] + arrived_ref[0, 1] + came_ref[0, 1]
    for g in range(plan.s):
        first = pltpu.roll(real, (plan.lp - g * plan.span) % plan.lp, 1)[:, : plan.ll]
        second = pltpu.roll(imag, (plan.lp - g * plan.span + plan.span) % plan.lp, 1)[:, : plan.ll]
        held_ref[g] = jnp.where(lane < plan.span, first, jnp.where(lane < 2 * plan.span, second, 0.0))
    for j, out_ref in enumerate(out_refs):
        out_ref[...] = held_ref[place_ref[3] ^ j]


def join_kernel(plan, slab_ref, *refs):
    piece_refs, total_ref, held_ref = refs[:-2], refs[-2], refs[-1]
    for j, piece_ref in enumerate(piece_refs):
        held_ref[j] = piece_ref[...]
    rows = held_ref.shape[1]
    lane = lax.broadcasted_iota(jnp.int32, (rows, plan.lp), 1)
    real = imag = jnp.zeros((rows, plan.lp), f32)
    blank = jnp.zeros((rows, plan.lp - plan.ll), f32)
    for g in range(plan.s):
        piece = jnp.concatenate([held_ref[slab_ref[0] ^ g], blank], axis=1)
        here = (lane >= g * plan.span) & (lane < (g + 1) * plan.span)
        real = jnp.where(here, pltpu.roll(piece, g * plan.span, 1), real)
        imag = jnp.where(here, pltpu.roll(piece, (g * plan.span - plan.span) % plan.lp, 1), imag)
    total_ref[0, 0] = real
    total_ref[0, 1] = imag


def whole(array):
    zeros = (0,) * array.ndim
    return pl.BlockSpec(array.shape, lambda i: zeros, pipeline_mode=pl.Buffered(1))


def whole_shape(shape):
    zeros = (0,) * len(shape)
    return pl.BlockSpec(shape, lambda i: zeros, pipeline_mode=pl.Buffered(1))


def leading(shape):
    rest = (0,) * (len(shape) - 1)
    return pl.BlockSpec(shape, lambda i: (i,) + rest)


def shaped(*shape):
    return jax.ShapeDtypeStruct(shape, f32)


def anywhere():
    return pl.BlockSpec(memory_space=pl.ANY)


def scalar():
    return pl.BlockSpec(memory_space=pltpu.SMEM)


def call(kernel, name, grid, in_specs, out_specs, out_shape, scratch, cost, before=(), aliases=None):
    skipped = len(before)
    run = pl.pallas_call(
        lambda *refs: kernel(*refs[skipped:]),
        grid=(grid,),
        in_specs=[anywhere()] * skipped + list(in_specs),
        out_specs=out_specs,
        out_shape=out_shape,
        scratch_shapes=scratch,
        name=name,
        input_output_aliases=aliases or {},
        compiler_params=pltpu.CompilerParams(vmem_limit_bytes=VMEM_LIMIT, dimension_semantics=("arbitrary",)),
        cost_estimate=pl.CostEstimate(flops=int(cost * 1.15e9), bytes_accessed=int(cost * 3.6e6), transcendentals=0),
    )
    return partial(run, *before)


def tie(value, *before):
    if not before:
        return value
    return pl.pallas_call(
        lambda *refs: None,
        in_specs=[anywhere()] * (1 + len(before)),
        out_specs=anywhere(),
        out_shape=jax.ShapeDtypeStruct(value.shape, value.dtype),
        input_output_aliases={0: 0},
        name="tie",
    )(value, *before)


class Program:
    def __init__(self, plan):
        self.plan = plan
        self.plane = jnp.asarray(plan.plane_table())
        self.depth = jnp.asarray(plan.depth_forward())
        self.inverse = jnp.asarray(plan.depth_inverse())
        slab, chan = lax.axis_index("slab"), lax.axis_index("chan")
        self.slab, self.chan = slab, chan
        self.turn = jnp.asarray(plan.turns().reshape(-1, 2, plan.lp))
        self.slab_index = slab.astype(jnp.int32).reshape(1)
        self.flag = jnp.stack(
            [chan % 2, chan // 2 % 2, slab * plan.ch + chan, slab, chan // (plan.ch // 2)]
        ).astype(jnp.int32)
        self.upper = (chan >= plan.half).astype(jnp.int32).reshape(1)
        tables = [plan.orders(m) for m in range(plan.chunks)]
        self.order = [jnp.asarray(t) for t in tables]
        self.disorder = [jnp.asarray(np.ascontiguousarray(np.swapaxes(t, 1, 2))) for t in tables]
        chosen, back = plan.selections()
        self.chosen, self.back = jnp.asarray(chosen), jnp.asarray(back)

    def half_shapes(self):
        plan = self.plan
        return [(plan.half, 2, rt, plan.lp) for rt in plan.rts]

    def field_spec(self):
        plan = self.plan
        return leading((plan.xb, plan.c, plan.ny, plan.nz))

    def table(self):
        plan = self.plan
        return leading((1, 3 * plan.blk, 2 * plan.lp))

    def lines(self):
        plan = self.plan
        return pltpu.VMEM((plan.cc, plan.rc, plan.blk), f32)

    def spectra(self):
        plan = self.plan
        rows = pltpu.VMEM((plan.cc * plan.rc, 2 * plan.lp), bf16)
        return [pltpu.VMEM((plan.cc, plan.rc, 2 * plan.lp), f32), rows, rows]

    def analyse(self, values):
        plan = self.plan
        halves = self.half_shapes()
        made = call(
            partial(analyse_kernel, plan), "analyse", plan.nx // plan.xb,
            [scalar(), self.field_spec(), self.table(), whole(self.depth), whole(self.turn)],
            [whole_shape(h) for h in halves * 2], [shaped(*h) for h in halves * 2],
            [self.lines(), self.spectra()[0]], 26,
        )(self.flag, values, self.plane, self.depth, self.turn)
        return made[:2], made[2:]

    def middle(self, groups, linear, cotangent):
        plan = self.plan
        halves = self.half_shapes()
        taken = [part for group in groups for part in group]
        field, spec = shaped(plan.nx, plan.c, plan.ny, plan.nz), self.field_spec()
        modes = [whole_shape(h) for h in halves * 2]
        output, gradient, *made = call(
            partial(middle_kernel, plan), "middle", plan.nx // plan.xb,
            [scalar(), *[whole(t) for t in taken], spec, spec, self.table(), whole(self.depth), whole(self.inverse), whole(self.turn)],
            [spec, spec, *modes], [field, field, *[shaped(*h) for h in halves * 2]],
            [self.lines(), self.lines(), *self.spectra()], 47,
        )(self.flag, *taken, linear, cotangent, self.plane, self.depth, self.inverse, self.turn)
        return output, gradient, made[:2], made[2:]

    def synthesise(self, before, groups, linear):
        plan = self.plan
        taken = [part for group in groups for part in group]
        spec = self.field_spec()
        return call(
            partial(synthesise_kernel, plan), "synthesise", plan.nx // plan.xb,
            [scalar(), *[whole(t) for t in taken], spec, self.table(),
             whole(self.inverse), whole(self.turn)],
            spec, shaped(plan.nx, plan.c, plan.ny, plan.nz),
            [self.lines(), *self.spectra()], 20, before,
        )(self.flag, *taken, linear, self.plane, self.inverse, self.turn)

    def linear(self, half, before, filled, values, matrix, bias):
        plan = self.plan
        bias = bias[None]
        steps = plan.nx // plan.lb // 2
        spec = pl.BlockSpec((plan.lb, plan.c, plan.ny, plan.nz), lambda i: (i + half * steps, 0, 0, 0))
        return call(
            partial(linear_kernel, plan), "linear", steps,
            [spec, whole(matrix), whole(bias)],
            spec, shaped(plan.nx, plan.c, plan.ny, plan.nz), [], 7, (*filled, *before), {0: 0} if filled else None,
        )(values, matrix, bias)

    def mix(self, kernel, name, chunk, before, own, mirror, weights):
        plan = self.plan
        modes = (plan.rts[chunk], plan.ll)
        order, disorder = self.order[chunk], self.disorder[chunk]
        ordered = pltpu.VMEM((2 * plan.tall, 2 * plan.ll), bf16)
        return call(
            partial(kernel, plan), name, plan.wb // plan.bb,
            [
                scalar(), whole_shape(modes), whole_shape(modes), whole(order), whole(disorder),
                leading((plan.bb,) + self.chosen.shape[1:]), leading((plan.bb,) + self.back.shape[1:]),
                leading((plan.bb, *weights.shape[1:])),
            ],
            [whole_shape(modes)] * 2, [shaped(*modes)] * 2,
            [ordered, pltpu.VMEM((plan.bb, plan.rows, 256), f32), pltpu.VMEM((plan.rows, 2 * plan.ll), f32)], 9, before,
        )(self.upper, own, mirror, order, disorder, self.chosen, self.back, weights)

    def outer(self, before, modes, grads, weights):
        plan = self.plan
        parts = [part for pair in (*modes, *grads) for part in pair]
        ordered = pltpu.VMEM((2 * plan.tall, 2 * plan.ll), bf16)
        out = leading((plan.bb, *weights.shape[1:]))
        return call(
            partial(outer_kernel, plan), "outer", plan.wb // plan.bb,
            [scalar(), *[whole(p) for p in parts], *[whole(o) for o in self.order], leading((plan.bb,) + self.chosen.shape[1:])],
            out, shaped(*weights.shape), [ordered, ordered], 9, before,
        )(self.upper, *parts, *self.order, self.chosen)

    def across(self, value, axis, bit):
        size = lax.axis_size(axis)
        return lax.ppermute(value, axis, [(i, i ^ bit) for i in range(size)])

    def mirrored(self, value):
        total = self.plan.s * self.plan.ch
        return lax.ppermute(value, ("slab", "chan"), [(i, total - 1 - i) for i in range(total)])

    def chosen_half(self, kernel, name, grid, in_specs, out_specs, out_shape, scratch, arrays):
        return pl.pallas_call(
            kernel,
            grid_spec=pltpu.PrefetchScalarGridSpec(
                num_scalar_prefetch=1, grid=grid, in_specs=in_specs, out_specs=out_specs, scratch_shapes=scratch
            ),
            out_shape=out_shape,
            name=name,
            compiler_params=pltpu.CompilerParams(vmem_limit_bytes=VMEM_LIMIT, dimension_semantics=("arbitrary",)),
            cost_estimate=pl.CostEstimate(flops=10**9, bytes_accessed=4 * 10**6, transcendentals=0),
        )(self.flag, *arrays)

    def sent_half(self, keep, arrived):
        other = 1 - self.chan // (self.plan.ch // 2)
        return lax.dynamic_index_in_dim(keep, other, 0) + lax.dynamic_index_in_dim(arrived, other, 0)

    def halve(self, keep, arrived, bit):
        mine = ((self.chan // bit) % 2).astype(jnp.int32).reshape(1)
        half = (keep.shape[0] // 2,) + keep.shape[1:]
        return call(
            halve_kernel, "halve", 1, [scalar(), whole(keep), whole(keep)], [whole_shape(half)] * 2,
            [shaped(*half)] * 2, [], 2,
        )(mine, keep, arrived)

    def sums_over_chan(self, keep, arrived, before):
        bit = 2
        while 2 * bit < self.plan.ch:
            keep, sent = self.halve(keep, arrived, bit)
            arrived = self.across(sent, "chan", bit)
            bit *= 2
        sent = tie(self.sent_half(keep, arrived), *before)
        return (keep, arrived), sent, self.across(sent, "chan", bit)

    def cut(self, kept, came):
        plan = self.plan
        size = (came.shape[2], plan.ll)
        block = (1,) + came.shape[1:]
        spec = pl.BlockSpec(block, lambda i, place: (place[4], 0, 0, 0))
        mine, *pieces = self.chosen_half(
            partial(cut_kernel, plan), "cut", (1,), [spec, spec, pl.BlockSpec(block, lambda i, place: (0, 0, 0, 0))],
            [pl.BlockSpec(size, lambda i, place: (0, 0))] * plan.s, [shaped(*size)] * plan.s,
            [pltpu.VMEM((plan.s, *size), f32)], (*kept, came),
        )
        return mine, pieces

    def join(self, mine, arrived):
        plan = self.plan
        total = (1, 2, mine.shape[0], plan.lp)
        return call(
            partial(join_kernel, plan), "join", 1, [scalar()] + [whole(mine)] * plan.s,
            whole_shape(total), shaped(*total), [pltpu.VMEM((plan.s, *mine.shape), f32)], 2,
        )(self.slab_index, mine, *arrived)

    def exchange(self, keeps, sends, mix, fillers):
        def fill(n, value, *before):
            return tie(value, fillers[n](before)) if fillers[n] else value

        plan = self.plan
        first = [self.across(send, "chan", 1) for send in sends]
        keep0, sent0, came0 = self.sums_over_chan(keeps[0], first[0], [])
        came0 = fill(0, came0, sent0, first[1])
        keep1, sent1, came1 = self.sums_over_chan(keeps[1], first[1], [came0])

        mine, pieces = self.cut(keep0, came0)
        arrived = [self.across(piece, "slab", j + 1) for j, piece in enumerate(pieces)]
        for piece in [fill(1, arrived[0], mine, sent1)] + arrived[1:]:
            mine = mine + piece
        own0 = mine
        mirror0 = self.mirrored(own0)
        mine, pieces = self.cut(keep1, tie(came1, own0))
        arrived = [self.across(piece, "slab", j + 1) for j, piece in enumerate(pieces)]
        out0, back0 = mix(0, [mine], own0, mirror0)
        full0 = out0 + self.mirrored(back0)
        for piece in [tie(arrived[0], full0)] + arrived[1:]:
            mine = mine + piece
        own1 = mine
        mirror1 = self.mirrored(own1)

        arrived = [self.across(full0, "slab", j) for j in range(1, plan.s)]
        out1, back1 = mix(1, [full0], own1, mirror1)
        full1 = out1 + self.mirrored(back1)
        total0 = self.join(full0, [tie(arrived[0], back1)] + arrived[1:])
        came0 = self.across(total0, "chan", plan.ch // 2)
        full1 = tie(full1, total0)
        arrived = [self.across(full1, "slab", j) for j in range(1, plan.s)]
        modes = ((own0, mirror0), (own1, mirror1))
        if fillers[2]:
            came0 = tie(came0, fillers[2]([total0], modes))
        total1 = tie(self.join(full1, arrived), came0)
        came1 = self.across(total1, "chan", plan.ch // 2)
        came1 = fill(3, came1, total1)

        groups = []
        for total, other in ((total0, came0), (total1, came1)):
            if groups:
                other = tie(other, *groups[0][2:])
            bit = plan.ch // 2
            while bit > 2:
                upper = (self.chan // bit) % 2 == 1
                total = jnp.stack([jnp.where(upper, other, total), jnp.where(upper, total, other)], axis=1)
                total = total.reshape((-1,) + total.shape[2:])
                bit //= 2
                other = self.across(total, "chan", bit)
            groups.append((total, other, self.across(total, "chan", 1), self.across(other, "chan", 1)))
        return groups, modes


def local(inputs, cotangent, spectral, local_weight, bias_vector):
    nx, ny, channels, nz = inputs.shape
    wb, wk = spectral.shape[0], spectral.shape[1]
    plan = Plan(nx, ny, nz, channels, wb, wk, spectral.shape[4] // channels, lax.axis_size("slab"), lax.axis_size("chan"))
    program = Program(plan)
    values = jnp.transpose(inputs, (0, 2, 1, 3))
    slopes = jnp.transpose(cotangent, (0, 2, 1, 3))
    weights = jnp.transpose(spectral, (0, 2, 3, 1, 4))

    held = {}

    def relaid(before):
        held["weights"] = tie(weights, *before)
        return held["weights"]

    def linear(half, name, values, matrix, bias):
        def run(before):
            filled = [held[name]] if half else []
            held[name] = program.linear(half, before, filled, values, matrix, bias)
            return held[name]

        return run

    def mix(kernel, name):
        return lambda m, before, own, mirror: program.mix(kernel, name, m, before, own, mirror, held["weights"])

    keeps, sends = program.analyse(values)
    there = [linear(half, "linear", values, local_weight.T, bias_vector) for half in range(2)]
    groups, modes = program.exchange(keeps, sends, mix(mix_kernel, "mix"), (relaid, there[0], None, there[1]))
    output, gradient, keeps, sends = program.middle(groups, held["linear"], slopes)

    def outer(before, grads):
        held["outer"] = program.outer(before, modes, grads, weights)
        return held["outer"]

    def placed(before):
        held["outer"] = tie(jnp.transpose(held["outer"], (0, 3, 2, 1, 4)), *before)
        return held["outer"]

    back = [linear(half, "back", gradient, local_weight, jnp.zeros_like(bias_vector)) for half in range(2)]
    groups, _ = program.exchange(
        keeps, sends, mix(mix_back_kernel, "mix_back"), (back[0], back[1], outer, placed)
    )
    grad_inputs = program.synthesise([], groups, held["back"])
    grad_spectral = held["outer"]
    return (
        jnp.transpose(output, (0, 2, 1, 3)),
        jnp.transpose(grad_inputs, (0, 2, 1, 3)),
        jnp.transpose(grad_spectral, (0, 1, 3, 2, 4)),
    )


def solution(mesh):
    in_specs = (
        P(("groups", "slab"), "chan", None, None),
        P(("groups", "slab"), "chan", None, None),
        P("slab", "chan", None, None, None),
        P(),
        P(),
    )
    out_specs = (
        P(("groups", "slab"), "chan", None, None),
        P(("groups", "slab"), "chan", None, None),
        P(("groups", "slab"), "chan", None, None, None),
    )
    return jax.shard_map(local, mesh=mesh, in_specs=in_specs, out_specs=out_specs, check_vma=False)
```

```python
from functools import partial
import math

import jax
import jax.numpy as jnp
import ml_dtypes
import numpy as np
from jax import lax
from jax.experimental import pallas as pl
from jax.experimental.pallas import tpu as pltpu
from jax.sharding import PartitionSpec as P

f32 = jnp.float32
bf16 = jnp.bfloat16
root_half = 0.7071067811865476
inv_root_two_pi = 0.3989422804014327
VMEM_LIMIT = 64 * 1024 * 1024
NT = (((1,), (1,)), ((), ()))
TN = (((0,), (0,)), ((), ()))


def round_up(value, unit):
    return -(-value // unit) * unit


class Plan:
    def __init__(self, nx, ny, nz, channels, wb, wk, mx, slab_count, chan_count):
        self.nx, self.ny, self.nz, self.c = nx, ny, nz, channels
        self.wb, self.wk, self.mx = wb, wk, mx
        self.s, self.ch = slab_count, chan_count
        self.half = chan_count // 2
        self.na = mx // 2 + 1
        self.span = (wb + 1) * self.na
        self.lw = slab_count * self.span
        self.lp = round_up(self.lw, 128)
        self.ll = round_up(2 * self.span, 128)
        self.mk = self.half * wk
        self.rc = round_up(2 * self.mk + 2 * self.half, 8)
        self.chunks = 2
        self.cc = channels
        self.w = (wk // 2, wk - wk // 2)
        self.rts = (round_up(channels * self.w[0], 8), round_up(channels * (self.w[1] + 1), 8))
        self.xb = math.gcd(8, nx)
        self.blk = self.xb * ny
        self.rows = self.cc * wk
        self.tall = round_up(self.rows, 16)
        self.bb = math.gcd(4, wb)
        self.lb = math.gcd(4, nx // 2)
        self.batch = max(d for d in range(1, 11) if self.cc % d == 0)
        self.full_x, self.full_y = nx * slab_count, ny * chan_count

    def segments(self, c):
        w0, w1 = self.w
        main = lambda first: lambda h, kind: kind * self.mk + h * self.wk + first
        return (
            (0, c * w0, w0, main(0)),
            (1, c * w1, w1, main(w0)),
            (1, self.c * w1 + c, 1, lambda h, kind: 2 * self.mk + kind * self.half + h),
        )

    def starts(self):
        kept = self.wb * self.s
        return [g * self.wb - (kept if 2 * g >= self.s else 0) for g in range(self.s)]

    def columns(self):
        b = np.concatenate([np.repeat(np.arange(st, st + self.wb + 1), self.na) for st in self.starts()])
        a = np.tile(np.arange(self.na), self.s * (self.wb + 1))
        return a, b

    def plane_table(self):
        a, b = self.columns()
        x = np.repeat(np.arange(self.nx), self.ny)[:, None]
        y = np.tile(np.arange(self.ny), self.nx)[:, None]
        total = self.full_x * self.full_y
        phase = (a * x * self.full_y + b * y * self.full_x) % total * (2.0 * np.pi / total)
        table = np.zeros((self.nx * self.ny, 2 * self.lp))
        scale = 1.0 / math.sqrt(total)
        table[:, : self.lw] = np.cos(phase) * scale
        table[:, self.lp : self.lp + self.lw] = -np.sin(phase) * scale
        high, low = (t.reshape(self.nx // self.xb, 1, self.blk, 2 * self.lp) for t in halves(table))
        return np.concatenate([high, high, low], 1).reshape(-1, 3 * self.blk, 2 * self.lp)

    def turns(self):
        a, b = self.columns()
        x = (np.arange(self.s) * self.nx)[:, None, None]
        y = (np.arange(self.ch) * self.ny)[None, :, None]
        total = self.full_x * self.full_y
        phase = (a * x * self.full_y + b * y * self.full_x) % total * (2.0 * np.pi / total)
        table = np.zeros((self.s, self.ch, 2, self.lp), np.float32)
        table[:, :, 0, : self.lw] = np.cos(phase)
        table[:, :, 1, : self.lw] = np.sin(phase)
        return table

    def depth_rows(self):
        main = np.arange(self.mk)
        edge = (np.arange(self.half) + 1) * self.wk
        z = np.arange(self.nz)
        scale = 1.0 / math.sqrt(self.nz)
        angle = lambda k: (k[:, None] * z) % self.nz * (2.0 * np.pi / self.nz)
        rows = [np.cos(angle(main)), np.sin(angle(main)), np.cos(angle(edge)), np.sin(angle(edge))]
        table = np.zeros((self.rc, self.nz))
        table[: 2 * self.mk + 2 * self.half] = np.concatenate(rows) * scale
        return halves(table)

    def depth_forward(self):
        high, low = self.depth_rows()
        return np.concatenate(
            [np.concatenate([high, high], 1), np.concatenate([low, np.zeros_like(low)], 1)], 0
        )

    def depth_inverse(self):
        high, low = self.depth_rows()
        table = np.zeros((round_up(3 * self.rc, 16), self.nz), ml_dtypes.bfloat16)
        table[: 3 * self.rc] = np.concatenate([high, high, low], 0)
        return table

    def selections(self):
        quarters = 128 // self.mx
        own = np.zeros((self.wb, 2, self.ll, 2, quarters, self.mx), np.float32)
        for b in range(self.wb):
            for r in range(2):
                for a in range(self.mx):
                    if a < self.mx // 2:
                        own[b, 0, r * self.span + b * self.na + a, r, :, a] = 1.0
                    else:
                        spot = r * self.span + (self.wb - b) * self.na + self.mx - a
                        own[b, 1, spot, r, :, a] = 1.0 - 2.0 * r
        own = own.reshape(self.wb, 2 * self.ll, 256)
        back = np.swapaxes(own, 1, 2)
        return own.astype(ml_dtypes.bfloat16), np.ascontiguousarray(back).astype(ml_dtypes.bfloat16)

    def orders(self, chunk):
        w0, w1 = self.w
        table = np.zeros((2, self.rows, self.rts[chunk]), np.float32)
        for c in range(self.c):
            for k in range(self.wk):
                for upper, index in enumerate((k, self.wk - k)):
                    if index < w0:
                        here, spot = 0, c * w0 + index
                    elif index < self.wk:
                        here, spot = 1, c * w1 + index - w0
                    else:
                        here, spot = 1, self.c * w1 + c
                    if here == chunk:
                        table[upper, c * self.wk + k, spot] = 1.0
        return table.astype(ml_dtypes.bfloat16)


def halves(table):
    high = table.astype(np.float32).astype(ml_dtypes.bfloat16)
    low = (table - high.astype(np.float64)).astype(np.float32).astype(ml_dtypes.bfloat16)
    return high, low


def dot(left, right, numbers=(((1,), (0,)), ((), ()))):
    return lax.dot_general(left, right, numbers, preferred_element_type=f32)


def split(value):
    high = value.astype(bf16)
    return high, (value - high.astype(f32)).astype(bf16)


def moved(value, chosen, left=False):
    first, second = split(value)
    if left:
        return dot(chosen, first) + dot(chosen, second)
    rows = value.shape[0]
    if rows % 16:
        return dot(first, chosen) + dot(second, chosen)
    both = dot(jnp.concatenate([first, second], axis=0), chosen)
    return both[:rows] + both[rows:]


def depth_analysis(plan, table_ref, values):
    rows = []
    for value in values:
        high, low = split(value)
        rows.append(jnp.concatenate([high, low], axis=1))
    both = dot(table_ref[...], jnp.concatenate(rows, axis=0), NT)
    lines = both[: plan.rc] + both[plan.rc :]
    return [lines[:, j * plan.blk : (j + 1) * plan.blk] for j in range(len(values))]


def depth_synthesis(plan, table_ref, rows):
    high = rows.astype(bf16).astype(f32)
    parts = [high, rows - high, high]
    extra = table_ref.shape[0] - 3 * plan.rc
    if extra:
        parts.append(jnp.zeros((extra, rows.shape[1]), f32))
    return dot(jnp.concatenate(parts, axis=0).astype(bf16), table_ref[...], TN)


def plane_analysis(plan, step, lines_ref, plane_ref, total_ref):
    high, low = split(lines_ref[...].reshape(plan.cc * plan.rc, plan.blk))
    rows = jnp.concatenate([high, low, high], axis=1)
    for start in range(0, 2 * plan.lp, 256):
        size = min(256, 2 * plan.lp - start)
        columns = pl.ds(start, size)
        part = dot(rows, plane_ref[0, :, columns]).reshape(plan.cc, plan.rc, size)

        @pl.when(step == 0)
        def _():
            total_ref[:, :, columns] = part

        @pl.when(step > 0)
        def _():
            total_ref[:, :, columns] += part


def plane_synthesis(plan, high_rows, low_rows, plane_ref, lines_ref):
    high_table, low_table = plane_ref[0, : plan.blk], plane_ref[0, 2 * plan.blk :]
    lines = (
        dot(high_rows[...], high_table, NT)
        + dot(low_rows[...], high_table, NT)
        + dot(high_rows[...], low_table, NT)
    )
    lines_ref[...] = lines.reshape(plan.cc, plan.rc, plan.blk)


def emit_modes(plan, flag_ref, turn_ref, total_ref, keep_refs, send_refs):
    lp, half = plan.lp, plan.half
    odd = flag_ref[0] == 1
    cosine, sine = turn_ref[flag_ref[2], 0:1, :], turn_ref[flag_ref[2], 1:2, :]
    for c in range(plan.c):
        real, imag = total_ref[c, :, :lp], total_ref[c, :, lp:]
        real, imag = real * cosine + imag * sine, imag * cosine - real * sine
        for m, base, size, place in plan.segments(c):
            made = []
            for g in range(plan.ch):
                h = g if g < half else plan.ch - 1 - g
                even, odd_rows = (slice(place(h, kind), place(h, kind) + size) for kind in (0, 1))
                if g < half:
                    made.append((real[even] + imag[odd_rows], imag[even] - real[odd_rows]))
                else:
                    made.append((real[even] - imag[odd_rows], imag[even] + real[odd_rows]))
            for pair in range(half):
                for r in range(2):
                    low, high = made[2 * pair][r], made[2 * pair + 1][r]
                    keep_refs[m][pair, r, base : base + size, :] = jnp.where(odd, high, low)
                    send_refs[m][pair, r, base : base + size, :] = jnp.where(odd, low, high)
    for m, used in enumerate((plan.c * plan.w[0], plan.c * (plan.w[1] + 1))):
        if used < plan.rts[m]:
            blank = jnp.zeros((half, 2, plan.rts[m] - used, lp), f32)
            keep_refs[m][:, :, used:, :] = blank
            send_refs[m][:, :, used:, :] = blank


def take_modes(plan, flag_ref, turn_ref, group_refs, total_ref, high_rows, low_rows):
    lp, half = plan.lp, plan.half
    odd, upper = flag_ref[0] == 1, flag_ref[1] == 1
    cosine, sine = turn_ref[flag_ref[2], 0:1, :], turn_ref[flag_ref[2], 1:2, :]

    def group(m, g, r, rows):
        here, there, core_here, core_there = (ref[g // 4, r, rows, :] for ref in group_refs[m])
        first, second = ((here, there), (core_here, core_there)) if g % 2 else ((core_here, core_there), (here, there))
        held, came = (jnp.where(odd, a, b) for a, b in zip(first, second))
        return jnp.where(upper, held, came) if g // 2 % 2 else jnp.where(upper, came, held)

    for c in range(plan.c):
        for m, base, size, place in plan.segments(c):
            rows = slice(base, base + size)
            for h in range(half):
                plus = [group(m, h, r, rows) for r in range(2)]
                minus = [group(m, plan.ch - 1 - h, r, rows) for r in range(2)]
                real, imag = plus[0] + minus[0], plus[1] + minus[1]
                here = slice(place(h, 0), place(h, 0) + size)
                total_ref[c, here, :lp] = real * cosine - imag * sine
                total_ref[c, here, lp:] = imag * cosine + real * sine
                real, imag = plus[0] - minus[0], plus[1] - minus[1]
                here = slice(place(h, 1), place(h, 1) + size)
                total_ref[c, here, :lp] = -(imag * cosine + real * sine)
                total_ref[c, here, lp:] = real * cosine - imag * sine
        used = 2 * plan.mk + 2 * half
        if used < plan.rc:
            total_ref[c, used:, :] = jnp.zeros((plan.rc - used, 2 * lp), f32)
    high, low = split(total_ref[...].reshape(plan.c * plan.rc, 2 * lp))
    high_rows[...] = high
    low_rows[...] = low


def analyse_kernel(plan, flag_ref, values_ref, plane_ref, depth_ref, turn_ref, *refs):
    keep_refs, send_refs, (lines_ref, total_ref) = refs[:2], refs[2:4], refs[4:]
    step = pl.program_id(0)

    @pl.loop(0, plan.cc, step=plan.batch)
    def _(c):
        values = [values_ref[:, c + j].reshape(plan.blk, plan.nz) for j in range(plan.batch)]
        for j, lines in enumerate(depth_analysis(plan, depth_ref, values)):
            lines_ref[c + j] = lines

    plane_analysis(plan, step, lines_ref, plane_ref, total_ref)

    @pl.when(step == pl.num_programs(0) - 1)
    def _():
        emit_modes(plan, flag_ref, turn_ref, total_ref, keep_refs, send_refs)


def fields(plan, inverse_ref, lines_ref, first):
    lines = jnp.concatenate([lines_ref[first + j] for j in range(plan.batch)], axis=1)
    values = depth_synthesis(plan, inverse_ref, lines)
    return [values[j * plan.blk : (j + 1) * plan.blk] for j in range(plan.batch)]


def middle_kernel(plan, flag_ref, *refs):
    group_refs, refs = (refs[:4], refs[4:8]), refs[8:]
    linear_ref, cotangent_ref, plane_ref, depth_ref, inverse_ref, turn_ref, output_ref, gradient_ref = refs[:8]
    keep_refs, send_refs, (lines_ref, back_ref, total_ref, high_rows, low_rows) = refs[8:10], refs[10:12], refs[12:]
    step = pl.program_id(0)

    @pl.when(step == 0)
    def _():
        take_modes(plan, flag_ref, turn_ref, group_refs, total_ref, high_rows, low_rows)

    plane_synthesis(plan, high_rows, low_rows, plane_ref, lines_ref)
    shape = (plan.xb, plan.ny, plan.nz)

    @pl.loop(0, plan.cc, step=plan.batch)
    def _(first):
        gradients = []
        for j, field in enumerate(fields(plan, inverse_ref, lines_ref, first)):
            value = field + linear_ref[:, first + j].reshape(plan.blk, plan.nz)
            gate = 0.5 * (1.0 + lax.erf(value * root_half))
            slope = gate + value * jnp.exp(-0.5 * value * value) * inv_root_two_pi
            output_ref[:, first + j] = (value * gate).reshape(shape)
            gradients.append(cotangent_ref[:, first + j].reshape(plan.blk, plan.nz) * slope)
            gradient_ref[:, first + j] = gradients[-1].reshape(shape)
        for j, lines in enumerate(depth_analysis(plan, depth_ref, gradients)):
            back_ref[first + j] = lines

    plane_analysis(plan, step, back_ref, plane_ref, total_ref)

    @pl.when(step == pl.num_programs(0) - 1)
    def _():
        emit_modes(plan, flag_ref, turn_ref, total_ref, keep_refs, send_refs)


def synthesise_kernel(plan, flag_ref, *refs):
    group_refs, refs = (refs[:4], refs[4:8]), refs[8:]
    linear_ref, plane_ref, inverse_ref, turn_ref, output_ref, lines_ref, total_ref, high_rows, low_rows = refs

    @pl.when(pl.program_id(0) == 0)
    def _():
        take_modes(plan, flag_ref, turn_ref, group_refs, total_ref, high_rows, low_rows)

    plane_synthesis(plan, high_rows, low_rows, plane_ref, lines_ref)

    @pl.loop(0, plan.cc, step=plan.batch)
    def _(first):
        for j, field in enumerate(fields(plan, inverse_ref, lines_ref, first)):
            value = field + linear_ref[:, first + j].reshape(plan.blk, plan.nz)
            output_ref[:, first + j] = value.reshape(plan.xb, plan.ny, plan.nz)


def linear_kernel(plan, values_ref, weight_ref, bias_ref, output_ref):
    tiles = [(x, slice(t * 8, (t + 1) * 8)) for x in range(plan.lb) for t in range(plan.ny // 8)]
    values = [values_ref[x, :, t, :].reshape(plan.c * 8, plan.nz) for x, t in tiles]
    high, low = split(jnp.concatenate(values, axis=1))
    size = 8 * plan.c
    row, column = (lax.broadcasted_iota(jnp.int32, (size, plan.c), n) for n in (0, 1))
    repeat = (row // 8 == column).astype(f32)
    exact = partial(lax.dot_general, precision=lax.Precision.HIGHEST, preferred_element_type=f32)
    spread = exact(exact(repeat, weight_ref[...], (((1,), (0,)), ((), ()))), repeat, NT)
    row, column = (lax.broadcasted_iota(jnp.int32, (size, size), n) for n in (0, 1))
    high_matrix, low_matrix = split(jnp.where(row % 8 == column % 8, spread, 0.0))
    bias = exact(repeat, bias_ref[...], (((1,), (1,)), ((), ())))
    matrix = jnp.concatenate([high_matrix, high_matrix, low_matrix], axis=1)
    mixed = dot(matrix, jnp.concatenate([high, low, high], axis=0)) + bias
    for n, (x, t) in enumerate(tiles):
        output_ref[x, :, t, :] = mixed[:, n * plan.nz : (n + 1) * plan.nz].reshape(plan.c, 8, plan.nz)


def pick(plan, upper_ref, parts, chosen_ref, ordered_ref):
    @pl.when(pl.program_id(0) == 0)
    def _():
        for n in range(2):
            found = [moved(part[n][...], part[2][upper_ref[0]], left=True) for part in parts]
            high, low = split(sum(found[1:], found[0]))
            ordered_ref[: plan.rows, n * plan.ll : (n + 1) * plan.ll] = high
            ordered_ref[plan.tall : plan.tall + plan.rows, n * plan.ll : (n + 1) * plan.ll] = low

    both = [dot(ordered_ref[...], chosen_ref[n]) for n in range(plan.bb)]
    return [b[: plan.rows] + b[plan.tall : plan.tall + plan.rows] for b in both]


def give(plan, upper_ref, made_ref, order_ref, back_ref, own_ref, mirror_ref, sums_ref):
    part = moved(made_ref[0], back_ref[0])
    for n in range(1, plan.bb):
        part = part + moved(made_ref[n], back_ref[n])
    step = pl.program_id(0)

    @pl.when(step == 0)
    def _():
        sums_ref[...] = part

    @pl.when(step > 0)
    def _():
        sums_ref[...] += part

    @pl.when(step == pl.num_programs(0) - 1)
    def _():
        own_ref[...] = moved(sums_ref[:, : plan.ll], order_ref[upper_ref[0]], left=True)
        mirror_ref[...] = moved(sums_ref[:, plan.ll :], order_ref[upper_ref[0]], left=True)


def mix_kernel(
    plan, upper_ref, own_ref, mirror_ref, order_ref, disorder_ref, chosen_ref, back_ref, weight_ref,
    own_out, mirror_out, ordered_ref, made_ref, sums_ref,
):
    wk, quarters = plan.wk, 128 // plan.mx
    picked = pick(plan, upper_ref, [(own_ref, mirror_ref, order_ref)], chosen_ref, ordered_ref)
    place = lax.broadcasted_iota(jnp.int32, (wk, 128), 1) // plan.mx
    for n, modes in enumerate(picked):
        for t in range(plan.c // quarters):
            columns = slice(t * 128, (t + 1) * 128)
            real = imag = 0.0
            for i in range(plan.c):
                x_real, x_imag = modes[i * wk : (i + 1) * wk, :128], modes[i * wk : (i + 1) * wk, 128:]
                w_real, w_imag = weight_ref[n, 0, i, :, columns], weight_ref[n, 1, i, :, columns]
                real = real + (w_real * x_real - w_imag * x_imag)
                imag = imag + (w_real * x_imag + w_imag * x_real)
            for q in range(quarters):
                o = t * quarters + q
                made_ref[n, o * wk : (o + 1) * wk, :128] = jnp.where(place == q, real, 0.0)
                made_ref[n, o * wk : (o + 1) * wk, 128:] = jnp.where(place == q, imag, 0.0)
    give(plan, upper_ref, made_ref, disorder_ref, back_ref, own_out, mirror_out, sums_ref)


def along(plan, modes):
    wk, quarters = plan.wk, 128 // plan.mx
    place = lax.broadcasted_iota(jnp.int32, (wk, 128), 1) // plan.mx
    lined = []
    for t in range(plan.c // quarters):
        real = imag = 0.0
        for q in range(quarters):
            o = t * quarters + q
            real = jnp.where(place == q, modes[o * wk : (o + 1) * wk, :128], real)
            imag = jnp.where(place == q, modes[o * wk : (o + 1) * wk, 128:], imag)
        lined.append((slice(t * 128, (t + 1) * 128), real, imag))
    return lined


def mix_back_kernel(
    plan, upper_ref, own_ref, mirror_ref, order_ref, disorder_ref, chosen_ref, back_ref, weight_ref,
    own_out, mirror_out, ordered_ref, made_ref, sums_ref,
):
    wk = plan.wk
    for n, grads in enumerate(pick(plan, upper_ref, [(own_ref, mirror_ref, order_ref)], chosen_ref, ordered_ref)):
        lined = along(plan, grads)
        for i in range(plan.c):
            back_real = back_imag = 0.0
            for columns, real, imag in lined:
                w_real, w_imag = weight_ref[n, 0, i, :, columns], weight_ref[n, 1, i, :, columns]
                back_real = back_real + (w_real * real + w_imag * imag)
                back_imag = back_imag + (w_real * imag - w_imag * real)
            made_ref[n, i * wk : (i + 1) * wk, :128] = back_real
            made_ref[n, i * wk : (i + 1) * wk, 128:] = back_imag
    give(plan, upper_ref, made_ref, disorder_ref, back_ref, own_out, mirror_out, sums_ref)


def outer_kernel(plan, upper_ref, *refs):
    parts = [refs[:8][2 * m : 2 * m + 2] for m in range(4)]
    orders, chosen_ref, gradient_ref, mode_rows, grad_rows = refs[8:10], refs[10], refs[11], refs[12], refs[13]
    wk = plan.wk
    modes = pick(plan, upper_ref, [(*parts[m], orders[m]) for m in range(2)], chosen_ref, mode_rows)
    grads = pick(plan, upper_ref, [(*parts[2 + m], orders[m]) for m in range(2)], chosen_ref, grad_rows)
    for n in range(plan.bb):
        lined = along(plan, grads[n])
        for i in range(plan.c):
            rows = slice(i * wk, (i + 1) * wk)
            x_real, x_imag = modes[n][rows, :128], modes[n][rows, 128:]
            for columns, real, imag in lined:
                gradient_ref[n, 0, i, :, columns] = real * x_real + imag * x_imag
                gradient_ref[n, 1, i, :, columns] = imag * x_real - real * x_imag


def halve_kernel(flag_ref, keep_ref, arrived_ref, kept_ref, send_ref):
    odd = flag_ref[0] == 1
    for pair in range(kept_ref.shape[0]):
        low = keep_ref[2 * pair] + arrived_ref[2 * pair]
        high = keep_ref[2 * pair + 1] + arrived_ref[2 * pair + 1]
        kept_ref[pair] = jnp.where(odd, high, low)
        send_ref[pair] = jnp.where(odd, low, high)


def cut_kernel(plan, place_ref, keep_ref, arrived_ref, came_ref, *refs):
    out_refs, held_ref = refs[:-1], refs[-1]
    lane = lax.broadcasted_iota(jnp.int32, held_ref.shape[1:], 1)
    real = keep_ref[0, 0] + arrived_ref[0, 0] + came_ref[0, 0]
    imag = keep_ref[0, 1] + arrived_ref[0, 1] + came_ref[0, 1]
    for g in range(plan.s):
        first = pltpu.roll(real, (plan.lp - g * plan.span) % plan.lp, 1)[:, : plan.ll]
        second = pltpu.roll(imag, (plan.lp - g * plan.span + plan.span) % plan.lp, 1)[:, : plan.ll]
        held_ref[g] = jnp.where(lane < plan.span, first, jnp.where(lane < 2 * plan.span, second, 0.0))
    for j, out_ref in enumerate(out_refs):
        out_ref[...] = held_ref[place_ref[3] ^ j]


def join_kernel(plan, slab_ref, *refs):
    piece_refs, total_ref, held_ref = refs[:-2], refs[-2], refs[-1]
    for j, piece_ref in enumerate(piece_refs):
        held_ref[j] = piece_ref[...]
    rows = held_ref.shape[1]
    lane = lax.broadcasted_iota(jnp.int32, (rows, plan.lp), 1)
    real = imag = jnp.zeros((rows, plan.lp), f32)
    blank = jnp.zeros((rows, plan.lp - plan.ll), f32)
    for g in range(plan.s):
        piece = jnp.concatenate([held_ref[slab_ref[0] ^ g], blank], axis=1)
        here = (lane >= g * plan.span) & (lane < (g + 1) * plan.span)
        real = jnp.where(here, pltpu.roll(piece, g * plan.span, 1), real)
        imag = jnp.where(here, pltpu.roll(piece, (g * plan.span - plan.span) % plan.lp, 1), imag)
    total_ref[0, 0] = real
    total_ref[0, 1] = imag


def whole(array):
    zeros = (0,) * array.ndim
    return pl.BlockSpec(array.shape, lambda i: zeros, pipeline_mode=pl.Buffered(1))


def whole_shape(shape):
    zeros = (0,) * len(shape)
    return pl.BlockSpec(shape, lambda i: zeros, pipeline_mode=pl.Buffered(1))


def leading(shape):
    rest = (0,) * (len(shape) - 1)
    return pl.BlockSpec(shape, lambda i: (i,) + rest)


def shaped(*shape):
    return jax.ShapeDtypeStruct(shape, f32)


def anywhere():
    return pl.BlockSpec(memory_space=pl.ANY)


def scalar():
    return pl.BlockSpec(memory_space=pltpu.SMEM)


def call(kernel, name, grid, in_specs, out_specs, out_shape, scratch, cost, before=(), aliases=None):
    skipped = len(before)
    run = pl.pallas_call(
        lambda *refs: kernel(*refs[skipped:]),
        grid=(grid,),
        in_specs=[anywhere()] * skipped + list(in_specs),
        out_specs=out_specs,
        out_shape=out_shape,
        scratch_shapes=scratch,
        name=name,
        input_output_aliases=aliases or {},
        compiler_params=pltpu.CompilerParams(vmem_limit_bytes=VMEM_LIMIT, dimension_semantics=("arbitrary",)),
        cost_estimate=pl.CostEstimate(flops=int(cost * 1.15e9), bytes_accessed=int(cost * 3.6e6), transcendentals=0),
    )
    return partial(run, *before)


def tie(value, *before):
    if not before:
        return value
    return pl.pallas_call(
        lambda *refs: None,
        in_specs=[anywhere()] * (1 + len(before)),
        out_specs=anywhere(),
        out_shape=jax.ShapeDtypeStruct(value.shape, value.dtype),
        input_output_aliases={0: 0},
        name="tie",
    )(value, *before)


class Program:
    def __init__(self, plan):
        self.plan = plan
        self.plane = jnp.asarray(plan.plane_table())
        self.depth = jnp.asarray(plan.depth_forward())
        self.inverse = jnp.asarray(plan.depth_inverse())
        slab, chan = lax.axis_index("slab"), lax.axis_index("chan")
        self.slab, self.chan = slab, chan
        self.turn = jnp.asarray(plan.turns().reshape(-1, 2, plan.lp))
        self.slab_index = slab.astype(jnp.int32).reshape(1)
        self.flag = jnp.stack(
            [chan % 2, chan // 2 % 2, slab * plan.ch + chan, slab, chan // (plan.ch // 2)]
        ).astype(jnp.int32)
        self.upper = (chan >= plan.half).astype(jnp.int32).reshape(1)
        tables = [plan.orders(m) for m in range(plan.chunks)]
        self.order = [jnp.asarray(t) for t in tables]
        self.disorder = [jnp.asarray(np.ascontiguousarray(np.swapaxes(t, 1, 2))) for t in tables]
        chosen, back = plan.selections()
        self.chosen, self.back = jnp.asarray(chosen), jnp.asarray(back)

    def half_shapes(self):
        plan = self.plan
        return [(plan.half, 2, rt, plan.lp) for rt in plan.rts]

    def field_spec(self):
        plan = self.plan
        return leading((plan.xb, plan.c, plan.ny, plan.nz))

    def table(self):
        plan = self.plan
        return leading((1, 3 * plan.blk, 2 * plan.lp))

    def lines(self):
        plan = self.plan
        return pltpu.VMEM((plan.cc, plan.rc, plan.blk), f32)

    def spectra(self):
        plan = self.plan
        rows = pltpu.VMEM((plan.cc * plan.rc, 2 * plan.lp), bf16)
        return [pltpu.VMEM((plan.cc, plan.rc, 2 * plan.lp), f32), rows, rows]

    def analyse(self, values):
        plan = self.plan
        halves = self.half_shapes()
        made = call(
            partial(analyse_kernel, plan), "analyse", plan.nx // plan.xb,
            [scalar(), self.field_spec(), self.table(), whole(self.depth), whole(self.turn)],
            [whole_shape(h) for h in halves * 2], [shaped(*h) for h in halves * 2],
            [self.lines(), self.spectra()[0]], 26,
        )(self.flag, values, self.plane, self.depth, self.turn)
        return made[:2], made[2:]

    def middle(self, groups, linear, cotangent):
        plan = self.plan
        halves = self.half_shapes()
        taken = [part for group in groups for part in group]
        field, spec = shaped(plan.nx, plan.c, plan.ny, plan.nz), self.field_spec()
        modes = [whole_shape(h) for h in halves * 2]
        output, gradient, *made = call(
            partial(middle_kernel, plan), "middle", plan.nx // plan.xb,
            [scalar(), *[whole(t) for t in taken], spec, spec, self.table(), whole(self.depth), whole(self.inverse), whole(self.turn)],
            [spec, spec, *modes], [field, field, *[shaped(*h) for h in halves * 2]],
            [self.lines(), self.lines(), *self.spectra()], 47,
        )(self.flag, *taken, linear, cotangent, self.plane, self.depth, self.inverse, self.turn)
        return output, gradient, made[:2], made[2:]

    def synthesise(self, before, groups, linear):
        plan = self.plan
        taken = [part for group in groups for part in group]
        spec = self.field_spec()
        return call(
            partial(synthesise_kernel, plan), "synthesise", plan.nx // plan.xb,
            [scalar(), *[whole(t) for t in taken], spec, self.table(),
             whole(self.inverse), whole(self.turn)],
            spec, shaped(plan.nx, plan.c, plan.ny, plan.nz),
            [self.lines(), *self.spectra()], 20, before,
        )(self.flag, *taken, linear, self.plane, self.inverse, self.turn)

    def linear(self, half, before, filled, values, matrix, bias):
        plan = self.plan
        bias = bias[None]
        steps = plan.nx // plan.lb // 2
        spec = pl.BlockSpec((plan.lb, plan.c, plan.ny, plan.nz), lambda i: (i + half * steps, 0, 0, 0))
        return call(
            partial(linear_kernel, plan), "linear", steps,
            [spec, whole(matrix), whole(bias)],
            spec, shaped(plan.nx, plan.c, plan.ny, plan.nz), [], 7, (*filled, *before), {0: 0} if filled else None,
        )(values, matrix, bias)

    def mix(self, kernel, name, chunk, before, own, mirror, weights):
        plan = self.plan
        modes = (plan.rts[chunk], plan.ll)
        order, disorder = self.order[chunk], self.disorder[chunk]
        ordered = pltpu.VMEM((2 * plan.tall, 2 * plan.ll), bf16)
        return call(
            partial(kernel, plan), name, plan.wb // plan.bb,
            [
                scalar(), whole_shape(modes), whole_shape(modes), whole(order), whole(disorder),
                leading((plan.bb,) + self.chosen.shape[1:]), leading((plan.bb,) + self.back.shape[1:]),
                leading((plan.bb, *weights.shape[1:])),
            ],
            [whole_shape(modes)] * 2, [shaped(*modes)] * 2,
            [ordered, pltpu.VMEM((plan.bb, plan.rows, 256), f32), pltpu.VMEM((plan.rows, 2 * plan.ll), f32)], 9, before,
        )(self.upper, own, mirror, order, disorder, self.chosen, self.back, weights)

    def outer(self, before, modes, grads, weights):
        plan = self.plan
        parts = [part for pair in (*modes, *grads) for part in pair]
        ordered = pltpu.VMEM((2 * plan.tall, 2 * plan.ll), bf16)
        out = leading((plan.bb, *weights.shape[1:]))
        return call(
            partial(outer_kernel, plan), "outer", plan.wb // plan.bb,
            [scalar(), *[whole(p) for p in parts], *[whole(o) for o in self.order], leading((plan.bb,) + self.chosen.shape[1:])],
            out, shaped(*weights.shape), [ordered, ordered], 9, before,
        )(self.upper, *parts, *self.order, self.chosen)

    def across(self, value, axis, bit):
        size = lax.axis_size(axis)
        return lax.ppermute(value, axis, [(i, i ^ bit) for i in range(size)])

    def mirrored(self, value):
        total = self.plan.s * self.plan.ch
        return lax.ppermute(value, ("slab", "chan"), [(i, total - 1 - i) for i in range(total)])

    def chosen_half(self, kernel, name, grid, in_specs, out_specs, out_shape, scratch, arrays):
        return pl.pallas_call(
            kernel,
            grid_spec=pltpu.PrefetchScalarGridSpec(
                num_scalar_prefetch=1, grid=grid, in_specs=in_specs, out_specs=out_specs, scratch_shapes=scratch
            ),
            out_shape=out_shape,
            name=name,
            compiler_params=pltpu.CompilerParams(vmem_limit_bytes=VMEM_LIMIT, dimension_semantics=("arbitrary",)),
            cost_estimate=pl.CostEstimate(flops=10**9, bytes_accessed=4 * 10**6, transcendentals=0),
        )(self.flag, *arrays)

    def sent_half(self, keep, arrived):
        other = 1 - self.chan // (self.plan.ch // 2)
        return lax.dynamic_index_in_dim(keep, other, 0) + lax.dynamic_index_in_dim(arrived, other, 0)

    def halve(self, keep, arrived, bit):
        mine = ((self.chan // bit) % 2).astype(jnp.int32).reshape(1)
        half = (keep.shape[0] // 2,) + keep.shape[1:]
        return call(
            halve_kernel, "halve", 1, [scalar(), whole(keep), whole(keep)], [whole_shape(half)] * 2,
            [shaped(*half)] * 2, [], 2,
        )(mine, keep, arrived)

    def sums_over_chan(self, keep, arrived, before):
        bit = 2
        while 2 * bit < self.plan.ch:
            keep, sent = self.halve(keep, arrived, bit)
            arrived = self.across(sent, "chan", bit)
            bit *= 2
        sent = tie(self.sent_half(keep, arrived), *before)
        return (keep, arrived), sent, self.across(sent, "chan", bit)

    def cut(self, kept, came):
        plan = self.plan
        size = (came.shape[2], plan.ll)
        block = (1,) + came.shape[1:]
        spec = pl.BlockSpec(block, lambda i, place: (place[4], 0, 0, 0))
        mine, *pieces = self.chosen_half(
            partial(cut_kernel, plan), "cut", (1,), [spec, spec, pl.BlockSpec(block, lambda i, place: (0, 0, 0, 0))],
            [pl.BlockSpec(size, lambda i, place: (0, 0))] * plan.s, [shaped(*size)] * plan.s,
            [pltpu.VMEM((plan.s, *size), f32)], (*kept, came),
        )
        return mine, pieces

    def join(self, mine, arrived):
        plan = self.plan
        total = (1, 2, mine.shape[0], plan.lp)
        return call(
            partial(join_kernel, plan), "join", 1, [scalar()] + [whole(mine)] * plan.s,
            whole_shape(total), shaped(*total), [pltpu.VMEM((plan.s, *mine.shape), f32)], 2,
        )(self.slab_index, mine, *arrived)

    def exchange(self, keeps, sends, mix, fillers):
        def fill(n, value, *before):
            return tie(value, fillers[n](before)) if fillers[n] else value

        plan = self.plan
        first = [self.across(send, "chan", 1) for send in sends]
        keep0, sent0, came0 = self.sums_over_chan(keeps[0], first[0], [])
        came0 = fill(0, came0, sent0, first[1])
        keep1, sent1, came1 = self.sums_over_chan(keeps[1], first[1], [came0])

        mine, pieces = self.cut(keep0, came0)
        arrived = [self.across(piece, "slab", j + 1) for j, piece in enumerate(pieces)]
        for piece in [fill(1, arrived[0], mine, sent1)] + arrived[1:]:
            mine = mine + piece
        own0 = mine
        mirror0 = self.mirrored(own0)
        mine, pieces = self.cut(keep1, tie(came1, own0))
        arrived = [self.across(piece, "slab", j + 1) for j, piece in enumerate(pieces)]
        out0, back0 = mix(0, [mine], own0, mirror0)
        full0 = out0 + self.mirrored(back0)
        for piece in [tie(arrived[0], full0)] + arrived[1:]:
            mine = mine + piece
        own1 = mine
        mirror1 = self.mirrored(own1)

        arrived = [self.across(full0, "slab", j) for j in range(1, plan.s)]
        out1, back1 = mix(1, [full0], own1, mirror1)
        full1 = out1 + self.mirrored(back1)
        total0 = self.join(full0, [tie(arrived[0], back1)] + arrived[1:])
        came0 = self.across(total0, "chan", plan.ch // 2)
        full1 = tie(full1, total0)
        arrived = [self.across(full1, "slab", j) for j in range(1, plan.s)]
        modes = ((own0, mirror0), (own1, mirror1))
        if fillers[2]:
            came0 = tie(came0, fillers[2]([total0], modes))
        total1 = tie(self.join(full1, arrived), came0)
        came1 = self.across(total1, "chan", plan.ch // 2)
        came1 = fill(3, came1, total1)

        groups = []
        for total, other in ((total0, came0), (total1, came1)):
            if groups:
                other = tie(other, *groups[0][2:])
            bit = plan.ch // 2
            while bit > 2:
                upper = (self.chan // bit) % 2 == 1
                total = jnp.stack([jnp.where(upper, other, total), jnp.where(upper, total, other)], axis=1)
                total = total.reshape((-1,) + total.shape[2:])
                bit //= 2
                other = self.across(total, "chan", bit)
            groups.append((total, other, self.across(total, "chan", 1), self.across(other, "chan", 1)))
        return groups, modes


def local(inputs, cotangent, spectral, local_weight, bias_vector):
    nx, ny, channels, nz = inputs.shape
    wb, wk = spectral.shape[0], spectral.shape[1]
    plan = Plan(nx, ny, nz, channels, wb, wk, spectral.shape[4] // channels, lax.axis_size("slab"), lax.axis_size("chan"))
    program = Program(plan)
    values = jnp.transpose(inputs, (0, 2, 1, 3))
    slopes = jnp.transpose(cotangent, (0, 2, 1, 3))
    weights = jnp.transpose(spectral, (0, 2, 3, 1, 4))

    held = {}

    def relaid(before):
        held["weights"] = tie(weights, *before)
        return held["weights"]

    def linear(half, name, values, matrix, bias):
        def run(before):
            filled = [held[name]] if half else []
            held[name] = program.linear(half, before, filled, values, matrix, bias)
            return held[name]

        return run

    def mix(kernel, name):
        return lambda m, before, own, mirror: program.mix(kernel, name, m, before, own, mirror, held["weights"])

    keeps, sends = program.analyse(values)
    there = [linear(half, "linear", values, local_weight.T, bias_vector) for half in range(2)]
    groups, modes = program.exchange(keeps, sends, mix(mix_kernel, "mix"), (relaid, there[0], None, there[1]))
    output, gradient, keeps, sends = program.middle(groups, held["linear"], slopes)

    def outer(before, grads):
        held["outer"] = program.outer(before, modes, grads, weights)
        return held["outer"]

    def placed(before):
        held["outer"] = tie(jnp.transpose(held["outer"], (0, 3, 2, 1, 4)), *before)
        return held["outer"]

    back = [linear(half, "back", gradient, local_weight, jnp.zeros_like(bias_vector)) for half in range(2)]
    groups, _ = program.exchange(
        keeps, sends, mix(mix_back_kernel, "mix_back"), (back[0], back[1], outer, placed)
    )
    grad_inputs = program.synthesise([], groups, held["back"])
    grad_spectral = held["outer"]
    return (
        jnp.transpose(output, (0, 2, 1, 3)),
        jnp.transpose(grad_inputs, (0, 2, 1, 3)),
        jnp.transpose(grad_spectral, (0, 1, 3, 2, 4)),
    )


def solution(mesh):
    in_specs = (
        P(("groups", "slab"), "chan", None, None),
        P(("groups", "slab"), "chan", None, None),
        P("slab", "chan", None, None, None),
        P(),
        P(),
    )
    out_specs = (
        P(("groups", "slab"), "chan", None, None),
        P(("groups", "slab"), "chan", None, None),
        P(("groups", "slab"), "chan", None, None, None),
    )
    return jax.shard_map(local, mesh=mesh, in_specs=in_specs, out_specs=out_specs, check_vma=False)
```
